32 devices in a mesh: dp: 2 (over y), context: 4 (over z), expert: 4 (over x, core).
Axes of the slice: x: 2, y: 2, z: 4, core: 2. Of those that a mesh axis runs over, the one named last changes fastest.
Arguments:
- block_input: bfloat16 [8192, 2048], P(('dp', 'context', 'expert')), may hold values from -6 to 6
- teacher_states: float32 [8192, 2048], P(('dp', 'context', 'expert')), may hold values from -6 to 6
- seq_lengths: int32 [2], P('dp'), may hold values from 1024 to 4096, as said below
- expert_routes: int32 [8192, 8], P(('dp', 'context', 'expert')), may hold values from 0 to 15, all different within a row; in each aligned block of 256 rows (0 to 255, 256 to 511, ...) at most 160 rows name the same one
- attn_gain: float32 [2048], replicated, may hold values from 0.5 to 1.5
- query_weight: bfloat16 [2048, 2048], P(None, 'expert'), may hold values from -0.125 to 0.125
- key_weight: bfloat16 [2048, 2048], P(None, 'expert'), may hold values from -0.125 to 0.125
- value_weight: bfloat16 [2048, 2048], P(None, 'expert'), may hold values from -0.125 to 0.125
- query_gain: float32 [2048], P('expert'), may hold values from 0.5 to 1.5
- key_gain: float32 [2048], P('expert'), may hold values from 0.5 to 1.5
- output_weight: bfloat16 [2048, 2048], P('expert'), may hold values from -4 to 4
- ffn_gain: float32 [2048], replicated, may hold values from 0.5 to 1.5
- router_weight: bfloat16 [2048, 16], replicated, may hold values from -0.0625 to 0.0625
- gate_weight: bfloat16 [16, 2048, 1024], P(('context', 'expert'), None, 'dp'), may hold values from -0.125 to 0.125
- up_weight: bfloat16 [16, 2048, 1024], P(('context', 'expert'), None, 'dp'), may hold values from -0.125 to 0.125
- down_weight: bfloat16 [16, 1024, 2048], P(('context', 'expert'), 'dp'), may hold values from -4 to 4
Outputs:
- block_output: bfloat16 [8192, 2048], P(('dp', 'context', 'expert'))
- loss_value: float32 [], replicated
- input_grad: float32 [8192, 2048], P(('dp', 'context', 'expert'))
- attn_gain_grad: float32 [2048], replicated
- query_weight_grad: float32 [2048, 2048], P(None, 'expert')
- key_weight_grad: float32 [2048, 2048], P(None, 'expert')
- value_weight_grad: float32 [2048, 2048], P(None, 'expert')
- query_gain_grad: float32 [2048], P('expert')
- key_gain_grad: float32 [2048], P('expert')
- output_weight_grad: float32 [2048, 2048], P('expert')
- ffn_gain_grad: float32 [2048], replicated
- router_weight_grad: float32 [2048, 16], replicated
- gate_weight_grad: float32 [16, 2048, 1024], P(('context', 'expert'), None, 'dp')
- up_weight_grad: float32 [16, 2048, 1024], P(('context', 'expert'), None, 'dp')
- down_weight_grad: float32 [16, 1024, 2048], P(('context', 'expert'), 'dp')
The draws below stay inside these ranges and needn't reach their ends.
Inputs may be any that keep to these rules, and one draw needn't show every extreme that they name: The first seq_lengths[s] of the 4096 positions of sequence s are valid tokens, the rest padding; at least one sequence is entirely valid. `expert_routes`: each row names 8 different experts. Within the rows of one device (aligned blocks of 256 rows) no expert is named more than 160 times, a bound that some block reaches.
All inputs are finite; a program needn't handle non-finite values.
Results may differ from the reference program's by a relative error of at most 0.02.
Values may be sent and summed in bfloat16 or wider, within the bound.
No kernel may reach another device: no remote copies, remote signals or barrier semaphores. Data moves between devices by JAX's collectives and lax.ppermute only.
A program may use at most 448 MiB of HBM per device.

```python
import math
import jax
import jax.numpy as jnp
import numpy as np
from jax import lax

D = 2048
HEADS = 16
HD = 128
EFF = 1024
TOPK = 8
LEN = 4096
SEQS = 2
TOKENS = 8192
TOK_DEV = 256
EXPERTS = 16
CAP = 160


def draw_seq_lengths(key, part):
    lengths = jax.random.randint(key, (SEQS,), LEN // 4, LEN + 1)
    longest = jax.random.randint(jax.random.fold_in(key, 7), (), 0, SEQS)
    return jnp.where(jnp.arange(SEQS) == longest, LEN, lengths).astype(jnp.int32)


def level_of(own_key, dims, cuts, smallest, high):
    loudness = 1.0
    for position, blocks in cuts:
        draws = jax.random.uniform(jax.random.fold_in(jax.random.fold_in(own_key, 6), position), (blocks,), jnp.float32, smallest / len(cuts), high / len(cuts))
        loudness = loudness * jnp.repeat(jnp.exp(draws), dims[position] // blocks).reshape((-1,) + (1,) * (len(dims) - 1 - position))
    return loudness


def shared_out(own_key, own, number, rows, count, top, limit, slope):
    sequence = jax.random.permutation(own_key, count)
    heavy_load, usual = load_shares(count, rows * top, limit, slope, True), load_shares(count, rows * top, limit, slope, False)
    places = jnp.arange(count)

    def named(tallies, offset_by):
        used = int((tallies > 0).sum())
        fixed = max(1, used // 4)
        moved = fixed + (places - fixed + offset_by * (used - fixed)) % max(1, count - fixed)
        return jnp.zeros((count,), jnp.int32).at[sequence[jnp.where(places < fixed, places, moved)]].set(jnp.asarray(tallies, jnp.int32))

    tallies = jnp.where(number % 4 == 0, named(heavy_load, number // 4), named(usual, number - number // 4 - 1))
    mixed = jax.random.permutation(jax.random.fold_in(own, 3), count)
    donor, taker = mixed[0:count // 2 * 2:2], mixed[1:count // 2 * 2:2]
    room = jnp.minimum(tallies[donor] - 1, limit - tallies[taker]) // 2
    room = jnp.where((donor == sequence[0]) | (taker == sequence[0]) | (tallies[taker] == 0), 0, jnp.maximum(room, 0))
    moved = jax.random.randint(jax.random.fold_in(own, 4), (count // 2,), 0, 1 << 20) % (room + 1)
    tallies = tallies.at[donor].add(-moved).at[taker].add(moved)
    labels = jnp.searchsorted(jnp.cumsum(tallies), jnp.arange(rows * top), side="right").astype(jnp.int32)
    grid = labels.reshape(top, rows).T
    grid = grid[jax.random.permutation(jax.random.fold_in(own, 1), rows)]
    offset_by = jax.random.randint(jax.random.fold_in(own, 2), (rows, 1), 0, top)
    return jnp.take_along_axis(grid, (jnp.arange(top)[None, :] + offset_by) % top, axis=1)


def load_shares(amount, total, reach, skew, full):
    weights = [(1 << 20) // math.isqrt(rank ** skew) + 1 for rank in range(1, amount + 1)]
    largest = reach if full else min(reach, max(-(-total // amount), total * weights[0] // sum(weights)))
    least = 1 if total - largest >= amount - 1 else 0
    given, spare = [largest] + [least] * (amount - 1), total - largest - least * (amount - 1)
    while spare > 0:
        free = [i for i in range(1, amount) if given[i] < largest] or [i for i in range(1, amount) if given[i] < reach]
        mass, remaining = sum([weights[i] for i in free]), spare
        for i in free:
            addition = min(reach - given[i], max(1, remaining * weights[i] // mass), spare)
            given[i] = given[i] + addition
            spare = spare - addition
    return np.array(given)


def gaussian(own_key, shape, scale, reach, split=(), kind=jnp.bfloat16):
    values = scale * jax.random.normal(own_key, shape, jnp.float32)
    if split:
        values = values * level_of(own_key, shape, split, -0.22, 0.18)
    return jnp.clip(values, -reach, reach).astype(kind)


def setup_inputs(seed: int = 0) -> dict:
    streams_of = jax.random.split(jax.random.key(seed), 17)
    block_input = gaussian(streams_of[0], (TOKENS, D), 1.0, 6.0, ((0, 32),))
    teacher_states = gaussian(streams_of[1], (TOKENS, D), 1.0, 6.0, ((0, 32),), jnp.float32)
    seq_lengths = draw_seq_lengths(jax.random.fold_in(streams_of[16], 71), 0)
    expert_routes_keys = jax.random.split(jax.random.fold_in(streams_of[3], 1), TOKENS // TOK_DEV)
    expert_routes_turns = jax.random.permutation(jax.random.fold_in(streams_of[3], 3), TOKENS // TOK_DEV)
    expert_routes = jax.vmap(lambda own, number: shared_out(jax.random.fold_in(streams_of[3], 2), own, number, TOK_DEV, EXPERTS, TOPK, CAP, 1))(expert_routes_keys, expert_routes_turns).reshape((TOKENS, TOPK))
    attn_gain = jnp.clip(1.0 + 0.1 * jax.random.normal(streams_of[4], (D,), jnp.float32), 0.5, 1.5)
    query_weight = gaussian(streams_of[5], (D, HEADS * HD), D ** -0.5, 0.125, ((1, 4),))
    key_weight = gaussian(streams_of[6], (D, HEADS * HD), D ** -0.5, 0.125, ((1, 4),))
    value_weight = gaussian(streams_of[7], (D, HEADS * HD), D ** -0.5, 0.125, ((1, 4),))
    query_gain = jnp.clip(1.0 + 0.1 * jax.random.normal(streams_of[8], (HEADS * HD,), jnp.float32), 0.5, 1.5)
    key_gain = jnp.clip(1.0 + 0.1 * jax.random.normal(streams_of[9], (HEADS * HD,), jnp.float32), 0.5, 1.5)
    output_weight = gaussian(streams_of[10], (HEADS * HD, D), (max(HEADS * HD * 4 // LEN, 1)) ** -0.5, 4.0, ((0, 4),))
    ffn_gain = jnp.clip(1.0 + 0.1 * jax.random.normal(streams_of[11], (D,), jnp.float32), 0.5, 1.5)
    router_weight = gaussian(streams_of[12], (D, EXPERTS), (4 * D) ** -0.5, 0.0625)
    gate_weight = gaussian(streams_of[13], (EXPERTS, D, EFF), D ** -0.5, 0.125, ((0, 16), (2, 2)))
    up_weight = gaussian(streams_of[14], (EXPERTS, D, EFF), D ** -0.5, 0.125, ((0, 16), (2, 2)))
    down_weight = gaussian(streams_of[15], (EXPERTS, EFF, D), (max(EFF // 512, 1)) ** -0.5, 4.0, ((0, 16), (1, 2)))
    return dict(block_input=block_input, teacher_states=teacher_states, seq_lengths=seq_lengths, expert_routes=expert_routes, attn_gain=attn_gain, query_weight=query_weight, key_weight=key_weight, value_weight=value_weight, query_gain=query_gain, key_gain=key_gain, output_weight=output_weight, ffn_gain=ffn_gain, router_weight=router_weight, gate_weight=gate_weight, up_weight=up_weight, down_weight=down_weight)


EPSILON = 1e-05
ROPE_BASE = 10000.0
NEGATIVE = -1e+30

@jax.custom_vjp
def low(v):
    return lax.optimization_barrier(v.astype(jnp.bfloat16)).astype(jnp.float32)

@jax.custom_vjp
def low_back(v):
    return v

def low_keep(v):
    return (low(v), None)

def low_pass(kept, grad):
    return (grad,)

def back_keep(v):
    return (v, None)

def back_low(kept, grad):
    return (low(grad),)
low.defvjp(low_keep, low_pass)
low_back.defvjp(back_keep, back_low)

def matmul(left, right):
    return jnp.dot(left, right, precision=lax.Precision.HIGHEST, preferred_element_type=jnp.float32)

def rms_scale(values):
    return lax.rsqrt(lax.optimization_barrier(jnp.mean(values * values, axis=-1, keepdims=True)) + EPSILON)

def rope_tables(positions):
    exponent = jnp.arange(HD // 2, dtype=jnp.float32) * (2.0 / HD)
    angles = positions.astype(jnp.float32)[:, None] * (ROPE_BASE ** (-exponent))[None, :]
    return (jnp.cos(angles), jnp.sin(angles))

def rotate(values, cosine, sine_part):
    halfway = values.shape[-1] // 2
    leading = values[..., :halfway]
    trailing = values[..., halfway:]
    cos_wide = cosine[:, None, :]
    sin_wide = sine_part[:, None, :]
    return jnp.concatenate([leading * cos_wide - trailing * sin_wide, trailing * cos_wide + leading * sin_wide], axis=-1)

def attend_sequence(packed):
    queries, key_rows, value_rows, length = packed
    row_block = min(512, LEN)
    key_pos = jnp.arange(LEN, dtype=jnp.int32)

    def one_block(inner_pack):
        query_part, offset = inner_pack
        raw_scores = jnp.einsum('qhd,khd->hqk', query_part, key_rows, precision=lax.Precision.HIGHEST) * HD ** (-0.5)
        scores = low_back(raw_scores)
        query_pos = offset + jnp.arange(row_block, dtype=jnp.int32)
        allowed = (key_pos[None, :] <= query_pos[:, None]) & (key_pos[None, :] < length)
        masked = jnp.where(allowed[None], scores, NEGATIVE)
        shifted = masked - lax.optimization_barrier(jnp.max(masked, axis=-1, keepdims=True))
        weights = jnp.exp(shifted)
        probabilities = weights / lax.optimization_barrier(jnp.sum(weights, axis=-1, keepdims=True))
        return jnp.einsum('hqk,khd->qhd', low(probabilities), value_rows, precision=lax.Precision.HIGHEST)
    starts = jnp.arange(LEN // row_block, dtype=jnp.int32) * row_block
    context_parts = lax.map(jax.checkpoint(one_block), (queries.reshape(LEN // row_block, row_block, HEADS, HD), starts))
    return context_parts.reshape(LEN, HEADS, HD)

def reference(block_input, teacher_states, seq_lengths, expert_routes, attn_gain, query_weight, key_weight, value_weight, query_gain, key_gain, output_weight, ffn_gain, router_weight, gate_weight, up_weight, down_weight):
    block_count = TOKENS // TOK_DEV
    positions = jnp.tile(jnp.arange(LEN, dtype=jnp.int32), SEQS)
    valid = (positions < jnp.repeat(seq_lengths, LEN)).astype(jnp.float32)
    valid_count = jnp.sum(seq_lengths).astype(jnp.float32)
    cosine, sine_part = rope_tables(positions)
    routes_flat = expert_routes.reshape(block_count, TOK_DEV * TOPK)
    onehot = (routes_flat[..., None] == jnp.arange(EXPERTS, dtype=jnp.int32)).astype(jnp.int32)
    earlier = jnp.cumsum(onehot, axis=1) - onehot
    slots_flat = lax.optimization_barrier(jnp.sum(earlier * onehot, axis=-1)).astype(jnp.int32)
    choose = (expert_routes[..., None] == jnp.arange(EXPERTS, dtype=jnp.int32)).astype(jnp.float32)
    seq_shape = (SEQS, LEN, HEADS, HD)

    def forward(inputs, gain_one, query_mat, key_mat, value_mat, query_scale, key_scale, out_mat, gain_two, router_mat, gate_mat, up_mat, down_mat):
        normed = low(inputs * rms_scale(inputs) * gain_one)
        query_raw = low_back(matmul(normed, query_mat))
        key_raw = low_back(matmul(normed, key_mat))
        value_raw = low_back(matmul(normed, value_mat))
        query_normed = query_raw * rms_scale(query_raw) * query_scale
        key_normed = key_raw * rms_scale(key_raw) * key_scale
        queries = low(rotate(query_normed.reshape(TOKENS, HEADS, HD), cosine, sine_part))
        key_rows = low(rotate(key_normed.reshape(TOKENS, HEADS, HD), cosine, sine_part))
        value_rows = low(value_raw).reshape(TOKENS, HEADS, HD)
        context = lax.map(attend_sequence, (queries.reshape(seq_shape), key_rows.reshape(seq_shape), value_rows.reshape(seq_shape), seq_lengths))
        context = low(low_back(context.reshape(TOKENS, HEADS * HD)))
        attn_out = low_back(matmul(context, out_mat))
        residual = inputs + attn_out
        ffn_in = low(residual * rms_scale(residual) * gain_two)
        logits = matmul(ffn_in, router_mat)
        shifted = logits - lax.optimization_barrier(jnp.max(logits, axis=-1, keepdims=True))
        weights = jnp.exp(shifted)
        router_probs = weights / lax.optimization_barrier(jnp.sum(weights, axis=-1, keepdims=True))
        gate_values = lax.optimization_barrier(jnp.sum(choose * router_probs[:, None, :], axis=-1))

        def expert_block(packed):
            block_rows, block_gates, block_experts, block_slots = packed
            picked_rows = low_back(jnp.repeat(block_rows, TOPK, axis=0))
            buffer = jnp.zeros((EXPERTS, CAP, D), jnp.float32).at[block_experts, block_slots].set(picked_rows)
            gate_part = low_back(jnp.einsum('ecd,edf->ecf', buffer, gate_mat, precision=lax.Precision.HIGHEST))
            up_part = low_back(jnp.einsum('ecd,edf->ecf', buffer, up_mat, precision=lax.Precision.HIGHEST))
            hidden = low(gate_part * jax.nn.sigmoid(gate_part) * up_part)
            expert_out = low(low_back(jnp.einsum('ecf,efd->ecd', hidden, down_mat, precision=lax.Precision.HIGHEST)))
            returned = expert_out[block_experts, block_slots].reshape(TOK_DEV, TOPK, D)
            return lax.optimization_barrier(jnp.sum(returned * block_gates[:, :, None], axis=1))
        mixture = lax.map(jax.checkpoint(expert_block), (ffn_in.reshape(block_count, TOK_DEV, D), gate_values.reshape(block_count, TOK_DEV, TOPK), routes_flat, slots_flat))
        output_full = residual + mixture.reshape(TOKENS, D)
        difference = output_full - teacher_states
        loss_value = jnp.sum(lax.optimization_barrier(jnp.sum(difference * difference, axis=-1)) * valid) / valid_count
        return (loss_value * (TOKENS / 2), (output_full, loss_value))
    floats = (block_input.astype(jnp.float32), attn_gain, query_weight.astype(jnp.float32), key_weight.astype(jnp.float32), value_weight.astype(jnp.float32), query_gain, key_gain, output_weight.astype(jnp.float32), ffn_gain, router_weight.astype(jnp.float32), gate_weight.astype(jnp.float32), up_weight.astype(jnp.float32), down_weight.astype(jnp.float32))
    scaled, backward_fn, extras = jax.vjp(forward, *floats, has_aux=True)
    gradients = backward_fn(jnp.ones_like(scaled))
    output_full, loss_value = extras
    return (output_full.astype(jnp.bfloat16), loss_value, gradients[0], gradients[1], gradients[2], gradients[3], gradients[4], gradients[5], gradients[6], gradients[7], gradients[8], gradients[9], gradients[10], gradients[11], gradients[12])
```

```python
import functools
import math

import jax
import jax.numpy as jnp
from jax import lax
from jax.experimental import pallas as pl
from jax.experimental.pallas import tpu as pltpu
from jax.sharding import PartitionSpec as P

HEADS = 16
HD = 128
TOPK = 8


EPSILON = 1e-05
ROPE_BASE = 10000.0
NEGATIVE = -1e30
LOG2E = math.log2(math.e)
SCORE_SCALE = HD ** (-0.5)
TOKEN_AXES = ("context", "expert")
ALL_AXES = ("dp", "context", "expert")
VMEM_LIMIT = 48 * 2**20


def rms_scale(values):
    return lax.rsqrt(jnp.mean(values * values, axis=-1, keepdims=True) + EPSILON)


def rope_tables(positions):
    exponent = jnp.arange(HD // 2, dtype=jnp.float32) * (2.0 / HD)
    angles = positions.astype(jnp.float32)[:, None] * (ROPE_BASE ** (-exponent))[None, :]
    return (jnp.cos(angles), jnp.sin(angles))


def rotate(values, cosine, sine_part):
    halfway = values.shape[-1] // 2
    leading = values[..., :halfway]
    trailing = values[..., halfway:]
    cos_wide = cosine[:, None, :]
    sin_wide = sine_part[:, None, :]
    return jnp.concatenate(
        [leading * cos_wide - trailing * sin_wide, trailing * cos_wide + leading * sin_wide],
        axis=-1,
    )


def rotate_back(gradient, cosine, sine_part):
    return rotate(gradient, cosine, -sine_part)


def silu_parts(gate_part):
    sigmoid = jax.nn.sigmoid(gate_part)
    return (gate_part * sigmoid, sigmoid * (1.0 + gate_part * (1.0 - sigmoid)))


def contract(left, right, left_dim, right_dim):
    return lax.dot_general(
        left,
        right,
        (((left_dim,), (right_dim,)), ((), ())),
        preferred_element_type=jnp.float32,
    )


def contract_rows(left, right):
    return contract(left, right, 0, 0)


def contract_last(left, right):
    return contract(left, right, 1, 1)


def low(values):
    return values.astype(jnp.bfloat16)


def gather_block(rows):
    return lax.all_gather(rows, "expert", axis=0, tiled=True)


def gather_sequence(rows):
    return lax.all_gather(rows, TOKEN_AXES, axis=0, tiled=True)


def scatter_sequence(rows):
    return lax.psum_scatter(low(rows), TOKEN_AXES, scatter_dimension=0, tiled=True).astype(
        jnp.float32
    )


def sum_low(values, axes):
    return lax.psum(low(values), axes).astype(jnp.float32)


def sum_half_over_dp(values, axis):
    size = lax.axis_size("dp")
    if size != 2:
        return lax.psum_scatter(low(values), "dp", scatter_dimension=axis, tiled=True).astype(
            jnp.float32
        )
    mine = lax.axis_index("dp")
    share = values.shape[axis] // 2
    sent = lax.dynamic_slice_in_dim(values, (1 - mine) * share, share, axis)
    kept = lax.dynamic_slice_in_dim(values, mine * share, share, axis)
    return kept + lax.ppermute(low(sent), "dp", ((0, 1), (1, 0))).astype(jnp.float32)


def flash_forward_kernel(length_ref, q_ref, k_ref, v_ref, out_ref, log_ref, *, block):
    row_block = pl.program_id(0)
    length = length_ref[0]
    queries = q_ref[...]

    def step(j, carry, masked):
        highest, total, acc = carry
        rows = pl.ds(pl.multiple_of(j * block, block), block)
        scores = contract_last(queries, k_ref[rows, :])
        if masked:
            query_pos = row_block * block + lax.broadcasted_iota(jnp.int32, (block, block), 0)
            key_pos = j * block + lax.broadcasted_iota(jnp.int32, (block, block), 1)
            allowed = (key_pos <= query_pos) & (key_pos < length)
            scores = jnp.where(allowed, scores, NEGATIVE)
        higher = jnp.maximum(highest, jnp.max(scores, axis=1, keepdims=True))
        weights = jnp.exp2(scores - higher)
        decay = jnp.exp2(highest - higher)
        total = total * decay + jnp.sum(weights, axis=1, keepdims=True)
        acc = acc * decay + contract(low(weights), v_ref[rows, :], 1, 0)
        return higher, total, acc

    start = (
        jnp.full((block, 1), NEGATIVE, jnp.float32),
        jnp.zeros((block, 1), jnp.float32),
        jnp.zeros((block, HD), jnp.float32),
    )
    full = jnp.minimum(row_block, length // block)
    end = jnp.minimum(row_block + 1, (length + block - 1) // block)
    carry = lax.fori_loop(0, full, lambda j, c: step(j, c, False), start)
    highest, total, acc = lax.fori_loop(full, end, lambda j, c: step(j, c, True), carry)
    out_ref[...] = low(acc / total)
    log_ref[...] = jnp.broadcast_to(highest + jnp.log2(total), (block, HD)).T[:8, :]


def flash_forward(queries, keys, values, length, block):
    rows = queries.shape[0]
    whole = pl.BlockSpec((rows, HD), lambda i, _: (0, 0))
    part = pl.BlockSpec((block, HD), lambda i, _: (i, 0))
    return pl.pallas_call(
        functools.partial(flash_forward_kernel, block=block),
        grid_spec=pltpu.PrefetchScalarGridSpec(
            num_scalar_prefetch=1,
            grid=(rows // block,),
            in_specs=[part, whole, whole],
            out_specs=[part, pl.BlockSpec((8, block), lambda i, _: (0, i))],
        ),
        out_shape=[
            jax.ShapeDtypeStruct((rows, HD), jnp.bfloat16),
            jax.ShapeDtypeStruct((8, rows), jnp.float32),
        ],
        compiler_params=pltpu.CompilerParams(vmem_limit_bytes=VMEM_LIMIT),
        cost_estimate=pl.CostEstimate(
            flops=8 * rows * rows * HD // 2,
            bytes_accessed=8 * rows * HD,
            transcendentals=rows * rows // 2,
        ),
    )(length, queries, keys, values)


def flash_backward_kernel(
    length_ref, q_ref, do_ref, log_ref, delta_ref, k_ref, v_ref, dq_ref, dk_ref, dv_ref, *, block
):
    key_block = pl.program_id(0)
    count = q_ref.shape[0] // block
    length = length_ref[0]

    @pl.when(key_block == 0)
    def _():
        dq_ref[...] = jnp.zeros_like(dq_ref)

    keys = k_ref[...]
    values = v_ref[...]

    def step(i, carry, masked):
        key_acc, value_acc = carry
        rows = pl.ds(pl.multiple_of(i * block, block), block)
        queries = q_ref[rows, :]
        grads = do_ref[rows, :]
        weights = jnp.exp2(contract_last(keys, queries) - log_ref[0:1, rows])
        if masked:
            query_pos = i * block + lax.broadcasted_iota(jnp.int32, (block, block), 1)
            key_pos = key_block * block + lax.broadcasted_iota(jnp.int32, (block, block), 0)
            allowed = (key_pos <= query_pos) & (key_pos < length)
            weights = jnp.where(allowed, weights, 0.0)
        grad_weights = contract_last(values, grads)
        grad_scores = low(weights * (grad_weights - delta_ref[0:1, rows]))
        value_acc = value_acc + contract(low(weights), grads, 1, 0)
        key_acc = key_acc + contract(grad_scores, queries, 1, 0)
        dq_ref[rows, :] += contract_rows(grad_scores, keys)
        return key_acc, value_acc

    zeros = jnp.zeros((block, HD), jnp.float32)
    beyond = key_block * block >= length
    ragged = (key_block + 1) * block > length
    start = jnp.where(beyond, count, key_block)
    masked_end = jnp.where(ragged, count, key_block + 1)
    carry = lax.fori_loop(start, masked_end, lambda i, c: step(i, c, True), (zeros, zeros))
    key_acc, value_acc = lax.fori_loop(
        masked_end, count, lambda i, c: step(i, c, False), carry
    )
    dk_ref[...] = key_acc * (1.0 / LOG2E)
    dv_ref[...] = value_acc

    @pl.when(key_block == count - 1)
    def _():
        dq_ref[...] = dq_ref[...] * SCORE_SCALE


def flash_backward(queries, keys, values, grads, logs, delta, length, block):
    rows = queries.shape[0]
    whole = pl.BlockSpec((rows, HD), lambda j, _: (0, 0))
    part = pl.BlockSpec((block, HD), lambda j, _: (j, 0))
    return pl.pallas_call(
        functools.partial(flash_backward_kernel, block=block),
        grid_spec=pltpu.PrefetchScalarGridSpec(
            num_scalar_prefetch=1,
            grid=(rows // block,),
            in_specs=[
                whole,
                whole,
                pl.BlockSpec((8, rows), lambda j, _: (0, 0)),
                pl.BlockSpec((1, rows), lambda j, _: (0, 0)),
                part,
                part,
            ],
            out_specs=[whole, part, part],
        ),
        out_shape=[jax.ShapeDtypeStruct((rows, HD), jnp.float32)] * 3,
        compiler_params=pltpu.CompilerParams(vmem_limit_bytes=VMEM_LIMIT),
        cost_estimate=pl.CostEstimate(
            flops=20 * rows * rows * HD // 2,
            bytes_accessed=20 * rows * HD,
            transcendentals=rows * rows // 2,
        ),
    )(length, queries, grads, logs, delta, keys, values)


class HeadAttention:
    def __init__(self, normed, length, weights, gains, output_weight):
        self.tok_rows = normed.shape[0]
        self.output_weight = output_weight
        self.length = length.reshape(1)
        head = lax.axis_index("context")

        def mine(array):
            return lax.dynamic_slice_in_dim(array, head * HD, HD, array.ndim - 1)

        self.weight = jnp.concatenate([mine(w) for w in weights], axis=1)
        self.query_gain, self.key_gain = (mine(g) for g in gains)
        self.normed = gather_sequence(normed)
        rows = self.normed.shape[0]
        self.block = math.gcd(1024, rows)
        self.tables = rope_tables(jnp.arange(rows, dtype=jnp.int32))
        projected = jnp.dot(self.normed, self.weight, preferred_element_type=jnp.float32)
        self.query_raw = projected[:, :HD]
        self.key_raw = projected[:, HD : 2 * HD]
        self.values = low(projected[:, 2 * HD :])
        totals = lax.psum(
            jnp.stack([jnp.sum(self.query_raw**2, axis=-1), jnp.sum(self.key_raw**2, axis=-1)]),
            TOKEN_AXES,
        )
        inverse = lax.rsqrt(totals / (HEADS * HD) + EPSILON)
        self.query_inv, self.key_inv = (inverse[0][:, None], inverse[1][:, None])
        turned = self.turn(self.query_raw * self.query_inv * self.query_gain, rotate)
        self.queries = low(turned * (SCORE_SCALE * LOG2E))
        self.keys = low(self.turn(self.key_raw * self.key_inv * self.key_gain, rotate))
        self.context, self.logs = flash_forward(
            self.queries, self.keys, self.values, self.length, self.block
        )
        self.context_block = self.to_block(self.context)

    def turn(self, values, how):
        return how(values[:, None, :], *self.tables)[:, 0, :]

    def to_block(self, rows):
        return lax.all_to_all(rows, "context", split_axis=0, concat_axis=1, tiled=True)

    def to_heads(self, rows):
        return lax.all_to_all(rows, "context", split_axis=1, concat_axis=0, tiled=True)

    def output(self):
        term = jnp.dot(
            self.context_block, self.output_weight, preferred_element_type=jnp.float32
        )
        return lax.psum_scatter(low(term), "expert", scatter_dimension=0, tiled=True).astype(
            jnp.float32
        )

    def backward(self, grad_attn):
        block_grad = gather_block(grad_attn)
        grad_context = self.to_heads(low(contract_last(block_grad, self.output_weight)))
        output_total = sum_low(
            contract_rows(self.context_block, block_grad), ("dp", "context")
        )
        delta = jnp.sum(
            grad_context.astype(jnp.float32) * self.context.astype(jnp.float32), axis=-1
        )[None]
        query_grad, key_grad, value_grad = flash_backward(
            self.queries,
            self.keys,
            self.values,
            grad_context,
            self.logs,
            delta,
            self.length,
            self.block,
        )
        grad_query_normed = self.turn(query_grad, rotate_back)
        grad_key_normed = self.turn(key_grad, rotate_back)
        gain_grads = jnp.concatenate(
            [
                jnp.sum(self.query_raw * self.query_inv * grad_query_normed, axis=0),
                jnp.sum(self.key_raw * self.key_inv * grad_key_normed, axis=0),
            ]
        )
        dots = lax.psum(
            jnp.stack(
                [
                    jnp.sum(self.query_raw * self.query_gain * grad_query_normed, axis=-1),
                    jnp.sum(self.key_raw * self.key_gain * grad_key_normed, axis=-1),
                ]
            ),
            TOKEN_AXES,
        ) / (HEADS * HD)
        grad_query = (
            self.query_inv * self.query_gain * grad_query_normed
            - self.query_raw * self.query_inv**3 * dots[0][:, None]
        )
        grad_key = (
            self.key_inv * self.key_gain * grad_key_normed
            - self.key_raw * self.key_inv**3 * dots[1][:, None]
        )
        grad_joint = low(jnp.concatenate([grad_query, grad_key, value_grad], axis=1))
        grad_normed = scatter_sequence(contract_last(grad_joint, self.weight))
        joint_grad = contract_rows(self.normed, grad_joint)
        joint_total = lax.all_gather(low(sum_low(joint_grad, "dp")), "context", axis=0)
        gains_total = lax.all_gather(lax.psum(gain_grads, "dp"), "context", axis=0)

        def spread(part):
            part = part.astype(jnp.float32)
            return jnp.moveaxis(part, 0, -2).reshape(part.shape[1:-1] + (-1,))

        return (
            grad_normed,
            *(spread(joint_total[..., i * HD : (i + 1) * HD]) for i in range(3)),
            *(spread(gains_total[..., i * HD : (i + 1) * HD]) for i in range(2)),
            output_total,
        )


class BlockAttention:
    def __init__(self, normed, length, weights, gains, output_weight):
        self.tok_rows = normed.shape[0]
        self.output_weight = output_weight
        self.length = length
        self.query_gain, self.key_gain = gains
        self.head_width = head_width = weights[0].shape[1]
        self.heads = head_width // HD
        self.weight = jnp.concatenate(weights, axis=1)
        self.normed = gather_block(normed)
        self.rows = rows = self.normed.shape[0]
        self.block_start = lax.axis_index("context") * rows
        projected = jnp.dot(self.normed, self.weight, preferred_element_type=jnp.float32)
        self.query_raw = projected[:, :head_width]
        self.key_raw = projected[:, head_width : 2 * head_width]
        value_raw = projected[:, 2 * head_width :]
        query_total, key_total = lax.psum(
            (jnp.sum(self.query_raw**2, axis=-1), jnp.sum(self.key_raw**2, axis=-1)), "expert"
        )
        self.query_inv = lax.rsqrt(query_total / (HEADS * HD) + EPSILON)[:, None]
        self.key_inv = lax.rsqrt(key_total / (HEADS * HD) + EPSILON)[:, None]
        self.tables = rope_tables(self.block_start + jnp.arange(rows, dtype=jnp.int32))
        query_rot = self.turn(self.query_raw * self.query_inv * self.query_gain, rotate)
        key_rot = self.turn(self.key_raw * self.key_inv * self.key_gain, rotate)
        self.keys, self.values = (
            lax.all_gather(low(key_rot), "context", axis=0, tiled=True),
            lax.all_gather(
                low(value_raw.reshape(rows, self.heads, HD)), "context", axis=0, tiled=True
            ),
        )
        self.query_block = min(512, rows)
        self.count = rows // self.query_block
        self.starts = jnp.arange(self.count, dtype=jnp.int32) * self.query_block
        self.queries = self.in_blocks(low(query_rot))

        def forward_block(packed):
            query_part, offset = packed
            masked, _ = self.scores_for(query_part, offset)
            highest = jnp.max(masked, axis=-1, keepdims=True)
            scores = jnp.exp(masked - highest)
            totals = jnp.sum(scores, axis=-1, keepdims=True)
            context = jnp.einsum(
                "hqk,khd->qhd",
                low(scores / totals),
                self.values,
                preferred_element_type=jnp.float32,
            )
            return (context, (highest + jnp.log(totals))[..., 0])

        context, self.logs = lax.map(forward_block, (self.queries, self.starts))
        self.context = low(context.reshape(rows, head_width))

    def turn(self, values, how):
        return how(values.reshape(self.rows, self.heads, HD), *self.tables)

    def in_blocks(self, values):
        return values.reshape(self.count, self.query_block, self.heads, HD)

    def scores_for(self, query_part, offset):
        raw_scores = (
            jnp.einsum("qhd,khd->hqk", query_part, self.keys, preferred_element_type=jnp.float32)
            * SCORE_SCALE
        )
        key_pos = jnp.arange(self.keys.shape[0], dtype=jnp.int32)
        query_pos = self.block_start + offset + jnp.arange(self.query_block, dtype=jnp.int32)
        allowed = (key_pos[None, :] <= query_pos[:, None]) & (key_pos[None, :] < self.length)
        return (jnp.where(allowed[None], raw_scores, NEGATIVE), allowed)

    def output(self):
        term = jnp.dot(self.context, self.output_weight, preferred_element_type=jnp.float32)
        return lax.psum_scatter(low(term), "expert", scatter_dimension=0, tiled=True).astype(
            jnp.float32
        )

    def backward(self, grad_attn):
        rows, heads = (self.rows, self.heads)
        block_grad = gather_block(grad_attn)
        output_total = sum_low(contract_rows(self.context, block_grad), ("dp", "context"))
        grad_blocks = self.in_blocks(low(contract_last(block_grad, self.output_weight)))

        def backward_block(running, packed):
            key_acc, value_acc = running
            query_part, grad_part, log_part, offset = packed
            masked, allowed = self.scores_for(query_part, offset)
            probs = jnp.where(allowed[None], jnp.exp(masked - log_part[..., None]), 0.0)
            grad_probs = jnp.einsum(
                "qhd,khd->hqk", grad_part, self.values, preferred_element_type=jnp.float32
            )
            row_dot = jnp.sum(probs * grad_probs, axis=-1, keepdims=True)
            grad_scores = low(probs * (grad_probs - row_dot))
            query_grad = (
                jnp.einsum(
                    "hqk,khd->qhd", grad_scores, self.keys, preferred_element_type=jnp.float32
                )
                * SCORE_SCALE
            )
            key_acc = (
                key_acc
                + jnp.einsum(
                    "hqk,qhd->khd", grad_scores, query_part, preferred_element_type=jnp.float32
                )
                * SCORE_SCALE
            )
            value_acc = value_acc + jnp.einsum(
                "hqk,qhd->khd", low(probs), grad_part, preferred_element_type=jnp.float32
            )
            return ((key_acc, value_acc), query_grad)

        zeros = jnp.zeros((self.keys.shape[0], heads, HD), jnp.float32)
        (key_acc, value_acc), query_grads = lax.scan(
            backward_block, (zeros, zeros), (self.queries, grad_blocks, self.logs, self.starts)
        )
        key_grad, value_grad = (
            lax.psum_scatter(low(acc), "context", scatter_dimension=0, tiled=True).astype(
                jnp.float32
            )
            for acc in (key_acc, value_acc)
        )
        grad_query_normed = self.turn(query_grads, rotate_back).reshape(rows, -1)
        grad_key_normed = self.turn(key_grad, rotate_back).reshape(rows, -1)
        query_dot, key_dot = lax.psum(
            (
                jnp.sum(self.query_raw * self.query_gain * grad_query_normed, axis=-1),
                jnp.sum(self.key_raw * self.key_gain * grad_key_normed, axis=-1),
            ),
            "expert",
        )
        grad_query = low(
            self.query_inv * self.query_gain * grad_query_normed
            - self.query_raw * self.query_inv**3 * (query_dot / (HEADS * HD))[:, None]
        )
        grad_key = low(
            self.key_inv * self.key_gain * grad_key_normed
            - self.key_raw * self.key_inv**3 * (key_dot / (HEADS * HD))[:, None]
        )
        grad_value = low(value_grad.reshape(rows, -1))
        grad_joint = jnp.concatenate([grad_query, grad_key, grad_value], axis=1)
        joint_total = sum_low(contract_rows(self.normed, grad_joint), ("dp", "context"))
        term = contract_last(grad_joint, self.weight)
        grad_normed = lax.psum_scatter(
            low(term), "expert", scatter_dimension=0, tiled=True
        ).astype(jnp.float32)
        gains_total = lax.psum(
            (
                jnp.sum(self.query_raw * self.query_inv * grad_query_normed, axis=0),
                jnp.sum(self.key_raw * self.key_inv * grad_key_normed, axis=0),
            ),
            ("dp", "context"),
        )
        return (grad_normed, *jnp.split(joint_total, 3, axis=1), *gains_total, output_total)


class Experts:
    def __init__(self, routes, capacity, gate_weight, up_weight, down_weight):
        tok_rows = routes.shape[0]
        expert = lax.axis_index("context") * lax.axis_size("expert") + lax.axis_index("expert")
        self.expert = expert
        everyone = lax.all_gather(routes.T, TOKEN_AXES, axis=0)
        member = jnp.any(everyone == expert, axis=1)
        token = jnp.arange(tok_rows, dtype=jnp.int32)
        before = low(token[:, None] < token[None, :])
        slots = jnp.dot(low(member), before, preferred_element_type=jnp.float32)
        slot_index = jnp.arange(capacity, dtype=jnp.int32)
        matches = slots.astype(jnp.int32)[:, None, :] == slot_index[None, :, None]
        self.picks = (matches & member[:, None, :]).astype(jnp.float32)
        self.pick = low(self.picks)
        gate_all, up_all = (
            lax.all_gather(w[0], "dp", axis=1, tiled=True) for w in (gate_weight, up_weight)
        )
        self.joint = jnp.concatenate([gate_all, up_all], axis=1)
        self.down = lax.all_gather(down_weight[0], "dp", axis=0, tiled=True)

    def rows_of(self, tokens):
        blocks = tokens.reshape(self.pick.shape[0], self.pick.shape[2], -1)
        rows = jnp.einsum("bst,btd->bsd", self.pick, blocks, preferred_element_type=jnp.float32)
        return rows.reshape(-1, blocks.shape[2])

    def tokens_of(self, pick, rows):
        blocks = low(rows).reshape(pick.shape[0], pick.shape[1], -1)
        tokens = jnp.einsum("bst,bsd->btd", pick, blocks, preferred_element_type=jnp.float32)
        return tokens.reshape(-1, blocks.shape[2])

    def forward(self, ffn_in, gates):
        everyone = lax.all_gather(gates.T, TOKEN_AXES, axis=0)
        gates_here = lax.dynamic_index_in_dim(everyone, self.expert, 1, keepdims=False)
        scaled_picks = self.picks * gates_here[:, None, :]
        self.row_gates = jnp.sum(scaled_picks, axis=-1).reshape(-1, 1)
        self.rows = low(self.rows_of(gather_sequence(ffn_in)))
        joint = low(jnp.dot(self.rows, self.joint, preferred_element_type=jnp.float32))
        self.gate_part, self.up_part = jnp.split(joint, 2, axis=1)
        silu_value, _ = silu_parts(self.gate_part.astype(jnp.float32))
        self.hidden = low(silu_value * self.up_part.astype(jnp.float32))
        self.out = low(jnp.dot(self.hidden, self.down, preferred_element_type=jnp.float32))
        return scatter_sequence(self.tokens_of(low(scaled_picks), self.out))

    def backward(self, grad_out):
        grads = self.rows_of(gather_sequence(low(grad_out)))
        gate_grads = jnp.sum(grads * self.out.astype(jnp.float32), axis=-1)
        tok_rows = self.picks.shape[2]
        gate_grads = jnp.sum(
            self.picks * gate_grads.reshape(self.picks.shape[:2])[:, :, None], axis=1
        )
        grad_gates = lax.all_to_all(
            gate_grads, TOKEN_AXES, split_axis=0, concat_axis=0, tiled=True
        ).T
        grad_rows_out = low(grads * self.row_gates)
        grad_hidden = contract_last(grad_rows_out, self.down)
        silu_value, silu_slope = silu_parts(self.gate_part.astype(jnp.float32))
        grad_joint = low(
            jnp.concatenate(
                [
                    grad_hidden * self.up_part.astype(jnp.float32) * silu_slope,
                    grad_hidden * silu_value,
                ],
                axis=1,
            )
        )
        grad_rows = contract_last(grad_joint, self.joint)
        grad_ffn = scatter_sequence(self.tokens_of(self.pick, grad_rows))
        joint_grad = contract_rows(self.rows, grad_joint)
        gate_grad, up_grad = jnp.split(joint_grad, 2, axis=1)
        down_grad = contract_rows(self.hidden, grad_rows_out)
        weight_grads = tuple(
            sum_half_over_dp(g, axis)[None]
            for g, axis in ((gate_grad, 1), (up_grad, 1), (down_grad, 0))
        )
        return grad_ffn, grad_gates, weight_grads


def per_device(
    block_input,
    teacher_states,
    seq_lengths,
    expert_routes,
    attn_gain,
    query_weight,
    key_weight,
    value_weight,
    query_gain,
    key_gain,
    output_weight,
    ffn_gain,
    router_weight,
    gate_weight,
    up_weight,
    down_weight,
):
    tok_rows = block_input.shape[0]
    experts_all = router_weight.shape[1]
    capacity = 5 * tok_rows * TOPK // (4 * experts_all)
    context_size = lax.axis_size("context")
    expert_size = lax.axis_size("expert")
    token_count_all = tok_rows * lax.axis_size("dp") * context_size * expert_size
    length = seq_lengths[0]
    own_start = (
        lax.axis_index("context") * expert_size + lax.axis_index("expert")
    ) * tok_rows
    tokens = block_input.astype(jnp.float32)
    inverse_one = rms_scale(tokens)
    normed = low(tokens * inverse_one * attn_gain)
    heads_here = query_weight.shape[1] // HD
    attention_kind = HeadAttention if heads_here == context_size else BlockAttention
    attention = attention_kind(
        normed,
        length,
        (query_weight, key_weight, value_weight),
        (query_gain, key_gain),
        output_weight,
    )
    experts = Experts(expert_routes, capacity, gate_weight, up_weight, down_weight)
    residual = tokens + attention.output()
    inverse_two = rms_scale(residual)
    ffn_in = low(residual * inverse_two * ffn_gain)
    logits = jnp.dot(ffn_in, router_weight, preferred_element_type=jnp.float32)
    weights_router = jnp.exp(logits - jnp.max(logits, axis=-1, keepdims=True))
    router_probs = weights_router / jnp.sum(weights_router, axis=-1, keepdims=True)
    expert_ids = jnp.arange(experts_all, dtype=jnp.int32)
    chosen = jnp.any(expert_routes[:, :, None] == expert_ids, axis=1)
    mixture = experts.forward(ffn_in, jnp.where(chosen, router_probs, 0.0))
    output_full = residual + mixture
    own_pos = own_start + jnp.arange(tok_rows, dtype=jnp.int32)
    valid = (own_pos < length).astype(jnp.float32)
    difference = output_full - teacher_states
    local_loss = jnp.sum(jnp.sum(difference * difference, axis=-1) * valid)
    count_total = lax.psum(length, "dp").astype(jnp.float32)
    grad_out = difference * (valid * (token_count_all / count_total))[:, None]
    grad_ffn_experts, grad_gates, expert_grads = experts.backward(grad_out)
    grad_router_probs = jnp.where(chosen, grad_gates, 0.0)
    grad_logits = router_probs * (
        grad_router_probs - jnp.sum(router_probs * grad_router_probs, axis=-1, keepdims=True)
    )
    router_grad = lax.dot_general(
        ffn_in.astype(jnp.float32),
        grad_logits,
        (((0,), (0,)), ((), ())),
        precision=lax.Precision.HIGHEST,
    )
    grad_ffn = grad_ffn_experts + lax.dot_general(
        grad_logits,
        router_weight.astype(jnp.float32),
        (((1,), (1,)), ((), ())),
        precision=lax.Precision.HIGHEST,
    )
    ffn_gain_grad = jnp.sum(residual * inverse_two * grad_ffn, axis=0)
    weighted_two = grad_ffn * ffn_gain
    grad_residual = (
        grad_out
        + inverse_two * weighted_two
        - residual * inverse_two**3 * jnp.mean(residual * weighted_two, axis=-1, keepdims=True)
    )
    (
        grad_normed,
        query_total,
        key_total,
        value_total,
        query_gain_total,
        key_gain_total,
        output_total,
    ) = attention.backward(low(grad_residual))
    attn_gain_grad = jnp.sum(tokens * inverse_one * grad_normed, axis=0)
    weighted_one = grad_normed * attn_gain
    input_grad = (
        grad_residual
        + inverse_one * weighted_one
        - tokens * inverse_one**3 * jnp.mean(tokens * weighted_one, axis=-1, keepdims=True)
    )
    loss_total, ffn_total, router_total = lax.psum(
        (local_loss, ffn_gain_grad, router_grad), ALL_AXES
    )
    attn_total = lax.psum(attn_gain_grad, ALL_AXES)
    return (
        low(output_full),
        loss_total / count_total,
        input_grad,
        attn_total,
        query_total,
        key_total,
        value_total,
        query_gain_total,
        key_gain_total,
        output_total,
        ffn_total,
        router_total,
        *expert_grads,
    )


def solution(mesh):
    rows = P(ALL_AXES, None)
    placed = (
        rows,
        rows,
        P("dp"),
        rows,
        P(),
        P(None, "expert"),
        P(None, "expert"),
        P(None, "expert"),
        P("expert"),
        P("expert"),
        P("expert", None),
        P(),
        P(),
        P(TOKEN_AXES, None, "dp"),
        P(TOKEN_AXES, None, "dp"),
        P(TOKEN_AXES, "dp", None),
    )
    return jax.shard_map(
        per_device,
        mesh=mesh,
        in_specs=placed,
        out_specs=(
            rows,
            P(),
            rows,
            P(),
            P(None, "expert"),
            P(None, "expert"),
            P(None, "expert"),
            P("expert"),
            P("expert"),
            P("expert", None),
            P(),
            P(),
            P(TOKEN_AXES, None, "dp"),
            P(TOKEN_AXES, None, "dp"),
            P(TOKEN_AXES, "dp", None),
        ),
        check_vma=False,
    )
```

```python
import functools
import math

import jax
import jax.numpy as jnp
from jax import lax
from jax.experimental import pallas as pl
from jax.experimental.pallas import tpu as pltpu
from jax.sharding import PartitionSpec as P

HEADS = 16
HD = 128
TOPK = 8


EPSILON = 1e-05
ROPE_BASE = 10000.0
NEGATIVE = -1e30
LOG2E = math.log2(math.e)
SCORE_SCALE = HD ** (-0.5)
TOKEN_AXES = ("context", "expert")
ALL_AXES = ("dp", "context", "expert")
VMEM_LIMIT = 56 * 2**20


def rms_scale(values):
    return lax.rsqrt(jnp.mean(values * values, axis=-1, keepdims=True) + EPSILON)


def rope_tables(positions):
    exponent = jnp.arange(HD // 2, dtype=jnp.float32) * (2.0 / HD)
    angles = positions.astype(jnp.float32)[:, None] * (ROPE_BASE ** (-exponent))[None, :]
    return (jnp.cos(angles), jnp.sin(angles))


def rotate(values, cosine, sine_part):
    halfway = values.shape[-1] // 2
    leading = values[..., :halfway]
    trailing = values[..., halfway:]
    cos_wide = cosine[:, None, :]
    sin_wide = sine_part[:, None, :]
    return jnp.concatenate(
        [leading * cos_wide - trailing * sin_wide, trailing * cos_wide + leading * sin_wide],
        axis=-1,
    )


def rotate_back(gradient, cosine, sine_part):
    return rotate(gradient, cosine, -sine_part)


def silu_parts(gate_part):
    sigmoid = jax.nn.sigmoid(gate_part)
    return (gate_part * sigmoid, sigmoid * (1.0 + gate_part * (1.0 - sigmoid)))


def contract(left, right, left_dim, right_dim):
    return lax.dot_general(
        left,
        right,
        (((left_dim,), (right_dim,)), ((), ())),
        preferred_element_type=jnp.float32,
    )


def contract_rows(left, right):
    return contract(left, right, 0, 0)


def contract_last(left, right):
    return contract(left, right, 1, 1)


def low(values):
    return values.astype(jnp.bfloat16)


def steps_back(axis, size, stride=1):
    group = size * stride
    total = lax.axis_size(axis)
    return tuple(
        (i, i // group * group + (i + stride) % group) for i in range(total)
    )


def moved(values, axis, pairs):
    return jax.tree.map(lambda v: lax.ppermute(v, axis, pairs), values)


def next_on(axis, values):
    return moved(values, axis, steps_back(axis, lax.axis_size(axis)))


def next_chip(values):
    return moved(values, "expert", steps_back("expert", chips_of_expert(), 2))


def partner(values):
    pairs = tuple((i, i ^ 1) for i in range(lax.axis_size("expert")))
    return moved(values, "expert", pairs)


def chips_of_expert():
    return lax.axis_size("expert") // 2


def together(*values):
    return lax.optimization_barrier(values)


def place_of(z, e):
    return z, e // 2, e % 2


def relative_to_absolute():
    ring, chips = (lax.axis_size("context"), chips_of_expert())
    z, x, c = place_of(lax.axis_index("context"), lax.axis_index("expert"))
    r = jnp.arange(ring * chips * 2, dtype=jnp.int32)
    s, dc, dx = (r // (2 * chips), r // chips % 2, r % chips)
    return ((z + ring - s) % ring * chips + (x + chips - dx) % chips) * 2 + (c + dc) % 2


def absolute_to_relative():
    ring, chips = (lax.axis_size("context"), chips_of_expert())
    z, x, c = place_of(lax.axis_index("context"), lax.axis_index("expert"))
    b = jnp.arange(ring * chips * 2, dtype=jnp.int32)
    bz, bx, bc = (b // (2 * chips), b // 2 % chips, b % 2)
    return ((z + ring - bz) % ring * 2 + (c + bc) % 2) * chips + (x + chips - bx) % chips


def reorder(blocks, order):
    count = blocks.shape[0]
    onehot = (order[:, None] == jnp.arange(count, dtype=jnp.int32)[None, :]).astype(jnp.float32)
    moved = lax.dot_general(
        onehot,
        blocks.reshape(count, -1),
        (((1,), (0,)), ((), ())),
        precision=lax.Precision.HIGHEST,
    )
    return moved.reshape(blocks.shape)


def gather_expert(rows):
    parts = [rows]
    for _ in range(chips_of_expert() - 1):
        parts.append(next_chip(parts[-1]))
    return parts + [partner(p) for p in parts]


def gather_chunks(rows, work, beside=(), slack=0):
    ring = lax.axis_size("context")
    results, done = ([], [])
    for s in range(ring):
        following = next_on("context", rows) if s < ring - 1 else rows
        parts = [rows]
        for _ in range(chips_of_expert() - 1):
            parts.append(next_chip(parts[-1]))
        extra = beside[s] if s < len(beside) else ()
        due = s - 1 - slack
        result = results[due] if due >= 0 else None
        following, parts[-1], result, extra = together(following, parts[-1], result, extra)
        if due >= 0:
            results[due] = result
        done.append(extra)
        results.append(work(s, parts + [partner(p) for p in parts]))
        rows = following
    return results, done


def scatter_expert(kept, sent, waiting=None, beside=()):
    terms = kept.astype(jnp.float32) + partner(low(sent)).astype(jnp.float32)
    running = low(terms[1])
    running, waiting, beside = together(running, waiting, beside)
    if waiting is not None:
        waiting = next_on("context", waiting)
    for d in range(2, terms.shape[0]):
        running = low(terms[d] + next_chip(running).astype(jnp.float32))
    total = terms[0] + next_chip(running).astype(jnp.float32)
    if waiting is not None:
        total = total + waiting.astype(jnp.float32)
    return total, beside


def scatter_chunks(term, works):
    ring = lax.axis_size("context")
    total, result = (None, ())
    for i, s in enumerate((*range(1, ring), 0)):
        arrays, work = works[i]
        kept, sent = term(s)
        waiting = None if total is None else low(total)
        total, (result, arrays) = scatter_expert(kept, sent, waiting, (result, arrays))
        result = work(result, *arrays)
    return total, result


def ring_sum_begin(parts, axis):
    running = parts[1]
    for part in parts[2:]:
        running = part + next_on(axis, low(running)).astype(jnp.float32)
    return parts[0], next_on(axis, low(running))


def ring_sum(parts, axis):
    kept, received = ring_sum_begin(parts, axis)
    return kept + received.astype(jnp.float32)


def ring_parts(values, axis, dim):
    size, me = (lax.axis_size(axis), lax.axis_index(axis))
    share = values.shape[dim] // size
    return [
        lax.dynamic_slice_in_dim(values, ((me - d) % size) * share, share, dim)
        for d in range(size)
    ]


def ring_gather(values, axis):
    parts = [values]
    for _ in range(lax.axis_size(axis) - 1):
        parts.append(next_on(axis, parts[-1]))
    return parts


def small_sum(values, axes):
    for axis in axes:
        size = lax.axis_size(axis)
        parts = [values] + [
            lax.ppermute(values, axis, tuple((i, i ^ bits) for i in range(size)))
            for bits in range(1, size)
        ]
        while len(parts) > 1:
            parts = [left + right for left, right in zip(parts[::2], parts[1::2])]
        values = parts[0]
    return values


def gather_block(rows):
    return lax.all_gather(rows, "expert", axis=0, tiled=True)


def sum_low(values, axes):
    return lax.psum(low(values), axes).astype(jnp.float32)


def as_row(column):
    return jnp.broadcast_to(column, (column.shape[0], HD)).T[0:1, :]


def project_kernel(places_ref, *refs, count):
    blocks, weight_ref = (refs[:count], refs[count])
    raw_ref, copy_ref, square_ref, member_ref = refs[-4:]
    width = weight_ref.shape[0]
    for i, block_ref in enumerate(blocks):

        @pl.when(pl.program_id(0) == i)
        def _(block_ref=block_ref):
            rows = block_ref[:, :width]
            raw = contract(rows, weight_ref[...], 1, 0)
            raw_ref[...] = raw
            copy_ref[...] = rows
            for j in range(2):
                part = raw[:, j * HD : (j + 1) * HD]
                square_ref[j : j + 1, :] = as_row(jnp.sum(part * part, axis=1, keepdims=True))
            chosen = block_ref[:, width:].astype(jnp.float32)
            lane = lax.broadcasted_iota(jnp.int32, chosen.shape, 1)
            here = lane == places_ref[count]
            member = jnp.sum(jnp.where(here, chosen, 0.0), axis=1, keepdims=True)
            member_ref[0] = as_row(member)


def project_chunk(blocks, weight, places, before, total_rows):
    count = len(blocks)
    tok_rows = blocks[0].shape[0]
    width, columns = weight.shape
    whole = fixed_spec(*blocks[0].shape)
    outs = [
        (
            (total_rows, columns),
            jnp.float32,
            pl.BlockSpec((tok_rows, columns), lambda i, places: (places[i], 0)),
        ),
        (
            (total_rows, width),
            jnp.bfloat16,
            pl.BlockSpec((tok_rows, width), lambda i, places: (places[i], 0)),
        ),
        (
            (2, total_rows),
            jnp.float32,
            pl.BlockSpec((2, tok_rows), lambda i, places: (0, places[i])),
        ),
        (
            (count, 1, tok_rows),
            jnp.float32,
            pl.BlockSpec((1, 1, tok_rows), lambda i, places: (i, 0, 0)),
        ),
    ]
    return chunk_call(
        functools.partial(project_kernel, count=count),
        (*blocks, weight),
        [whole] * count + [fixed_spec(width, columns)],
        outs,
        dict(enumerate(before)),
        [],
        count,
        pl.CostEstimate(
            flops=2 * count * tok_rows * width * columns,
            bytes_accessed=4 * count * tok_rows * width + 2 * width * columns,
            transcendentals=0,
        ),
        (places,),
    )


def inverse_norms(totals):
    return lax.rsqrt(totals * (1.0 / (HEADS * HD)) + EPSILON).T


def turn_kernel(raw_ref, total_ref, gain_ref, cos_ref, sin_ref, q_ref, k_ref, v_ref):
    inverse = inverse_norms(total_ref[...])
    cosine, sine_part = (cos_ref[...], sin_ref[...])
    for i, (out_ref, factor) in enumerate(((q_ref, SCORE_SCALE * LOG2E), (k_ref, 1.0))):
        values = raw_ref[:, i * HD : (i + 1) * HD] * inverse[:, i : i + 1] * gain_ref[i : i + 1, :]
        turned = values * cosine + pltpu.roll(values, HD // 2, 1) * sine_part
        out_ref[...] = low(turned * factor)
    v_ref[...] = low(raw_ref[:, 2 * HD :])


def turned_back(grad, cosine, sine_part):
    return grad * cosine - pltpu.roll(grad, HD // 2, 1) * sine_part


def turn_grad_kernel(
    raw_ref, total_ref, gain_ref, cos_ref, sin_ref, dq_ref, dk_ref, dots_ref, gains_ref
):
    @pl.when(pl.program_id(0) == 0)
    def _():
        gains_ref[...] = jnp.zeros_like(gains_ref)

    inverse = inverse_norms(total_ref[...])
    for i, grad_ref in enumerate((dq_ref, dk_ref)):
        back = turned_back(grad_ref[...], cos_ref[...], sin_ref[...])
        scaled = raw_ref[:, i * HD : (i + 1) * HD] * back
        dots = jnp.sum(scaled * gain_ref[i : i + 1, :], axis=1, keepdims=True)
        dots_ref[i : i + 1, :] = as_row(dots)
        gains_ref[i : i + 1, :] += jnp.sum(scaled * inverse[:, i : i + 1], axis=0, keepdims=True)


def norm_grad_kernel(
    places_ref,
    raw_ref,
    total_ref,
    gain_ref,
    cos_ref,
    sin_ref,
    dq_ref,
    dk_ref,
    dv_ref,
    dots_ref,
    out_ref,
    relative_ref,
    *,
    share,
):
    inverse = inverse_norms(total_ref[...])
    dots = dots_ref[...].T
    for i, grad_ref in enumerate((dq_ref, dk_ref)):
        back = turned_back(grad_ref[...], cos_ref[...], sin_ref[...])
        raw = raw_ref[:, i * HD : (i + 1) * HD]
        inv = inverse[:, i : i + 1]
        shared = inv * inv * inv * dots[:, i : i + 1] * (1.0 / (HEADS * HD))
        out_ref[:, i * HD : (i + 1) * HD] = low(
            back * gain_ref[i : i + 1, :] * inv - raw * shared
        )
    out_ref[:, 2 * HD :] = low(dv_ref[...])
    spread_relative(places_ref, out_ref, relative_ref, share)


def spread_relative(places_ref, from_ref, to_ref, share):
    ring = places_ref.shape[0] - share
    rows = from_ref.shape[0] // share
    for b in range(share):
        place = pl.multiple_of(places_ref[ring + b] * rows, rows)
        to_ref[pl.ds(place, rows), :] = from_ref[b * rows : (b + 1) * rows, :]


def context_grad_kernel(places_ref, grad_ref, context_ref, out_ref, delta_ref, *, share):
    ring = places_ref.shape[0] - share
    rows = out_ref.shape[0] // share
    for b in range(share):
        place = pl.multiple_of(places_ref[ring + b] * rows, rows)
        here = pl.ds(b * rows, rows)
        grads = grad_ref[pl.ds(place, rows), :]
        out_ref[here, :] = grads
        product = grads.astype(jnp.float32) * context_ref[here, :].astype(jnp.float32)
        delta_ref[0:1, here] = as_row(jnp.sum(product, axis=1, keepdims=True))


def sequence_places():
    ring, chips = (lax.axis_size("context"), chips_of_expert())
    z, x, c = place_of(lax.axis_index("context"), lax.axis_index("expert"))
    distances = (z + ring - jnp.arange(ring, dtype=jnp.int32)) % ring
    b = jnp.arange(2 * chips, dtype=jnp.int32)
    places = (c + b % 2) % 2 * chips + (x + chips - b // 2) % chips
    return jnp.concatenate([distances, places])


def block_call(kernel, arrays, in_specs, out_specs, out_shape, count, places=None):
    prefetch = [] if places is None else [places]
    return pl.pallas_call(
        kernel,
        grid_spec=pltpu.PrefetchScalarGridSpec(
            num_scalar_prefetch=len(prefetch),
            grid=(count,),
            in_specs=in_specs,
            out_specs=out_specs,
        ),
        out_shape=out_shape,
        compiler_params=pltpu.CompilerParams(vmem_limit_bytes=VMEM_LIMIT),
        cost_estimate=pl.CostEstimate(
            flops=2**22, bytes_accessed=2**23, transcendentals=0
        ),
    )(*prefetch, *arrays)


def rows_spec(rows, width):
    return pl.BlockSpec((rows, width), lambda b, *_: (b, 0))


def distance_spec(rows, width):
    return pl.BlockSpec((rows, width), lambda b, places: (places[b], 0))


def scalars_spec(rows, count=8):
    return pl.BlockSpec((count, rows), lambda b, *_: (0, b))


def fixed_spec(*shape):
    return pl.BlockSpec(shape, lambda *_: (0,) * len(shape))


def flash_forward_kernel(
    length_ref, places_ref, q_ref, k_ref, v_ref, out_ref, log_ref, relative_ref, *, block, share
):
    row_block = pl.program_id(0)
    length = length_ref[0]
    queries = q_ref[...]

    def step(j, carry, masked):
        highest, total, acc = carry
        rows = pl.ds(pl.multiple_of(j * block, block), block)
        scores = contract_last(queries, k_ref[rows, :])
        if masked:
            query_pos = row_block * block + lax.broadcasted_iota(jnp.int32, (block, block), 0)
            key_pos = j * block + lax.broadcasted_iota(jnp.int32, (block, block), 1)
            allowed = (key_pos <= query_pos) & (key_pos < length)
            scores = jnp.where(allowed, scores, NEGATIVE)
        higher = jnp.maximum(highest, jnp.max(scores, axis=1, keepdims=True))
        weights = jnp.exp2(scores - higher)
        decay = jnp.exp2(highest - higher)
        total = total * decay + jnp.sum(weights, axis=1, keepdims=True)
        acc = acc * decay + contract(low(weights), v_ref[rows, :], 1, 0)
        return higher, total, acc

    start = (
        jnp.full((block, 1), NEGATIVE, jnp.float32),
        jnp.zeros((block, 1), jnp.float32),
        jnp.zeros((block, HD), jnp.float32),
    )
    full = jnp.minimum(row_block, length // block)
    end = jnp.minimum(row_block + 1, (length + block - 1) // block)
    carry = lax.fori_loop(0, full, lambda j, c: step(j, c, False), start)
    highest, total, acc = lax.fori_loop(full, end, lambda j, c: step(j, c, True), carry)
    out_ref[...] = low(acc / total)
    log_ref[...] = jnp.broadcast_to(highest + jnp.log2(total), (block, HD)).T[:8, :]
    spread_relative(places_ref, out_ref, relative_ref, share)


def flash_forward(queries, keys, values, length, places, block, share):
    rows = queries.shape[0]
    whole = pl.BlockSpec((rows, HD), lambda i, *_: (0, 0))
    part = pl.BlockSpec((block, HD), lambda i, *_: (i, 0))
    return pl.pallas_call(
        functools.partial(flash_forward_kernel, block=block, share=share),
        grid_spec=pltpu.PrefetchScalarGridSpec(
            num_scalar_prefetch=2,
            grid=(rows // block,),
            in_specs=[part, whole, whole],
            out_specs=[
                part,
                pl.BlockSpec((8, block), lambda i, *_: (0, i)),
                pl.BlockSpec((block, HD), lambda i, _, places: (places[i], 0)),
            ],
        ),
        out_shape=[
            jax.ShapeDtypeStruct((rows, HD), jnp.bfloat16),
            jax.ShapeDtypeStruct((8, rows), jnp.float32),
            jax.ShapeDtypeStruct((rows, HD), jnp.bfloat16),
        ],
        compiler_params=pltpu.CompilerParams(vmem_limit_bytes=VMEM_LIMIT),
        cost_estimate=pl.CostEstimate(
            flops=8 * rows * rows * HD // 2,
            bytes_accessed=8 * rows * HD,
            transcendentals=rows * rows // 2,
        ),
    )(length, places, queries, keys, values)


def flash_backward_kernel(
    length_ref, q_ref, do_ref, log_ref, delta_ref, k_ref, v_ref, dq_ref, dk_ref, dv_ref, *, block
):
    key_block = pl.program_id(0)
    count = q_ref.shape[0] // block
    length = length_ref[0]

    @pl.when(key_block == 0)
    def _():
        dq_ref[...] = jnp.zeros_like(dq_ref)

    keys = k_ref[...]
    values = v_ref[...]

    def step(i, carry, masked):
        key_acc, value_acc = carry
        rows = pl.ds(pl.multiple_of(i * block, block), block)
        queries = q_ref[rows, :]
        grads = do_ref[rows, :]
        weights = jnp.exp2(contract_last(keys, queries) - log_ref[0:1, rows])
        if masked:
            query_pos = i * block + lax.broadcasted_iota(jnp.int32, (block, block), 1)
            key_pos = key_block * block + lax.broadcasted_iota(jnp.int32, (block, block), 0)
            allowed = (key_pos <= query_pos) & (key_pos < length)
            weights = jnp.where(allowed, weights, 0.0)
        grad_weights = contract_last(values, grads)
        grad_scores = low(weights * (grad_weights - delta_ref[0:1, rows]))
        value_acc = value_acc + contract(low(weights), grads, 1, 0)
        key_acc = key_acc + contract(grad_scores, queries, 1, 0)
        dq_ref[rows, :] += contract_rows(grad_scores, keys)
        return key_acc, value_acc

    zeros = jnp.zeros((block, HD), jnp.float32)
    beyond = key_block * block >= length
    ragged = (key_block + 1) * block > length
    start = jnp.where(beyond, count, key_block)
    masked_end = jnp.where(ragged, count, key_block + 1)
    carry = lax.fori_loop(start, masked_end, lambda i, c: step(i, c, True), (zeros, zeros))
    key_acc, value_acc = lax.fori_loop(
        masked_end, count, lambda i, c: step(i, c, False), carry
    )
    dk_ref[...] = key_acc * (1.0 / LOG2E)
    dv_ref[...] = value_acc

    @pl.when(key_block == count - 1)
    def _():
        dq_ref[...] = dq_ref[...] * SCORE_SCALE


def flash_backward(queries, keys, values, grads, logs, delta, length, block):
    rows = queries.shape[0]
    whole = pl.BlockSpec((rows, HD), lambda j, _: (0, 0))
    part = pl.BlockSpec((block, HD), lambda j, _: (j, 0))
    return pl.pallas_call(
        functools.partial(flash_backward_kernel, block=block),
        grid_spec=pltpu.PrefetchScalarGridSpec(
            num_scalar_prefetch=1,
            grid=(rows // block,),
            in_specs=[
                whole,
                whole,
                pl.BlockSpec((8, rows), lambda j, _: (0, 0)),
                pl.BlockSpec((8, rows), lambda j, _: (0, 0)),
                part,
                part,
            ],
            out_specs=[whole, part, part],
        ),
        out_shape=[jax.ShapeDtypeStruct((rows, HD), jnp.float32)] * 3,
        compiler_params=pltpu.CompilerParams(vmem_limit_bytes=VMEM_LIMIT),
        cost_estimate=pl.CostEstimate(
            flops=20 * rows * rows * HD // 2,
            bytes_accessed=20 * rows * HD,
            transcendentals=rows * rows // 2,
        ),
    )(length, queries, grads, logs, delta, keys, values)


def finish(pending):
    return [(kept + received.astype(jnp.float32))[None] for kept, received in pending]


def permute_by(axis, values, distance):
    size = lax.axis_size(axis)
    return lax.ppermute(values, axis, tuple((i, (i + distance) % size) for i in range(size)))


class HeadAttention:
    def __init__(self, normed, length, weights, gains, output_weight, experts, count):
        self.ring = ring = lax.axis_size("context")
        self.share = share = 2 * chips_of_expert()
        self.tok_rows = tok_rows = normed.shape[0]
        self.block = block = share * tok_rows
        self.rows = rows = ring * block
        self.length = length.reshape(1)
        head = lax.axis_index("context")

        def mine(array):
            return lax.dynamic_slice_in_dim(array, head * HD, HD, array.ndim - 1)

        self.weight = jnp.concatenate([mine(w) for w in weights], axis=1)
        self.gains = jnp.pad(jnp.stack([mine(g) for g in gains]), ((0, 6), (0, 0)))
        self.output_weight = jnp.concatenate(
            [
                lax.dynamic_slice_in_dim(output_weight, (head + d) % ring * HD, HD, 0)
                for d in range(ring)
            ]
        )
        self.places = sequence_places()
        absolute = relative_to_absolute()
        cosine, sine_part = rope_tables(jnp.arange(rows, dtype=jnp.int32))
        tables = (
            jnp.concatenate([cosine, cosine], axis=1),
            jnp.concatenate([-sine_part, sine_part], axis=1),
        )
        made = [()]

        def project(s, blocks):
            places = absolute[s * share : (s + 1) * share]
            places = jnp.concatenate([places, experts.expert.reshape(1).astype(jnp.int32)])
            results = project_chunk(blocks, self.weight, places, made[0], rows)
            made[0] = results[:3]
            experts.pick(results[3][:, 0, :])
            return results[3]

        gates, ups, downs = experts.weights
        _, done = gather_chunks(
            jnp.concatenate([normed, experts.chosen], axis=1),
            project,
            [(), (tables, gates), (), ups],
            1,
        )
        tables, gates = done[1]
        self.count_total = count
        self.raw, self.normed, squares = made[0]
        squares, downs = together(squares, downs)
        experts.weights = (gates, done[3], downs)
        totals = small_sum(squares, TOKEN_AXES)
        self.common = (self.raw, totals, self.gains, *tables)
        self.common_specs = [
            rows_spec(block, 3 * HD),
            scalars_spec(block, 2),
            fixed_spec(8, HD),
            rows_spec(block, HD),
            rows_spec(block, HD),
        ]
        self.queries, self.keys, self.values = block_call(
            turn_kernel,
            self.common,
            self.common_specs,
            [rows_spec(block, HD)] * 3,
            [jax.ShapeDtypeStruct((rows, HD), jnp.bfloat16)] * 3,
            ring,
        )
        self.context, self.logs, pieces = flash_forward(
            self.queries, self.keys, self.values, self.length, self.places, block, share
        )
        pieces = jnp.split(pieces, ring)
        self.context_block = jnp.concatenate(
            [pieces[0]] + [permute_by("context", pieces[d], -d) for d in range(1, ring)], axis=1
        )

    def output(self):
        shape = (self.share // 2, self.tok_rows, self.output_weight.shape[1])
        half = self.block // 2
        kept, sent = (
            contract(part, self.output_weight, 1, 0).reshape(shape)
            for part in (self.context_block[:half], self.context_block[half:])
        )
        return scatter_expert(kept, sent)[0]

    def backward(self, grad_attn, sums, pending):
        tok_rows, ring, block, rows = (self.tok_rows, self.ring, self.block, self.rows)
        block_grad = gather_expert(grad_attn)
        sums, block_grad[-1] = together(small_sum(sums, ("context",)), block_grad[-1])
        block_grad = jnp.concatenate(block_grad)
        grad_context = low(contract_last(block_grad, self.output_weight))
        sums, grad_context = together(sums, grad_context)
        sums = small_sum(sums, ("expert",))
        pieces = jnp.split(grad_context, ring, axis=1)
        pieces = jnp.concatenate(
            [pieces[0]] + [permute_by("context", pieces[d], d) for d in range(1, ring)]
        )
        grad_context, delta = block_call(
            functools.partial(context_grad_kernel, share=self.share),
            (pieces, self.context),
            [distance_spec(block, HD), rows_spec(block, HD)],
            [rows_spec(block, HD), scalars_spec(block)],
            [
                jax.ShapeDtypeStruct((rows, HD), jnp.bfloat16),
                jax.ShapeDtypeStruct((8, rows), jnp.float32),
            ],
            ring,
            self.places,
        )
        sums, delta = together(sums, delta)
        sums = small_sum(sums, ("dp",))
        output_grad = contract_rows(self.context_block, block_grad)
        head = lax.axis_index("context")
        output_grad = jnp.concatenate(
            [
                lax.dynamic_slice_in_dim(output_grad, (h + ring - head) % ring * HD, HD, 0)
                for h in range(ring)
            ]
        )
        output_total = lax.psum(low(output_grad), ("dp", "context"))
        query_grad, key_grad, value_grad = flash_backward(
            self.queries,
            self.keys,
            self.values,
            grad_context,
            self.logs,
            delta,
            self.length,
            block,
        )
        kept, received = zip(*pending)
        query_grad, kept = together(query_grad, kept)
        self.finished = finish(zip(kept, received))
        dots, gain_grads = block_call(
            turn_grad_kernel,
            (*self.common, query_grad, key_grad),
            self.common_specs + [rows_spec(block, HD)] * 2,
            [scalars_spec(block, 2), fixed_spec(8, HD)],
            [
                jax.ShapeDtypeStruct((2, rows), jnp.float32),
                jax.ShapeDtypeStruct((8, HD), jnp.float32),
            ],
            ring,
        )
        dots = small_sum(dots, TOKEN_AXES)
        grad_joint, relative = block_call(
            functools.partial(norm_grad_kernel, share=self.share),
            (*self.common, query_grad, key_grad, value_grad, dots),
            self.common_specs + [rows_spec(block, HD)] * 3 + [scalars_spec(block, 2)],
            [rows_spec(block, 3 * HD), distance_spec(block, 3 * HD)],
            [jax.ShapeDtypeStruct((rows, 3 * HD), jnp.bfloat16)] * 2,
            ring,
            self.places,
        )
        half = block // 2

        def term(s):
            return tuple(
                contract_last(relative[start : start + half], self.weight).reshape(
                    -1, tok_rows, self.weight.shape[0]
                )
                for start in (s * block, s * block + half)
            )

        joint = JointTotal(ring, self.weight.shape[0] // lax.axis_size("dp"))

        def first(_, rows, right, gain_grads):
            joint_grad = contract_rows(rows, right)
            product = jnp.sum(joint_grad * self.weight.astype(jnp.float32), axis=1)
            here = (lax.axis_index("expert") * ring + head) * HD
            gains = lax.dynamic_update_slice(
                jnp.zeros((2, product.shape[0]), jnp.float32), gain_grads[:2], (0, here)
            )
            share = ring_sum(ring_parts(joint_grad, "dp", 0), "dp")
            return (low(share), jnp.concatenate([product[None], gains]), ())

        def later(i):
            def work(result):
                piece, gains, outs = result
                joint.outs = outs
                joint.add(piece, i)
                axes = ("expert", "context", "dp")
                gains = small_sum(gains, axes[i : i + 1])
                return (next_on("context", piece), gains, joint.outs)

            return work

        works = [((self.normed, grad_joint, gain_grads), first)]
        works += [((), later(i)) for i in range(ring - 1)]
        total, (piece, gains, joint.outs) = scatter_chunks(term, works)
        if ring < 4:
            gains = small_sum(gains, ("expert", "context", "dp")[ring - 1 :])
        joint.add(piece, ring - 1)
        output_total, total = together(output_total, total)
        return (
            total,
            sums,
            gains[0],
            *joint.outs,
            *lax.dynamic_slice_in_dim(
                gains[1:], lax.axis_index("expert") * ring * HD, ring * HD, 1
            ),
            output_total.astype(jnp.float32),
        )


def spread_kernel(place_ref, in_ref, *refs):
    for i, out_ref in enumerate(refs[-3:]):
        out_ref[...] = in_ref[:, i * HD : (i + 1) * HD].astype(jnp.float32)


class JointTotal:
    def __init__(self, ring, rows):
        self.ring, self.rows = (ring, rows)
        self.outs = ()

    def add(self, piece, distance):
        ring, rows, size = (self.ring, self.rows, lax.axis_size("dp"))
        head = (lax.axis_index("context") + ring - distance) % ring
        for j, part in enumerate(ring_gather(piece, "dp")):
            half = (lax.axis_index("dp") + size - j) % size
            self.outs = pl.pallas_call(
                spread_kernel,
                grid_spec=pltpu.PrefetchScalarGridSpec(
                    num_scalar_prefetch=1,
                    grid=(1,),
                    in_specs=[fixed_spec(rows, 3 * HD)]
                    + [pl.BlockSpec(memory_space=pl.ANY)] * len(self.outs),
                    out_specs=[pl.BlockSpec((rows, HD), lambda i, place: (place[0], place[1]))]
                    * 3,
                ),
                out_shape=[jax.ShapeDtypeStruct((rows * size, ring * HD), jnp.float32)] * 3,
                input_output_aliases={2 + i: i for i in range(len(self.outs))},
                compiler_params=pltpu.CompilerParams(vmem_limit_bytes=VMEM_LIMIT),
                cost_estimate=pl.CostEstimate(
                    flops=0, bytes_accessed=18 * rows * HD, transcendentals=0
                ),
            )(jnp.stack([half, head]).astype(jnp.int32), part, *self.outs)


class BlockAttention:
    def __init__(self, normed, length, weights, gains, output_weight, experts, count):
        self.tok_rows = normed.shape[0]
        self.output_weight = output_weight
        self.count_total = count
        gather_chunks(experts.chosen, lambda s, blocks: experts.pick(experts.here(blocks)))
        self.length = length
        self.query_gain, self.key_gain = gains
        self.head_width = head_width = weights[0].shape[1]
        self.heads = head_width // HD
        self.weight = jnp.concatenate(weights, axis=1)
        self.normed = gather_block(normed)
        self.rows = rows = self.normed.shape[0]
        self.block_start = lax.axis_index("context") * rows
        projected = jnp.dot(self.normed, self.weight, preferred_element_type=jnp.float32)
        self.query_raw = projected[:, :head_width]
        self.key_raw = projected[:, head_width : 2 * head_width]
        value_raw = projected[:, 2 * head_width :]
        query_total, key_total = lax.psum(
            (jnp.sum(self.query_raw**2, axis=-1), jnp.sum(self.key_raw**2, axis=-1)), "expert"
        )
        self.query_inv = lax.rsqrt(query_total / (HEADS * HD) + EPSILON)[:, None]
        self.key_inv = lax.rsqrt(key_total / (HEADS * HD) + EPSILON)[:, None]
        self.tables = rope_tables(self.block_start + jnp.arange(rows, dtype=jnp.int32))
        query_rot = self.turn(self.query_raw * self.query_inv * self.query_gain, rotate)
        key_rot = self.turn(self.key_raw * self.key_inv * self.key_gain, rotate)
        self.keys, self.values = (
            lax.all_gather(low(key_rot), "context", axis=0, tiled=True),
            lax.all_gather(
                low(value_raw.reshape(rows, self.heads, HD)), "context", axis=0, tiled=True
            ),
        )
        self.query_block = min(512, rows)
        self.count = rows // self.query_block
        self.starts = jnp.arange(self.count, dtype=jnp.int32) * self.query_block
        self.queries = self.in_blocks(low(query_rot))

        def forward_block(packed):
            query_part, offset = packed
            masked, _ = self.scores_for(query_part, offset)
            highest = jnp.max(masked, axis=-1, keepdims=True)
            scores = jnp.exp(masked - highest)
            totals = jnp.sum(scores, axis=-1, keepdims=True)
            context = jnp.einsum(
                "hqk,khd->qhd",
                low(scores / totals),
                self.values,
                preferred_element_type=jnp.float32,
            )
            return (context, (highest + jnp.log(totals))[..., 0])

        context, self.logs = lax.map(forward_block, (self.queries, self.starts))
        self.context = low(context.reshape(rows, head_width))

    def turn(self, values, how):
        return how(values.reshape(self.rows, self.heads, HD), *self.tables)

    def in_blocks(self, values):
        return values.reshape(self.count, self.query_block, self.heads, HD)

    def scores_for(self, query_part, offset):
        raw_scores = (
            jnp.einsum("qhd,khd->hqk", query_part, self.keys, preferred_element_type=jnp.float32)
            * SCORE_SCALE
        )
        key_pos = jnp.arange(self.keys.shape[0], dtype=jnp.int32)
        query_pos = self.block_start + offset + jnp.arange(self.query_block, dtype=jnp.int32)
        allowed = (key_pos[None, :] <= query_pos[:, None]) & (key_pos[None, :] < self.length)
        return (jnp.where(allowed[None], raw_scores, NEGATIVE), allowed)

    def output(self):
        term = jnp.dot(self.context, self.output_weight, preferred_element_type=jnp.float32)
        return lax.psum_scatter(low(term), "expert", scatter_dimension=0, tiled=True).astype(
            jnp.float32
        )

    def backward(self, grad_attn, sums, pending):
        self.finished = finish(pending)
        sums = small_sum(sums, ALL_AXES)
        rows, heads = (self.rows, self.heads)
        block_grad = gather_block(grad_attn)
        output_total = sum_low(contract_rows(self.context, block_grad), ("dp", "context"))
        grad_blocks = self.in_blocks(low(contract_last(block_grad, self.output_weight)))

        def backward_block(running, packed):
            key_acc, value_acc = running
            query_part, grad_part, log_part, offset = packed
            masked, allowed = self.scores_for(query_part, offset)
            probs = jnp.where(allowed[None], jnp.exp(masked - log_part[..., None]), 0.0)
            grad_probs = jnp.einsum(
                "qhd,khd->hqk", grad_part, self.values, preferred_element_type=jnp.float32
            )
            row_dot = jnp.sum(probs * grad_probs, axis=-1, keepdims=True)
            grad_scores = low(probs * (grad_probs - row_dot))
            query_grad = (
                jnp.einsum(
                    "hqk,khd->qhd", grad_scores, self.keys, preferred_element_type=jnp.float32
                )
                * SCORE_SCALE
            )
            key_acc = (
                key_acc
                + jnp.einsum(
                    "hqk,qhd->khd", grad_scores, query_part, preferred_element_type=jnp.float32
                )
                * SCORE_SCALE
            )
            value_acc = value_acc + jnp.einsum(
                "hqk,qhd->khd", low(probs), grad_part, preferred_element_type=jnp.float32
            )
            return ((key_acc, value_acc), query_grad)

        zeros = jnp.zeros((self.keys.shape[0], heads, HD), jnp.float32)
        (key_acc, value_acc), query_grads = lax.scan(
            backward_block, (zeros, zeros), (self.queries, grad_blocks, self.logs, self.starts)
        )
        key_grad, value_grad = (
            lax.psum_scatter(low(acc), "context", scatter_dimension=0, tiled=True).astype(
                jnp.float32
            )
            for acc in (key_acc, value_acc)
        )
        grad_query_normed = self.turn(query_grads, rotate_back).reshape(rows, -1)
        grad_key_normed = self.turn(key_grad, rotate_back).reshape(rows, -1)
        query_dot, key_dot = lax.psum(
            (
                jnp.sum(self.query_raw * self.query_gain * grad_query_normed, axis=-1),
                jnp.sum(self.key_raw * self.key_gain * grad_key_normed, axis=-1),
            ),
            "expert",
        )
        grad_query = low(
            self.query_inv * self.query_gain * grad_query_normed
            - self.query_raw * self.query_inv**3 * (query_dot / (HEADS * HD))[:, None]
        )
        grad_key = low(
            self.key_inv * self.key_gain * grad_key_normed
            - self.key_raw * self.key_inv**3 * (key_dot / (HEADS * HD))[:, None]
        )
        grad_value = low(value_grad.reshape(rows, -1))
        grad_joint = jnp.concatenate([grad_query, grad_key, grad_value], axis=1)
        joint_total = sum_low(contract_rows(self.normed, grad_joint), ("dp", "context"))
        term = contract_last(grad_joint, self.weight)
        grad_normed = lax.psum_scatter(
            low(term), "expert", scatter_dimension=0, tiled=True
        ).astype(jnp.float32)
        gains_total = lax.psum(
            (
                jnp.sum(self.query_raw * self.query_inv * grad_query_normed, axis=0),
                jnp.sum(self.key_raw * self.key_inv * grad_key_normed, axis=0),
            ),
            ("dp", "context"),
        )
        gain_product = jnp.sum(joint_total * self.weight.astype(jnp.float32), axis=1)
        gain_product = lax.psum(gain_product, "expert")
        return (
            grad_normed,
            sums,
            gain_product,
            *jnp.split(joint_total, 3, axis=1),
            *gains_total,
            output_total,
        )


UNIT_TILE = 256
WIDTH_TILE = 512


def expert_forward_kernel(expert_ref, *refs, count, experts_all, unit_tiles):
    blocks = refs[:count]
    pick_ref, router_ref, gate_weight_ref, up_weight_ref, down_weight_ref = refs[
        count : count + 5
    ]
    (
        rows_ref,
        gate_ref,
        up_ref,
        hidden_ref,
        out_ref,
        row_gate_ref,
        kept_ref,
        sent_ref,
        scaled_ref,
        units_ref,
    ) = refs[-10:]
    step = pl.program_id(0)
    capacity = pick_ref.shape[1]

    @pl.when(step == 0)
    def _():
        for i, block_ref in enumerate(blocks):
            here = pl.ds(i * capacity, capacity)
            tokens = block_ref[...]
            pick = pick_ref[i]
            rows_ref[here, :] = low(contract(pick, tokens, 1, 0))
            logits = contract(tokens, router_ref[...], 1, 0)
            lane = lax.broadcasted_iota(jnp.int32, logits.shape, 1)
            logits = jnp.where(lane < experts_all, logits, NEGATIVE)
            weights = jnp.exp(logits - jnp.max(logits, axis=1, keepdims=True))
            chosen = jnp.sum(
                jnp.where(lane == expert_ref[0], weights, 0.0), axis=1, keepdims=True
            )
            gates = as_row(chosen / jnp.sum(weights, axis=1, keepdims=True))
            scaled = pick.astype(jnp.float32) * gates
            scaled_ref[i] = low(scaled)
            row_gates = jnp.sum(scaled, axis=1, keepdims=True)
            row_gate_ref[here, :] = jnp.broadcast_to(row_gates, (capacity, HD))

    @pl.when(step < unit_tiles)
    def _():
        rows = rows_ref[...]
        gate_part = contract(rows, gate_weight_ref[...], 1, 0)
        up_part = contract(rows, up_weight_ref[...], 1, 0)
        hidden = low(silu_parts(gate_part)[0] * up_part)
        gate_ref[...] = low(gate_part)
        up_ref[...] = low(up_part)
        hidden_ref[...] = hidden
        for j in range(unit_tiles):

            @pl.when(step == j)
            def _(j=j):
                units_ref[:, j * UNIT_TILE : (j + 1) * UNIT_TILE] = hidden

    @pl.when(step >= unit_tiles)
    def _():
        out_ref[...] = low(contract(units_ref[...], down_weight_ref[...], 1, 0))
        spread_tokens(scaled_ref, out_ref, kept_ref, sent_ref)


def spread_tokens(pick_ref, rows_ref, kept_ref, sent_ref):
    count, capacity, tok_rows = pick_ref.shape
    half = count // 2
    for i in range(count):
        terms = contract_rows(pick_ref[i], rows_ref[pl.ds(i * capacity, capacity), :])
        if i < half:
            kept_ref[i] = low(terms)
        else:
            sent_ref[i - half] = low(terms)


def expert_backward_kernel(*refs, count, unit_tiles):
    blocks = refs[:count]
    (
        pick_ref,
        row_gate_ref,
        gate_ref,
        up_ref,
        out_ref,
        down_weight_ref,
        gate_weight_ref,
        up_weight_ref,
    ) = refs[count : count + 8]
    (
        gate_grad_ref,
        grad_out_ref,
        grad_gate_ref,
        grad_up_ref,
        kept_ref,
        sent_ref,
        gates_ref,
        ups_ref,
        rows_ref,
    ) = refs[-9:]
    step = pl.program_id(0)
    capacity = pick_ref.shape[1]

    @pl.when(step == 0)
    def _():
        for i, block_ref in enumerate(blocks):
            here = pl.ds(i * capacity, capacity)
            pick = pick_ref[i]
            grads = contract(pick, block_ref[...], 1, 0)
            dots = jnp.sum(grads * out_ref[here, :].astype(jnp.float32), axis=1, keepdims=True)
            gate_grad_ref[i : i + 1, :] = jnp.sum(
                pick.astype(jnp.float32) * dots, axis=0, keepdims=True
            )
            grad_out_ref[here, :] = low(grads * row_gate_ref[here, 0:1])

    @pl.when(step < unit_tiles)
    def _():
        grad_hidden = contract_last(grad_out_ref[...], down_weight_ref[...])
        silu_value, silu_slope = silu_parts(gate_ref[...].astype(jnp.float32))
        grad_gate = low(grad_hidden * up_ref[...].astype(jnp.float32) * silu_slope)
        grad_up = low(grad_hidden * silu_value)
        grad_gate_ref[...] = grad_gate
        grad_up_ref[...] = grad_up
        for j in range(unit_tiles):

            @pl.when(step == j)
            def _(j=j):
                gates_ref[:, j * UNIT_TILE : (j + 1) * UNIT_TILE] = grad_gate
                ups_ref[:, j * UNIT_TILE : (j + 1) * UNIT_TILE] = grad_up

    @pl.when(step >= unit_tiles)
    def _():
        rows_ref[...] = low(
            contract_last(gates_ref[...], gate_weight_ref[...])
            + contract_last(ups_ref[...], up_weight_ref[...])
        )
        spread_tokens(pick_ref, rows_ref, kept_ref, sent_ref)


def chunk_call(kernel, arrays, in_specs, outs, before, scratch, steps, cost, prefetch=()):
    first = len(prefetch) + len(arrays)
    return pl.pallas_call(
        kernel,
        grid_spec=pltpu.PrefetchScalarGridSpec(
            num_scalar_prefetch=len(prefetch),
            grid=(steps,),
            in_specs=in_specs + [pl.BlockSpec(memory_space=pl.ANY)] * len(before),
            out_specs=[out[2] for out in outs],
            scratch_shapes=scratch,
        ),
        out_shape=[jax.ShapeDtypeStruct(out[0], out[1]) for out in outs],
        input_output_aliases={first + i: j for i, j in enumerate(before)},
        compiler_params=pltpu.CompilerParams(vmem_limit_bytes=VMEM_LIMIT),
        cost_estimate=cost,
    )(*prefetch, *arrays, *before.values())


class Experts:
    def __init__(self, routes, capacity, router_weight, gate_weight, up_weight, down_weight):
        self.capacity = -(-capacity // 16) * 16
        self.experts_all = router_weight.shape[1]
        self.expert = lax.axis_index("context") * lax.axis_size("expert") + lax.axis_index(
            "expert"
        )
        self.router_weight = jnp.pad(router_weight, ((0, 0), (0, HD - self.experts_all)))
        expert_ids = jnp.arange(HD, dtype=jnp.int32)
        self.chosen = low(jnp.any(routes[:, :, None] == expert_ids, axis=1))
        gates = ring_gather(gate_weight[0], "dp")
        _, up_first = together(gates[-1], up_weight[0])
        ups = ring_gather(up_first, "dp")
        _, down_first = together(ups[-1], down_weight[0])
        self.weights = (gates, ups, ring_gather(down_first, "dp"))
        self.picks = []

    def here(self, blocks):
        lane = jnp.arange(HD, dtype=jnp.int32) == self.expert
        return jnp.sum(jnp.where(lane, jnp.stack(blocks).astype(jnp.float32), 0.0), axis=-1)

    def pick(self, here):
        member = here > 0
        tok_rows = member.shape[1]
        token = jnp.arange(tok_rows, dtype=jnp.int32)
        before = low(token[:, None] < token[None, :])
        slots = contract(low(member), before, 1, 0).astype(jnp.int32)
        slot_index = jnp.arange(self.capacity, dtype=jnp.int32)
        matches = slots[:, None, :] == slot_index[None, :, None]
        self.picks.append(low(matches & member[:, None, :]))

    def begin(self):
        self.gate_weight, self.up_weight = (
            jnp.concatenate(parts, axis=1) for parts in self.weights[:2]
        )
        self.down_weight = jnp.concatenate(self.weights[2], axis=0)
        self.units = self.gate_weight.shape[1]
        self.picks = jnp.stack(self.picks)
        self.chained, self.chained_back = ((), ())
        self.terms, self.terms_back = ({}, {})

    def shapes(self):
        ring, count, capacity, tok_rows = self.picks.shape
        width = self.gate_weight.shape[0]
        return ring, count, count * capacity, tok_rows, width

    def plan(self, s):
        ring, count, rows, tok_rows, width = self.shapes()
        tiles = self.units // UNIT_TILE
        tile = math.gcd(WIDTH_TILE, width)

        def unit(j):
            return jnp.minimum(j, tiles - 1)

        def column(j):
            return jnp.maximum(j - tiles, 0)

        half = count // 2
        all_rows = ring * rows
        term = (
            (half, tok_rows, width),
            jnp.bfloat16,
            pl.BlockSpec((half, tok_rows, tile), lambda j, *_: (0, 0, column(j))),
        )
        unit_spec = pl.BlockSpec((rows, UNIT_TILE), lambda j, *_: (s, unit(j)))
        whole_spec = pl.BlockSpec((rows, width), lambda j, *_: (s, 0))
        scalar_spec = pl.BlockSpec((rows, HD), lambda j, *_: (s, 0))
        column_spec = pl.BlockSpec((rows, tile), lambda j, *_: (s, column(j)))
        block_specs = [pl.BlockSpec((tok_rows, width), lambda j, *_: (0, 0))] * count
        pick_spec = pl.BlockSpec((None, *self.picks.shape[1:]), lambda j, *_: (s, 0, 0, 0))
        narrow = ((all_rows, self.units), jnp.bfloat16, unit_spec)
        wide = ((all_rows, width), jnp.bfloat16, whole_spec)
        cost = pl.CostEstimate(
            flops=6 * rows * width * self.units,
            bytes_accessed=6 * self.units * width + 12 * rows * width,
            transcendentals=rows * self.units,
        )
        return (
            unit,
            column,
            tiles,
            tile,
            term,
            unit_spec,
            whole_spec,
            scalar_spec,
            column_spec,
            block_specs,
            pick_spec,
            narrow,
            wide,
            cost,
        )

    def forward_chunk(self, s, blocks):
        ring, count, rows, tok_rows, width = self.shapes()
        (
            unit,
            column,
            tiles,
            tile,
            term,
            unit_spec,
            whole_spec,
            scalar_spec,
            column_spec,
            block_specs,
            pick_spec,
            narrow,
            wide,
            cost,
        ) = self.plan(s)
        results = chunk_call(
            functools.partial(
                expert_forward_kernel,
                count=count,
                experts_all=self.experts_all,
                unit_tiles=tiles,
            ),
            (
                *blocks,
                self.picks,
                self.router_weight,
                self.gate_weight,
                self.up_weight,
                self.down_weight,
            ),
            [
                *block_specs,
                pick_spec,
                fixed_spec(width, HD),
                pl.BlockSpec((width, UNIT_TILE), lambda j, *_: (0, unit(j))),
                pl.BlockSpec((width, UNIT_TILE), lambda j, *_: (0, unit(j))),
                pl.BlockSpec((self.units, tile), lambda j, *_: (0, column(j))),
            ],
            [
                wide,
                narrow,
                narrow,
                narrow,
                (wide[0], wide[1], column_spec),
                ((ring * rows, HD), jnp.float32, scalar_spec),
                term,
                term,
            ],
            dict(enumerate(self.chained)),
            [
                pltpu.VMEM(self.picks.shape[1:], jnp.bfloat16),
                pltpu.VMEM((rows, self.units), jnp.bfloat16),
            ],
            tiles + width // tile,
            cost,
            (self.expert.reshape(1).astype(jnp.int32),),
        )
        self.chained = results[:6]
        self.terms[s] = results[6:]
        return results[7]

    def forward(self, ffn_in):
        last = lax.axis_size("context") - 1
        done, _ = gather_chunks(ffn_in, self.forward_chunk, slack=1)
        idle = ((), lambda result: result)
        works = [((), lambda result: done[last])] + [idle] * last
        mixture, _ = scatter_chunks(lambda s: self.terms[s], works)
        return mixture

    def backward_chunk(self, s, blocks):
        ring, count, rows, tok_rows, width = self.shapes()
        (
            unit,
            column,
            tiles,
            tile,
            term,
            unit_spec,
            whole_spec,
            scalar_spec,
            column_spec,
            block_specs,
            pick_spec,
            narrow,
            wide,
            cost,
        ) = self.plan(s)
        chunk_rows, gate_part, up_part, hidden, out, row_gates = self.chained
        results = chunk_call(
            functools.partial(expert_backward_kernel, count=count, unit_tiles=tiles),
            (
                *blocks,
                self.picks,
                row_gates,
                gate_part,
                up_part,
                out,
                self.down_weight,
                self.gate_weight,
                self.up_weight,
            ),
            [
                *block_specs,
                pick_spec,
                scalar_spec,
                unit_spec,
                unit_spec,
                whole_spec,
                pl.BlockSpec((UNIT_TILE, width), lambda j, *_: (unit(j), 0)),
                pl.BlockSpec((tile, self.units), lambda j, *_: (column(j), 0)),
                pl.BlockSpec((tile, self.units), lambda j, *_: (column(j), 0)),
            ],
            [
                ((count, tok_rows), jnp.float32, fixed_spec(count, tok_rows)),
                wide,
                narrow,
                narrow,
                term,
                term,
            ],
            {j + 1: array for j, array in enumerate(self.chained_back)},
            [
                pltpu.VMEM((rows, self.units), jnp.bfloat16),
                pltpu.VMEM((rows, self.units), jnp.bfloat16),
                pltpu.VMEM((rows, tile), jnp.bfloat16),
            ],
            tiles + width // tile,
            cost,
        )
        self.chained_back = results[1:4]
        self.terms_back[s] = results[4:]
        return results[0]

    def backward(self, grad_out):
        last = lax.axis_size("context") - 1
        gate_grads, _ = gather_chunks(low(grad_out), self.backward_chunk, slack=1)
        grad_rows_out, grad_gate, grad_up = self.chained_back
        chunk_rows, hidden = (self.chained[0], self.chained[3])
        size = lax.axis_size("dp")

        def parts(left, right, axis):
            return jnp.split(contract_rows(left, right), size, axis=axis)

        def first(_):
            return gate_grads[last]

        def second(_, grad, rows, right):
            grad_gates = lax.all_to_all(
                reorder(grad, absolute_to_relative()),
                TOKEN_AXES,
                split_axis=0,
                concat_axis=0,
                tiled=True,
            ).T
            return grad_gates, parts(rows, right, 1)

        def third(result, rows, right):
            return *result, parts(rows, right, 1)

        works = [((), first)] + [((), lambda result: result)] * last
        works[1] = ((jnp.concatenate(gate_grads), chunk_rows, grad_gate), second)
        works[2] = ((chunk_rows, grad_up), third)
        grad_ffn, (grad_gates, *grads) = scatter_chunks(lambda s: self.terms_back[s], works)
        grads.append(parts(hidden, grad_rows_out, 0))
        pending = [ring_sum_begin(part, "dp") for part in grads]
        return grad_ffn, grad_gates, pending


def per_device(
    block_input,
    teacher_states,
    seq_lengths,
    expert_routes,
    attn_gain,
    query_weight,
    key_weight,
    value_weight,
    query_gain,
    key_gain,
    output_weight,
    ffn_gain,
    router_weight,
    gate_weight,
    up_weight,
    down_weight,
):
    tok_rows = block_input.shape[0]
    experts_all = router_weight.shape[1]
    capacity = 5 * tok_rows * TOPK // (4 * experts_all)
    context_size = lax.axis_size("context")
    expert_size = lax.axis_size("expert")
    token_count_all = tok_rows * lax.axis_size("dp") * context_size * expert_size
    length = seq_lengths[0]
    own_start = (
        lax.axis_index("context") * expert_size + lax.axis_index("expert")
    ) * tok_rows
    tokens = block_input.astype(jnp.float32)
    inverse_one = rms_scale(tokens)
    normed = low(tokens * inverse_one * attn_gain)
    heads_here = query_weight.shape[1] // HD
    count_total = small_sum(jnp.full((8, 128), length, jnp.int32), ("dp",))
    count_total, gate_weight = together(count_total, gate_weight)
    experts = Experts(
        expert_routes, capacity, router_weight, gate_weight, up_weight, down_weight
    )
    attention_kind = HeadAttention if heads_here == context_size else BlockAttention
    attention = attention_kind(
        normed,
        length,
        (query_weight, key_weight, value_weight),
        (query_gain, key_gain),
        output_weight,
        experts,
        count_total,
    )
    experts.begin()
    count_total = attention.count_total[0, 0].astype(jnp.float32)
    residual = tokens + attention.output()
    inverse_two = rms_scale(residual)
    ffn_in = low(residual * inverse_two * ffn_gain)
    logits = jnp.dot(ffn_in, router_weight, preferred_element_type=jnp.float32)
    weights_router = jnp.exp(logits - jnp.max(logits, axis=-1, keepdims=True))
    router_probs = weights_router / jnp.sum(weights_router, axis=-1, keepdims=True)
    expert_ids = jnp.arange(experts_all, dtype=jnp.int32)
    chosen = jnp.any(expert_routes[:, :, None] == expert_ids, axis=1)
    mixture = experts.forward(ffn_in)
    output_full = residual + mixture
    own_pos = own_start + jnp.arange(tok_rows, dtype=jnp.int32)
    valid = (own_pos < length).astype(jnp.float32)
    difference = output_full - teacher_states
    local_loss = jnp.sum(jnp.sum(difference * difference, axis=-1) * valid)
    grad_out = difference * (valid * (token_count_all / count_total))[:, None]
    grad_ffn_experts, grad_gates, pending = experts.backward(grad_out)
    grad_router_probs = jnp.where(chosen, grad_gates, 0.0)
    grad_logits = router_probs * (
        grad_router_probs - jnp.sum(router_probs * grad_router_probs, axis=-1, keepdims=True)
    )
    router_grad = lax.dot_general(
        grad_logits,
        ffn_in.astype(jnp.float32),
        (((0,), (0,)), ((), ())),
        precision=lax.Precision.HIGHEST,
    )
    grad_ffn = grad_ffn_experts + lax.dot_general(
        grad_logits,
        router_weight.astype(jnp.float32),
        (((1,), (1,)), ((), ())),
        precision=lax.Precision.HIGHEST,
    )
    ffn_gain_grad = jnp.sum(residual * inverse_two * grad_ffn, axis=0)
    weighted_two = grad_ffn * ffn_gain
    grad_residual = (
        grad_out
        + inverse_two * weighted_two
        - residual * inverse_two**3 * jnp.mean(residual * weighted_two, axis=-1, keepdims=True)
    )
    sums = jnp.concatenate(
        [
            router_grad,
            ffn_gain_grad[None],
            jnp.broadcast_to(local_loss, ffn_gain_grad.shape)[None],
        ]
    )
    (
        grad_normed,
        sums,
        attn_gain_product,
        query_total,
        key_total,
        value_total,
        query_gain_total,
        key_gain_total,
        output_total,
    ) = attention.backward(low(grad_residual), sums, pending)
    weighted_one = grad_normed * attn_gain
    input_grad = (
        grad_residual
        + inverse_one * weighted_one
        - tokens * inverse_one**3 * jnp.mean(tokens * weighted_one, axis=-1, keepdims=True)
    )
    router_total, ffn_total = (sums[:experts_all].T, sums[experts_all])
    loss_total = sums[experts_all + 1, 0]
    return (
        low(output_full),
        loss_total / count_total,
        input_grad,
        attn_gain_product / attn_gain,
        query_total,
        key_total,
        value_total,
        query_gain_total,
        key_gain_total,
        output_total,
        ffn_total,
        router_total,
        *attention.finished,
    )


def solution(mesh):
    rows = P(ALL_AXES, None)
    placed = (
        rows,
        rows,
        P("dp"),
        rows,
        P(),
        P(None, "expert"),
        P(None, "expert"),
        P(None, "expert"),
        P("expert"),
        P("expert"),
        P("expert", None),
        P(),
        P(),
        P(TOKEN_AXES, None, "dp"),
        P(TOKEN_AXES, None, "dp"),
        P(TOKEN_AXES, "dp", None),
    )
    return jax.shard_map(
        per_device,
        mesh=mesh,
        in_specs=placed,
        out_specs=(
            rows,
            P(),
            rows,
            P(),
            P(None, "expert"),
            P(None, "expert"),
            P(None, "expert"),
            P("expert"),
            P("expert"),
            P("expert", None),
            P(),
            P(),
            P(TOKEN_AXES, None, "dp"),
            P(TOKEN_AXES, None, "dp"),
            P(TOKEN_AXES, "dp", None),
        ),
        check_vma=False,
    )
```

```python
import functools
import math

import jax
import jax.numpy as jnp
from jax import lax
from jax.experimental import pallas as pl
from jax.experimental.pallas import tpu as pltpu
from jax.sharding import PartitionSpec as P

HEADS = 16
HD = 128
TOPK = 8


EPSILON = 1e-05
ROPE_BASE = 10000.0
NEGATIVE = -1e30
LOG2E = math.log2(math.e)
SCORE_SCALE = HD ** (-0.5)
TOKEN_AXES = ("context", "expert")
ALL_AXES = ("dp", "context", "expert")
VMEM_LIMIT = 56 * 2**20


def takes(microseconds):
    return pl.CostEstimate(
        flops=int(microseconds * 1.1e9), bytes_accessed=int(microseconds * 3e6), transcendentals=0
    )


def rms_scale(values):
    return lax.rsqrt(jnp.mean(values * values, axis=-1, keepdims=True) + EPSILON)


def rope_tables(positions):
    exponent = jnp.arange(HD // 2, dtype=jnp.float32) * (2.0 / HD)
    angles = positions.astype(jnp.float32)[:, None] * (ROPE_BASE ** (-exponent))[None, :]
    return (jnp.cos(angles), jnp.sin(angles))


def rotate(values, cosine, sine_part):
    halfway = values.shape[-1] // 2
    leading = values[..., :halfway]
    trailing = values[..., halfway:]
    cos_wide = cosine[:, None, :]
    sin_wide = sine_part[:, None, :]
    return jnp.concatenate(
        [leading * cos_wide - trailing * sin_wide, trailing * cos_wide + leading * sin_wide],
        axis=-1,
    )


def rotate_back(gradient, cosine, sine_part):
    return rotate(gradient, cosine, -sine_part)


def silu_parts(gate_part):
    sigmoid = jax.nn.sigmoid(gate_part)
    return (gate_part * sigmoid, sigmoid * (1.0 + gate_part * (1.0 - sigmoid)))


def contract(left, right, left_dim, right_dim):
    return lax.dot_general(
        left,
        right,
        (((left_dim,), (right_dim,)), ((), ())),
        preferred_element_type=jnp.float32,
    )


def contract_rows(left, right):
    return contract(left, right, 0, 0)


def contract_last(left, right):
    return contract(left, right, 1, 1)


def low(values):
    return values.astype(jnp.bfloat16)


def steps_back(axis, size, stride=1):
    group = size * stride
    total = lax.axis_size(axis)
    return tuple(
        (i, i // group * group + (i + stride) % group) for i in range(total)
    )


def moved(values, axis, pairs):
    return jax.tree.map(lambda v: lax.ppermute(v, axis, pairs), values)


def next_on(axis, values):
    return moved(values, axis, steps_back(axis, lax.axis_size(axis)))


def next_chip(values):
    return moved(values, "expert", steps_back("expert", chips_of_expert(), 2))


def partner(values):
    pairs = tuple((i, i ^ 1) for i in range(lax.axis_size("expert")))
    return moved(values, "expert", pairs)


def chips_of_expert():
    return lax.axis_size("expert") // 2


def together(*values):
    return lax.optimization_barrier(values)


def place_of(z, e):
    return z, e // 2, e % 2


def relative_to_absolute():
    ring, chips = (lax.axis_size("context"), chips_of_expert())
    z, x, c = place_of(lax.axis_index("context"), lax.axis_index("expert"))
    r = jnp.arange(ring * chips * 2, dtype=jnp.int32)
    s, dc, dx = (r // (2 * chips), r // chips % 2, r % chips)
    return ((z + ring - s) % ring * chips + (x + chips - dx) % chips) * 2 + (c + dc) % 2


def absolute_to_relative():
    ring, chips = (lax.axis_size("context"), chips_of_expert())
    z, x, c = place_of(lax.axis_index("context"), lax.axis_index("expert"))
    b = jnp.arange(ring * chips * 2, dtype=jnp.int32)
    bz, bx, bc = (b // (2 * chips), b // 2 % chips, b % 2)
    return ((z + ring - bz) % ring * 2 + (c + bc) % 2) * chips + (x + chips - bx) % chips


def reorder(blocks, order):
    count = blocks.shape[0]
    onehot = (order[:, None] == jnp.arange(count, dtype=jnp.int32)[None, :]).astype(jnp.float32)
    moved = lax.dot_general(
        onehot,
        blocks.reshape(count, -1),
        (((1,), (0,)), ((), ())),
        precision=lax.Precision.HIGHEST,
    )
    return moved.reshape(blocks.shape)


def gather_expert(rows):
    parts = [rows]
    for _ in range(chips_of_expert() - 1):
        parts.append(next_chip(parts[-1]))
    return parts + [partner(p) for p in parts]


def gather_chunks(rows, work, beside=(), slack=0):
    ring = lax.axis_size("context")
    results, done = ([], [])
    for s in range(ring):
        following = next_on("context", rows) if s < ring - 1 else rows
        parts = [rows]
        for _ in range(chips_of_expert() - 1):
            parts.append(next_chip(parts[-1]))
        extra = beside[s] if s < len(beside) else ()
        due = s - 1 - slack
        result = results[due] if due >= 0 else None
        following, parts[-1], result, extra = together(following, parts[-1], result, extra)
        if due >= 0:
            results[due] = result
        done.append(extra)
        results.append(work(s, parts + [partner(p) for p in parts]))
        rows = following
    return results, done


def core_sum(kept, sent):
    return kept.astype(jnp.float32) + partner(low(sent)).astype(jnp.float32)


def scatter_chips(terms, waiting=None, beside=()):
    running = low(terms[1])
    running, waiting, beside = together(running, waiting, beside)
    if waiting is not None:
        waiting = next_on("context", waiting)
    for d in range(2, terms.shape[0]):
        running = low(terms[d] + next_chip(running).astype(jnp.float32))
    total = terms[0] + next_chip(running).astype(jnp.float32)
    rest = None
    if waiting is not None:
        count = total.shape[0]
        total = total + waiting[:count].astype(jnp.float32)
        rest = waiting[count:]
    return total, rest, beside


def scatter_chunks(term, works, rider=None):
    ring = lax.axis_size("context")
    order = (*range(1, ring), 0)
    total, result = (None, ())
    terms = core_sum(*term(order[0]))
    for i in range(ring):
        arrays, work = works[i]
        ahead = core_sum(*term(order[i + 1])) if i + 1 < ring else None
        waiting = None if total is None else low(total)
        if i:
            if rider is not None:
                waiting = jnp.concatenate([waiting, rider(result)])
            total, rest, (result, arrays, ahead) = scatter_chips(
                terms, waiting, (result, arrays, ahead)
            )
            if rider is not None:
                arrays = (rest, *arrays)
        else:
            total, _, (result, arrays) = scatter_chips(terms, waiting, (result, arrays))
        terms = ahead
        result = work(result, *arrays)
    return total, result


def ring_sum_begin(parts, axis):
    running = parts[1]
    for part in parts[2:]:
        running = part + next_on(axis, low(running)).astype(jnp.float32)
    return parts[0], next_on(axis, low(running))


def ring_sum(parts, axis):
    kept, received = ring_sum_begin(parts, axis)
    return kept + received.astype(jnp.float32)


def ring_parts(values, axis, dim):
    size, me = (lax.axis_size(axis), lax.axis_index(axis))
    share = values.shape[dim] // size
    return [
        lax.dynamic_slice_in_dim(values, ((me - d) % size) * share, share, dim)
        for d in range(size)
    ]


def ring_gather(values, axis):
    parts = [values]
    for _ in range(lax.axis_size(axis) - 1):
        parts.append(next_on(axis, parts[-1]))
    return parts


def small_sum(values, axes):
    for axis in axes:
        size = lax.axis_size(axis)
        parts = [values] + [
            lax.ppermute(values, axis, tuple((i, i ^ bits) for i in range(size)))
            for bits in range(1, size)
        ]
        while len(parts) > 1:
            parts = [left + right for left, right in zip(parts[::2], parts[1::2])]
        values = parts[0]
    return values


def gather_block(rows):
    return lax.all_gather(rows, "expert", axis=0, tiled=True)


def sum_low(values, axes):
    return lax.psum(low(values), axes).astype(jnp.float32)


def as_row(column):
    return jnp.broadcast_to(column, (column.shape[0], HD)).T[0:1, :]


def project_kernel(places_ref, *refs, count):
    blocks, weight_ref = (refs[:count], refs[count])
    raw_ref, copy_ref, square_ref, member_ref = refs[-4:]
    width = weight_ref.shape[0]
    for i, block_ref in enumerate(blocks):

        @pl.when(pl.program_id(0) == i)
        def _(block_ref=block_ref):
            rows = block_ref[:, :width]
            raw = contract(rows, weight_ref[...], 1, 0)
            raw_ref[...] = raw
            copy_ref[...] = rows
            for j in range(2):
                part = raw[:, j * HD : (j + 1) * HD]
                square_ref[j : j + 1, :] = as_row(jnp.sum(part * part, axis=1, keepdims=True))
            chosen = block_ref[:, width:].astype(jnp.float32)
            lane = lax.broadcasted_iota(jnp.int32, chosen.shape, 1)
            here = lane == places_ref[count]
            member = jnp.sum(jnp.where(here, chosen, 0.0), axis=1, keepdims=True)
            member_ref[0] = as_row(member)


def project_chunk(blocks, weight, places, before, total_rows):
    count = len(blocks)
    tok_rows = blocks[0].shape[0]
    width, columns = weight.shape
    whole = fixed_spec(*blocks[0].shape)
    outs = [
        (
            (total_rows, columns),
            jnp.float32,
            pl.BlockSpec((tok_rows, columns), lambda i, places: (places[i], 0)),
        ),
        (
            (total_rows, width),
            jnp.bfloat16,
            pl.BlockSpec((tok_rows, width), lambda i, places: (places[i], 0)),
        ),
        (
            (2, total_rows),
            jnp.float32,
            pl.BlockSpec((2, tok_rows), lambda i, places: (0, places[i])),
        ),
        (
            (count, 1, tok_rows),
            jnp.float32,
            pl.BlockSpec((1, 1, tok_rows), lambda i, places: (i, 0, 0)),
        ),
    ]
    return chunk_call(
        functools.partial(project_kernel, count=count),
        (*blocks, weight),
        [whole] * count + [fixed_spec(width, columns)],
        outs,
        dict(enumerate(before)),
        [],
        count,
        takes(8.5),
        (places,),
    )


def inverse_norms(totals):
    return lax.rsqrt(totals * (1.0 / (HEADS * HD)) + EPSILON).T


def turn_kernel(raw_ref, total_ref, gain_ref, cos_ref, sin_ref, q_ref, k_ref, v_ref):
    inverse = inverse_norms(total_ref[...])
    cosine, sine_part = (cos_ref[...], sin_ref[...])
    for i, (out_ref, factor) in enumerate(((q_ref, SCORE_SCALE * LOG2E), (k_ref, 1.0))):
        values = raw_ref[:, i * HD : (i + 1) * HD] * inverse[:, i : i + 1] * gain_ref[i : i + 1, :]
        turned = values * cosine + pltpu.roll(values, HD // 2, 1) * sine_part
        out_ref[...] = low(turned * factor)
    v_ref[...] = low(raw_ref[:, 2 * HD :])


def turned_back(grad, cosine, sine_part):
    return grad * cosine - pltpu.roll(grad, HD // 2, 1) * sine_part


def turn_grad_kernel(
    raw_ref, total_ref, gain_ref, cos_ref, sin_ref, dq_ref, dk_ref, dots_ref, gains_ref
):
    @pl.when(pl.program_id(0) == 0)
    def _():
        gains_ref[...] = jnp.zeros_like(gains_ref)

    inverse = inverse_norms(total_ref[...])
    for i, grad_ref in enumerate((dq_ref, dk_ref)):
        back = turned_back(grad_ref[...], cos_ref[...], sin_ref[...])
        scaled = raw_ref[:, i * HD : (i + 1) * HD] * back
        dots = jnp.sum(scaled * gain_ref[i : i + 1, :], axis=1, keepdims=True)
        dots_ref[i : i + 1, :] = as_row(dots)
        gains_ref[i : i + 1, :] += jnp.sum(scaled * inverse[:, i : i + 1], axis=0, keepdims=True)


def norm_grad_kernel(
    places_ref,
    raw_ref,
    total_ref,
    gain_ref,
    cos_ref,
    sin_ref,
    dq_ref,
    dk_ref,
    dv_ref,
    dots_ref,
    out_ref,
    relative_ref,
    *,
    share,
):
    inverse = inverse_norms(total_ref[...])
    dots = dots_ref[...].T
    for i, grad_ref in enumerate((dq_ref, dk_ref)):
        back = turned_back(grad_ref[...], cos_ref[...], sin_ref[...])
        raw = raw_ref[:, i * HD : (i + 1) * HD]
        inv = inverse[:, i : i + 1]
        shared = inv * inv * inv * dots[:, i : i + 1] * (1.0 / (HEADS * HD))
        out_ref[:, i * HD : (i + 1) * HD] = low(
            back * gain_ref[i : i + 1, :] * inv - raw * shared
        )
    out_ref[:, 2 * HD :] = low(dv_ref[...])
    spread_relative(places_ref, out_ref, relative_ref, share)


def spread_relative(places_ref, from_ref, to_ref, share):
    ring = places_ref.shape[0] - share
    rows = from_ref.shape[0] // share
    for b in range(share):
        place = pl.multiple_of(places_ref[ring + b] * rows, rows)
        to_ref[pl.ds(place, rows), :] = from_ref[b * rows : (b + 1) * rows, :]


def context_grad_kernel(places_ref, grad_ref, context_ref, out_ref, delta_ref, *, share):
    ring = places_ref.shape[0] - share
    rows = out_ref.shape[0] // share
    for b in range(share):
        place = pl.multiple_of(places_ref[ring + b] * rows, rows)
        here = pl.ds(b * rows, rows)
        grads = grad_ref[pl.ds(place, rows), :]
        out_ref[here, :] = grads
        product = grads.astype(jnp.float32) * context_ref[here, :].astype(jnp.float32)
        delta_ref[0:1, here] = as_row(jnp.sum(product, axis=1, keepdims=True))


def sequence_places():
    ring, chips = (lax.axis_size("context"), chips_of_expert())
    z, x, c = place_of(lax.axis_index("context"), lax.axis_index("expert"))
    distances = (z + ring - jnp.arange(ring, dtype=jnp.int32)) % ring
    b = jnp.arange(2 * chips, dtype=jnp.int32)
    places = (c + b % 2) % 2 * chips + (x + chips - b // 2) % chips
    return jnp.concatenate([distances, places])


def block_call(kernel, arrays, in_specs, out_specs, out_shape, count, time, places=None):
    prefetch = [] if places is None else [places]
    return pl.pallas_call(
        kernel,
        grid_spec=pltpu.PrefetchScalarGridSpec(
            num_scalar_prefetch=len(prefetch),
            grid=(count,),
            in_specs=in_specs,
            out_specs=out_specs,
        ),
        out_shape=out_shape,
        compiler_params=pltpu.CompilerParams(vmem_limit_bytes=VMEM_LIMIT),
        cost_estimate=takes(time),
    )(*prefetch, *arrays)


def rows_spec(rows, width):
    return pl.BlockSpec((rows, width), lambda b, *_: (b, 0))


def distance_spec(rows, width):
    return pl.BlockSpec((rows, width), lambda b, places: (places[b], 0))


def scalars_spec(rows, count=8):
    return pl.BlockSpec((count, rows), lambda b, *_: (0, b))


def fixed_spec(*shape):
    return pl.BlockSpec(shape, lambda *_: (0,) * len(shape))


def flash_forward_kernel(
    length_ref, places_ref, q_ref, k_ref, v_ref, out_ref, log_ref, relative_ref, *, block, share
):
    row_block = pl.program_id(0)
    length = length_ref[0]
    queries = q_ref[...]

    def step(j, carry, masked):
        highest, total, acc = carry
        rows = pl.ds(pl.multiple_of(j * block, block), block)
        scores = contract_last(queries, k_ref[rows, :])
        if masked:
            query_pos = row_block * block + lax.broadcasted_iota(jnp.int32, (block, block), 0)
            key_pos = j * block + lax.broadcasted_iota(jnp.int32, (block, block), 1)
            allowed = (key_pos <= query_pos) & (key_pos < length)
            scores = jnp.where(allowed, scores, NEGATIVE)
        higher = jnp.maximum(highest, jnp.max(scores, axis=1, keepdims=True))
        weights = jnp.exp2(scores - higher)
        decay = jnp.exp2(highest - higher)
        total = total * decay + jnp.sum(weights, axis=1, keepdims=True)
        acc = acc * decay + contract(low(weights), v_ref[rows, :], 1, 0)
        return higher, total, acc

    start = (
        jnp.full((block, 1), NEGATIVE, jnp.float32),
        jnp.zeros((block, 1), jnp.float32),
        jnp.zeros((block, HD), jnp.float32),
    )
    full = jnp.minimum(row_block, length // block)
    end = jnp.minimum(row_block + 1, (length + block - 1) // block)
    carry = lax.fori_loop(0, full, lambda j, c: step(j, c, False), start)
    highest, total, acc = lax.fori_loop(full, end, lambda j, c: step(j, c, True), carry)
    out_ref[...] = low(acc / total)
    log_ref[...] = jnp.broadcast_to(highest + jnp.log2(total), (block, HD)).T[:8, :]
    spread_relative(places_ref, out_ref, relative_ref, share)


def flash_forward(queries, keys, values, length, places, block, share):
    rows = queries.shape[0]
    whole = pl.BlockSpec((rows, HD), lambda i, *_: (0, 0))
    part = pl.BlockSpec((block, HD), lambda i, *_: (i, 0))
    return pl.pallas_call(
        functools.partial(flash_forward_kernel, block=block, share=share),
        grid_spec=pltpu.PrefetchScalarGridSpec(
            num_scalar_prefetch=2,
            grid=(rows // block,),
            in_specs=[part, whole, whole],
            out_specs=[
                part,
                pl.BlockSpec((8, block), lambda i, *_: (0, i)),
                pl.BlockSpec((block, HD), lambda i, _, places: (places[i], 0)),
            ],
        ),
        out_shape=[
            jax.ShapeDtypeStruct((rows, HD), jnp.bfloat16),
            jax.ShapeDtypeStruct((8, rows), jnp.float32),
            jax.ShapeDtypeStruct((rows, HD), jnp.bfloat16),
        ],
        compiler_params=pltpu.CompilerParams(vmem_limit_bytes=VMEM_LIMIT),
        cost_estimate=takes(20.0),
    )(length, places, queries, keys, values)


def flash_backward_kernel(
    length_ref, q_ref, do_ref, log_ref, delta_ref, k_ref, v_ref, dq_ref, dk_ref, dv_ref, *, block
):
    key_block = pl.program_id(0)
    count = q_ref.shape[0] // block
    length = length_ref[0]

    @pl.when(key_block == 0)
    def _():
        dq_ref[...] = jnp.zeros_like(dq_ref)

    keys = k_ref[...]
    values = v_ref[...]

    def step(i, carry, masked):
        key_acc, value_acc = carry
        rows = pl.ds(pl.multiple_of(i * block, block), block)
        queries = q_ref[rows, :]
        grads = do_ref[rows, :]
        weights = jnp.exp2(contract_last(keys, queries) - log_ref[0:1, rows])
        if masked:
            query_pos = i * block + lax.broadcasted_iota(jnp.int32, (block, block), 1)
            key_pos = key_block * block + lax.broadcasted_iota(jnp.int32, (block, block), 0)
            allowed = (key_pos <= query_pos) & (key_pos < length)
            weights = jnp.where(allowed, weights, 0.0)
        grad_weights = contract_last(values, grads)
        grad_scores = low(weights * (grad_weights - delta_ref[0:1, rows]))
        value_acc = value_acc + contract(low(weights), grads, 1, 0)
        key_acc = key_acc + contract(grad_scores, queries, 1, 0)
        dq_ref[rows, :] += contract_rows(grad_scores, keys)
        return key_acc, value_acc

    zeros = jnp.zeros((block, HD), jnp.float32)
    beyond = key_block * block >= length
    ragged = (key_block + 1) * block > length
    start = jnp.where(beyond, count, key_block)
    masked_end = jnp.where(ragged, count, key_block + 1)
    carry = lax.fori_loop(start, masked_end, lambda i, c: step(i, c, True), (zeros, zeros))
    key_acc, value_acc = lax.fori_loop(
        masked_end, count, lambda i, c: step(i, c, False), carry
    )
    dk_ref[...] = key_acc * (1.0 / LOG2E)
    dv_ref[...] = value_acc

    @pl.when(key_block == count - 1)
    def _():
        dq_ref[...] = dq_ref[...] * SCORE_SCALE


def flash_backward(queries, keys, values, grads, logs, delta, length, block):
    rows = queries.shape[0]
    whole = pl.BlockSpec((rows, HD), lambda j, _: (0, 0))
    part = pl.BlockSpec((block, HD), lambda j, _: (j, 0))
    return pl.pallas_call(
        functools.partial(flash_backward_kernel, block=block),
        grid_spec=pltpu.PrefetchScalarGridSpec(
            num_scalar_prefetch=1,
            grid=(rows // block,),
            in_specs=[
                whole,
                whole,
                pl.BlockSpec((8, rows), lambda j, _: (0, 0)),
                pl.BlockSpec((8, rows), lambda j, _: (0, 0)),
                part,
                part,
            ],
            out_specs=[whole, part, part],
        ),
        out_shape=[jax.ShapeDtypeStruct((rows, HD), jnp.float32)] * 3,
        compiler_params=pltpu.CompilerParams(vmem_limit_bytes=VMEM_LIMIT),
        cost_estimate=takes(30.0),
    )(length, queries, grads, logs, delta, keys, values)


def finish(kept, received):
    halves = [part + other.astype(jnp.float32) for part, other in zip(kept, received)]
    return [jnp.concatenate(halves[i : i + 2])[None] for i in (0, 2, 4)]


def place_kernel(order_ref, in_ref, out_ref):
    out_ref[...] = in_ref[...].astype(out_ref.dtype)


def place(blocks, order, dtype):
    count, rows, width = blocks.shape
    return pl.pallas_call(
        place_kernel,
        grid_spec=pltpu.PrefetchScalarGridSpec(
            num_scalar_prefetch=1,
            grid=(count,),
            in_specs=[pl.BlockSpec((1, rows, width), lambda b, order: (order[b], 0, 0))],
            out_specs=pl.BlockSpec((1, rows, width), lambda b, order: (b, 0, 0)),
        ),
        out_shape=jax.ShapeDtypeStruct(blocks.shape, dtype),
        compiler_params=pltpu.CompilerParams(vmem_limit_bytes=VMEM_LIMIT),
        cost_estimate=takes(4.0),
    )(order, blocks)


class OutputTotal:
    def __init__(self, ring, grad):
        self.ring, self.width = (ring, grad.shape[1])
        self.state = ring_parts(grad.reshape(ring, HD, self.width), "dp", 1)

    def over_dp(self):
        self.state = list(ring_sum_begin(self.state, "dp"))
        self.taken = 0

    def step(self):
        ring = self.ring
        if not self.taken:
            kept, received = self.state
            total = kept + received.astype(jnp.float32)
            self.state = [total[(ring - d) % ring] for d in range(ring)]
            arrived = 0.0
        else:
            *self.state, arrived = self.state
            arrived = arrived.astype(jnp.float32)
        self.taken += 1
        self.state = [*self.state, next_on("context", low(self.state[self.taken] + arrived))]

    def finish(self):
        for _ in range(self.taken, self.ring - 1):
            self.step()
        *parts, arrived = self.state
        self.state = [low(parts[0] + arrived.astype(jnp.float32))]

    def collect(self):
        self.state = [*self.state, next_on("context", self.state[-1])]

    def exchange(self):
        here = jnp.stack(self.state)
        self.state = [here, *ring_gather(here, "dp")[1:]]

    def total(self):
        ring, size = (self.ring, lax.axis_size("dp"))
        z, y = (lax.axis_index("context"), lax.axis_index("dp"))
        order = jnp.stack(
            [((y - j) % size) * ring + (z - i) % ring for i in range(ring) for j in range(size)]
        ).astype(jnp.int32)
        placed = place(jnp.concatenate(self.state), order, jnp.float32)
        return placed.reshape(ring * HD, self.width)


def context_terms_kernel(*refs, count):
    blocks, weight_ref, outs = (refs[:count], refs[count], refs[count + 1 :])
    for i, block_ref in enumerate(blocks):

        @pl.when(pl.program_id(0) == i)
        def _(block_ref=block_ref):
            terms = low(contract_last(block_ref[...], weight_ref[...]))
            for d, out_ref in enumerate(outs):
                out_ref[...] = terms[:, d * HD : (d + 1) * HD]


def context_terms(blocks, weight, ring):
    count = len(blocks)
    tok_rows, width = blocks[0].shape
    return pl.pallas_call(
        functools.partial(context_terms_kernel, count=count),
        grid=(count,),
        in_specs=[fixed_spec(tok_rows, width)] * count + [fixed_spec(*weight.shape)],
        out_specs=[rows_spec(tok_rows, HD)] * ring,
        out_shape=[jax.ShapeDtypeStruct((count * tok_rows, HD), jnp.bfloat16)] * ring,
        compiler_params=pltpu.CompilerParams(vmem_limit_bytes=VMEM_LIMIT),
        cost_estimate=takes(6.0),
    )(*blocks, weight)


def permute_by(axis, values, distance):
    size = lax.axis_size(axis)
    return lax.ppermute(values, axis, tuple((i, (i + distance) % size) for i in range(size)))


class HeadAttention:
    def __init__(self, normed, length, weights, gains, output_weight, experts, count):
        self.ring = ring = lax.axis_size("context")
        self.share = share = 2 * chips_of_expert()
        self.tok_rows = tok_rows = normed.shape[0]
        self.block = block = share * tok_rows
        self.rows = rows = ring * block
        self.length = length.reshape(1)
        head = lax.axis_index("context")

        def mine(array):
            return lax.dynamic_slice_in_dim(array, head * HD, HD, array.ndim - 1)

        self.weight = jnp.concatenate([mine(w) for w in weights], axis=1)
        self.gains = jnp.pad(jnp.stack([mine(g) for g in gains]), ((0, 6), (0, 0)))
        self.output_weight = jnp.concatenate(
            [
                lax.dynamic_slice_in_dim(output_weight, (head + d) % ring * HD, HD, 0)
                for d in range(ring)
            ]
        )
        self.places = sequence_places()
        absolute = relative_to_absolute()
        cosine, sine_part = rope_tables(jnp.arange(rows, dtype=jnp.int32))
        tables = (
            jnp.concatenate([cosine, cosine], axis=1),
            jnp.concatenate([-sine_part, sine_part], axis=1),
        )
        made = [()]

        def project(s, blocks):
            places = absolute[s * share : (s + 1) * share]
            places = jnp.concatenate([places, experts.expert.reshape(1).astype(jnp.int32)])
            results = project_chunk(blocks, self.weight, places, made[0], rows)
            made[0] = results[:3]
            experts.pick(results[3][:, 0, :])
            return results[3]

        arriving = experts.arriving
        _, done = gather_chunks(
            jnp.concatenate([normed, experts.chosen], axis=1),
            project,
            [arriving[0], (tables, arriving[1]), arriving[2], (arriving[3], count)],
            1,
        )
        tables, second = done[1]
        fourth, self.count_total = done[3]
        self.raw, self.normed, squares = made[0]
        totals = small_sum(squares, TOKEN_AXES)
        self.common = (self.raw, totals, self.gains, *tables)
        self.common_specs = [
            rows_spec(block, 3 * HD),
            scalars_spec(block, 2),
            fixed_spec(8, HD),
            rows_spec(block, HD),
            rows_spec(block, HD),
        ]
        self.queries, self.keys, self.values = block_call(
            turn_kernel,
            self.common,
            self.common_specs,
            [rows_spec(block, HD)] * 3,
            [jax.ShapeDtypeStruct((rows, HD), jnp.bfloat16)] * 3,
            ring,
            7.5,
        )
        self.queries, fifth = together(self.queries, arriving[4])
        self.context, self.logs, pieces = flash_forward(
            self.queries, self.keys, self.values, self.length, self.places, block, share
        )
        pieces, sixth = together(pieces, arriving[5])
        experts.arriving = [done[0], second, done[2], fourth, fifth, sixth]
        pieces = jnp.split(pieces, ring)
        self.context_block = jnp.concatenate(
            [pieces[0]] + [permute_by("context", pieces[d], -d) for d in range(1, ring)], axis=1
        )

    def output(self):
        shape = (self.share // 2, self.tok_rows, self.output_weight.shape[1])
        half = self.block // 2
        kept, sent = (
            contract(part, self.output_weight, 1, 0).reshape(shape)
            for part in (self.context_block[:half], self.context_block[half:])
        )
        return scatter_chips(core_sum(kept, sent))[0]

    def backward(self, grad_attn, sums, pending):
        tok_rows, ring, block, rows = (self.tok_rows, self.ring, self.block, self.rows)
        kept, received = (list(part) for part in zip(*pending))
        block_grad = gather_expert(grad_attn)
        sums, block_grad[-1], received[2] = together(
            small_sum(sums, ("context",)), block_grad[-1], received[2]
        )
        pieces = context_terms(block_grad, self.output_weight, ring)
        sums, pieces = together(sums, pieces)
        sums = small_sum(sums, ("expert",))
        output_grad = contract_rows(self.context_block, jnp.concatenate(block_grad))
        output_sum = OutputTotal(ring, output_grad)
        pieces = jnp.concatenate(
            [pieces[0]] + [permute_by("context", pieces[d], d) for d in range(1, ring)]
        )
        pieces, output_sum.state, received[3] = together(pieces, output_sum.state, received[3])
        output_sum.over_dp()
        grad_context, delta = block_call(
            functools.partial(context_grad_kernel, share=self.share),
            (pieces, self.context),
            [distance_spec(block, HD), rows_spec(block, HD)],
            [rows_spec(block, HD), scalars_spec(block)],
            [
                jax.ShapeDtypeStruct((rows, HD), jnp.bfloat16),
                jax.ShapeDtypeStruct((8, rows), jnp.float32),
            ],
            ring,
            5.0,
            self.places,
        )
        sums, delta = together(sums, delta)
        sums = small_sum(sums, ("dp",))
        query_grad, key_grad, value_grad = flash_backward(
            self.queries,
            self.keys,
            self.values,
            grad_context,
            self.logs,
            delta,
            self.length,
            block,
        )
        query_grad, kept, received[4], output_sum.state = together(
            query_grad, kept, received[4], output_sum.state
        )
        output_sum.step()
        dots, gain_grads = block_call(
            turn_grad_kernel,
            (*self.common, query_grad, key_grad),
            self.common_specs + [rows_spec(block, HD)] * 2,
            [scalars_spec(block, 2), fixed_spec(8, HD)],
            [
                jax.ShapeDtypeStruct((2, rows), jnp.float32),
                jax.ShapeDtypeStruct((8, HD), jnp.float32),
            ],
            ring,
            10.0,
        )
        dots, output_sum.state = together(dots, output_sum.state)
        output_sum.step()
        dots = small_sum(dots, TOKEN_AXES)
        dots, received[5], output_sum.state = together(dots, received[5], output_sum.state)
        output_sum.step()
        self.finished = finish(kept, received)
        grad_joint, relative = block_call(
            functools.partial(norm_grad_kernel, share=self.share),
            (*self.common, query_grad, key_grad, value_grad, dots),
            self.common_specs + [rows_spec(block, HD)] * 3 + [scalars_spec(block, 2)],
            [rows_spec(block, 3 * HD), distance_spec(block, 3 * HD)],
            [jax.ShapeDtypeStruct((rows, 3 * HD), jnp.bfloat16)] * 2,
            ring,
            12.0,
            self.places,
        )
        grad_joint, relative, output_sum.state = together(grad_joint, relative, output_sum.state)
        output_sum.finish()
        output_sum.collect()
        head = lax.axis_index("context")
        half = block // 2
        width = self.weight.shape[0]
        joint_grad = contract_rows(grad_joint, self.normed)
        here = (lax.axis_index("expert") * ring + head) * HD
        gains = lax.dynamic_update_slice(
            jnp.zeros((2, width), jnp.float32), gain_grads[:2], (0, here)
        )
        parts = ring_parts(joint_grad.reshape(3, HD, width), "dp", 1)
        mine, others = ring_sum_begin([part.reshape(-1, width) for part in parts], "dp")
        relative, mine, output_sum.state = together(relative, mine, output_sum.state)

        def term(s):
            return tuple(
                contract_last(relative[start : start + half], self.weight).reshape(
                    -1, tok_rows, width
                )
                for start in (s * block, s * block + half)
            )

        joint = JointTotal(ring)

        def first(_):
            for _ in range(ring - 2):
                output_sum.collect()
            return low(mine + others.astype(jnp.float32)), (), output_sum.state

        def later(i):
            def work(result, rest):
                piece, joint.outs, output_sum.state = result
                joint.add(piece, i)
                if not i:
                    output_sum.exchange()
                return rest, joint.outs, output_sum.state

            return work

        works = [((), first)] + [((), later(i)) for i in range(ring - 1)]
        total, result = scatter_chunks(term, works, lambda result: result[0])
        piece, joint.outs, output_sum.state = result
        joint.add(piece, ring - 1)
        return total, sums, gains, *joint.outs, output_sum.total()


def spread_kernel(place_ref, *refs, size):
    parts, outs = (refs[:size], refs[-3:])
    rows = HD // size
    for i, out_ref in enumerate(outs):
        slabs = []
        for j in range(size):
            slab = 0.0
            for d, part in enumerate(parts):
                here = part[i * rows : (i + 1) * rows, :].astype(jnp.float32)
                slab = slab + jnp.where(place_ref[1 + d] == j, here, 0.0)
            slabs.append(slab)
        out_ref[...] = jnp.concatenate(slabs, axis=0).T


class JointTotal:
    def __init__(self, ring):
        self.ring = ring
        self.outs = ()

    def add(self, piece, distance):
        ring, size = (self.ring, lax.axis_size("dp"))
        head = (lax.axis_index("context") + ring - distance) % ring
        parts = ring_gather(piece, "dp")
        width = piece.shape[1]
        place = [head] + [(lax.axis_index("dp") + size - d) % size for d in range(size)]
        out = ((width, ring * HD), jnp.float32, pl.BlockSpec((width, HD), lambda i, p: (0, p[0])))
        self.outs = chunk_call(
            functools.partial(spread_kernel, size=size),
            parts,
            [fixed_spec(*piece.shape)] * size,
            [out] * 3,
            dict(enumerate(self.outs)),
            [],
            1,
            takes(5.0),
            (jnp.stack(place).astype(jnp.int32),),
        )


class BlockAttention:
    def __init__(self, normed, length, weights, gains, output_weight, experts, count):
        self.tok_rows = normed.shape[0]
        self.output_weight = output_weight
        self.count_total = count
        gather_chunks(experts.chosen, lambda s, blocks: experts.pick(experts.here(blocks)))
        self.length = length
        self.query_gain, self.key_gain = gains
        self.head_width = head_width = weights[0].shape[1]
        self.heads = head_width // HD
        self.weight = jnp.concatenate(weights, axis=1)
        self.normed = gather_block(normed)
        self.rows = rows = self.normed.shape[0]
        self.block_start = lax.axis_index("context") * rows
        projected = jnp.dot(self.normed, self.weight, preferred_element_type=jnp.float32)
        self.query_raw = projected[:, :head_width]
        self.key_raw = projected[:, head_width : 2 * head_width]
        value_raw = projected[:, 2 * head_width :]
        query_total, key_total = lax.psum(
            (jnp.sum(self.query_raw**2, axis=-1), jnp.sum(self.key_raw**2, axis=-1)), "expert"
        )
        self.query_inv = lax.rsqrt(query_total / (HEADS * HD) + EPSILON)[:, None]
        self.key_inv = lax.rsqrt(key_total / (HEADS * HD) + EPSILON)[:, None]
        self.tables = rope_tables(self.block_start + jnp.arange(rows, dtype=jnp.int32))
        query_rot = self.turn(self.query_raw * self.query_inv * self.query_gain, rotate)
        key_rot = self.turn(self.key_raw * self.key_inv * self.key_gain, rotate)
        self.keys, self.values = (
            lax.all_gather(low(key_rot), "context", axis=0, tiled=True),
            lax.all_gather(
                low(value_raw.reshape(rows, self.heads, HD)), "context", axis=0, tiled=True
            ),
        )
        self.query_block = min(512, rows)
        self.count = rows // self.query_block
        self.starts = jnp.arange(self.count, dtype=jnp.int32) * self.query_block
        self.queries = self.in_blocks(low(query_rot))

        def forward_block(packed):
            query_part, offset = packed
            masked, _ = self.scores_for(query_part, offset)
            highest = jnp.max(masked, axis=-1, keepdims=True)
            scores = jnp.exp(masked - highest)
            totals = jnp.sum(scores, axis=-1, keepdims=True)
            context = jnp.einsum(
                "hqk,khd->qhd",
                low(scores / totals),
                self.values,
                preferred_element_type=jnp.float32,
            )
            return (context, (highest + jnp.log(totals))[..., 0])

        context, self.logs = lax.map(forward_block, (self.queries, self.starts))
        self.context = low(context.reshape(rows, head_width))

    def turn(self, values, how):
        return how(values.reshape(self.rows, self.heads, HD), *self.tables)

    def in_blocks(self, values):
        return values.reshape(self.count, self.query_block, self.heads, HD)

    def scores_for(self, query_part, offset):
        raw_scores = (
            jnp.einsum("qhd,khd->hqk", query_part, self.keys, preferred_element_type=jnp.float32)
            * SCORE_SCALE
        )
        key_pos = jnp.arange(self.keys.shape[0], dtype=jnp.int32)
        query_pos = self.block_start + offset + jnp.arange(self.query_block, dtype=jnp.int32)
        allowed = (key_pos[None, :] <= query_pos[:, None]) & (key_pos[None, :] < self.length)
        return (jnp.where(allowed[None], raw_scores, NEGATIVE), allowed)

    def output(self):
        term = jnp.dot(self.context, self.output_weight, preferred_element_type=jnp.float32)
        return lax.psum_scatter(low(term), "expert", scatter_dimension=0, tiled=True).astype(
            jnp.float32
        )

    def backward(self, grad_attn, sums, pending):
        self.finished = finish(*zip(*pending))
        sums = small_sum(sums, ALL_AXES)
        rows, heads = (self.rows, self.heads)
        block_grad = gather_block(grad_attn)
        output_total = sum_low(contract_rows(self.context, block_grad), ("dp", "context"))
        grad_blocks = self.in_blocks(low(contract_last(block_grad, self.output_weight)))

        def backward_block(running, packed):
            key_acc, value_acc = running
            query_part, grad_part, log_part, offset = packed
            masked, allowed = self.scores_for(query_part, offset)
            probs = jnp.where(allowed[None], jnp.exp(masked - log_part[..., None]), 0.0)
            grad_probs = jnp.einsum(
                "qhd,khd->hqk", grad_part, self.values, preferred_element_type=jnp.float32
            )
            row_dot = jnp.sum(probs * grad_probs, axis=-1, keepdims=True)
            grad_scores = low(probs * (grad_probs - row_dot))
            query_grad = (
                jnp.einsum(
                    "hqk,khd->qhd", grad_scores, self.keys, preferred_element_type=jnp.float32
                )
                * SCORE_SCALE
            )
            key_acc = (
                key_acc
                + jnp.einsum(
                    "hqk,qhd->khd", grad_scores, query_part, preferred_element_type=jnp.float32
                )
                * SCORE_SCALE
            )
            value_acc = value_acc + jnp.einsum(
                "hqk,qhd->khd", low(probs), grad_part, preferred_element_type=jnp.float32
            )
            return ((key_acc, value_acc), query_grad)

        zeros = jnp.zeros((self.keys.shape[0], heads, HD), jnp.float32)
        (key_acc, value_acc), query_grads = lax.scan(
            backward_block, (zeros, zeros), (self.queries, grad_blocks, self.logs, self.starts)
        )
        key_grad, value_grad = (
            lax.psum_scatter(low(acc), "context", scatter_dimension=0, tiled=True).astype(
                jnp.float32
            )
            for acc in (key_acc, value_acc)
        )
        grad_query_normed = self.turn(query_grads, rotate_back).reshape(rows, -1)
        grad_key_normed = self.turn(key_grad, rotate_back).reshape(rows, -1)
        query_dot, key_dot = lax.psum(
            (
                jnp.sum(self.query_raw * self.query_gain * grad_query_normed, axis=-1),
                jnp.sum(self.key_raw * self.key_gain * grad_key_normed, axis=-1),
            ),
            "expert",
        )
        grad_query = low(
            self.query_inv * self.query_gain * grad_query_normed
            - self.query_raw * self.query_inv**3 * (query_dot / (HEADS * HD))[:, None]
        )
        grad_key = low(
            self.key_inv * self.key_gain * grad_key_normed
            - self.key_raw * self.key_inv**3 * (key_dot / (HEADS * HD))[:, None]
        )
        grad_value = low(value_grad.reshape(rows, -1))
        grad_joint = jnp.concatenate([grad_query, grad_key, grad_value], axis=1)
        joint_total = sum_low(contract_rows(self.normed, grad_joint), ("dp", "context"))
        term = contract_last(grad_joint, self.weight)
        grad_normed = lax.psum_scatter(
            low(term), "expert", scatter_dimension=0, tiled=True
        ).astype(jnp.float32)
        gains_total = lax.psum(
            (
                jnp.sum(self.query_raw * self.query_inv * grad_query_normed, axis=0),
                jnp.sum(self.key_raw * self.key_inv * grad_key_normed, axis=0),
            ),
            ("dp", "context"),
        )
        gains = jnp.zeros((2, self.weight.shape[0]), jnp.float32)
        here = lax.axis_index("expert") * self.head_width
        own = jnp.stack(gains_total) / (lax.axis_size("dp") * lax.axis_size("context"))
        gains = lax.dynamic_update_slice(gains, own, (0, here))
        return (grad_normed, sums, gains, *jnp.split(joint_total, 3, axis=1), output_total)


UNIT_TILE = 256
WIDTH_TILE = 512


def expert_forward_kernel(expert_ref, *refs, count, experts_all, unit_tiles):
    blocks = refs[:count]
    pick_ref, router_ref, gate_weight_ref, up_weight_ref, down_weight_ref = refs[
        count : count + 5
    ]
    (
        rows_ref,
        gate_ref,
        up_ref,
        hidden_ref,
        out_ref,
        row_gate_ref,
        kept_ref,
        sent_ref,
        scaled_ref,
        units_ref,
    ) = refs[-10:]
    step = pl.program_id(0)
    capacity = pick_ref.shape[1]

    @pl.when(step == 0)
    def _():
        for i, block_ref in enumerate(blocks):
            here = pl.ds(i * capacity, capacity)
            tokens = block_ref[...]
            pick = pick_ref[i]
            rows_ref[here, :] = low(contract(pick, tokens, 1, 0))
            logits = contract(tokens, router_ref[...], 1, 0)
            lane = lax.broadcasted_iota(jnp.int32, logits.shape, 1)
            logits = jnp.where(lane < experts_all, logits, NEGATIVE)
            weights = jnp.exp(logits - jnp.max(logits, axis=1, keepdims=True))
            chosen = jnp.sum(
                jnp.where(lane == expert_ref[0], weights, 0.0), axis=1, keepdims=True
            )
            gates = as_row(chosen / jnp.sum(weights, axis=1, keepdims=True))
            scaled = pick.astype(jnp.float32) * gates
            scaled_ref[i] = low(scaled)
            row_gates = jnp.sum(scaled, axis=1, keepdims=True)
            row_gate_ref[here, :] = jnp.broadcast_to(row_gates, (capacity, HD))

    @pl.when(step < unit_tiles)
    def _():
        rows = rows_ref[...]
        gate_part = contract(rows, gate_weight_ref[...], 1, 0)
        up_part = contract(rows, up_weight_ref[...], 1, 0)
        hidden = low(silu_parts(gate_part)[0] * up_part)
        gate_ref[...] = low(gate_part)
        up_ref[...] = low(up_part)
        hidden_ref[...] = hidden
        for j in range(unit_tiles):

            @pl.when(step == j)
            def _(j=j):
                units_ref[:, j * UNIT_TILE : (j + 1) * UNIT_TILE] = hidden

    @pl.when(step >= unit_tiles)
    def _():
        out_ref[...] = low(contract(units_ref[...], down_weight_ref[...], 1, 0))
        spread_tokens(scaled_ref, out_ref, kept_ref, sent_ref)


def spread_tokens(pick_ref, rows_ref, kept_ref, sent_ref):
    count, capacity, tok_rows = pick_ref.shape
    half = count // 2
    for i in range(count):
        terms = contract_rows(pick_ref[i], rows_ref[pl.ds(i * capacity, capacity), :])
        if i < half:
            kept_ref[i, :tok_rows, :] = low(terms)
        else:
            sent_ref[i - half, :tok_rows, :] = low(terms)


def spread_scalars(expert, values_ref, kept_ref, sent_ref):
    count, tok_rows = values_ref.shape
    half = count // 2
    for i in range(count):
        out_ref, place = (kept_ref, i) if i < half else (sent_ref, i - half)
        values = values_ref[i : i + 1, :]
        first = low(values).astype(jnp.float32)
        both = jnp.concatenate([first, values - first], axis=1)
        rows, width = (out_ref.shape[1] - tok_rows, out_ref.shape[2])
        out_ref[place, tok_rows:, :] = jnp.zeros((rows, width), jnp.bfloat16)
        row = lax.broadcasted_iota(jnp.int32, (rows, 2 * tok_rows), 0)
        out_ref[place, tok_rows:, : 2 * tok_rows] = low(jnp.where(row == expert, both, 0.0))


def expert_backward_kernel(expert_ref, *refs, count, unit_tiles):
    blocks = refs[:count]
    (
        pick_ref,
        row_gate_ref,
        gate_ref,
        up_ref,
        out_ref,
        down_weight_ref,
        gate_weight_ref,
        up_weight_ref,
    ) = refs[count : count + 8]
    (
        gate_grad_ref,
        grad_out_ref,
        grad_gate_ref,
        grad_up_ref,
        kept_ref,
        sent_ref,
        gates_ref,
        ups_ref,
        rows_ref,
    ) = refs[-9:]
    step = pl.program_id(0)
    capacity = pick_ref.shape[1]

    @pl.when(step == 0)
    def _():
        for i, block_ref in enumerate(blocks):
            here = pl.ds(i * capacity, capacity)
            pick = pick_ref[i]
            grads = contract(pick, block_ref[...], 1, 0)
            dots = jnp.sum(grads * out_ref[here, :].astype(jnp.float32), axis=1, keepdims=True)
            gate_grad_ref[i : i + 1, :] = jnp.sum(
                pick.astype(jnp.float32) * dots, axis=0, keepdims=True
            )
            grad_out_ref[here, :] = low(grads * row_gate_ref[here, 0:1])

    @pl.when(step < unit_tiles)
    def _():
        grad_hidden = contract_last(grad_out_ref[...], down_weight_ref[...])
        silu_value, silu_slope = silu_parts(gate_ref[...].astype(jnp.float32))
        grad_gate = low(grad_hidden * up_ref[...].astype(jnp.float32) * silu_slope)
        grad_up = low(grad_hidden * silu_value)
        grad_gate_ref[...] = grad_gate
        grad_up_ref[...] = grad_up
        for j in range(unit_tiles):

            @pl.when(step == j)
            def _(j=j):
                gates_ref[:, j * UNIT_TILE : (j + 1) * UNIT_TILE] = grad_gate
                ups_ref[:, j * UNIT_TILE : (j + 1) * UNIT_TILE] = grad_up

    @pl.when(step >= unit_tiles)
    def _():
        rows_ref[...] = low(
            contract_last(gates_ref[...], gate_weight_ref[...])
            + contract_last(ups_ref[...], up_weight_ref[...])
        )
        spread_tokens(pick_ref, rows_ref, kept_ref, sent_ref)

        @pl.when(step == unit_tiles)
        def _():
            spread_scalars(expert_ref[0], gate_grad_ref, kept_ref, sent_ref)

        @pl.when(step > unit_tiles)
        def _():
            tok_rows = gate_grad_ref.shape[1]
            for out_ref in (kept_ref, sent_ref):
                rest = out_ref.shape[0], out_ref.shape[1] - tok_rows, out_ref.shape[2]
                out_ref[:, tok_rows:, :] = jnp.zeros(rest, jnp.bfloat16)


def chunk_call(kernel, arrays, in_specs, outs, before, scratch, steps, cost, prefetch=()):
    first = len(prefetch) + len(arrays)
    return pl.pallas_call(
        kernel,
        grid_spec=pltpu.PrefetchScalarGridSpec(
            num_scalar_prefetch=len(prefetch),
            grid=(steps,),
            in_specs=in_specs + [pl.BlockSpec(memory_space=pl.ANY)] * len(before),
            out_specs=[out[2] for out in outs],
            scratch_shapes=scratch,
        ),
        out_shape=[jax.ShapeDtypeStruct(out[0], out[1]) for out in outs],
        input_output_aliases={first + i: j for i, j in enumerate(before)},
        compiler_params=pltpu.CompilerParams(vmem_limit_bytes=VMEM_LIMIT),
        cost_estimate=cost,
    )(*prefetch, *arrays, *before.values())


class Experts:
    def __init__(self, routes, capacity, router_weight, gate_weight, up_weight, down_weight):
        self.capacity = -(-capacity // 16) * 16
        self.experts_all = router_weight.shape[1]
        self.expert = lax.axis_index("context") * lax.axis_size("expert") + lax.axis_index(
            "expert"
        )
        self.router_weight = jnp.pad(router_weight, ((0, 0), (0, HD - self.experts_all)))
        expert_ids = jnp.arange(HD, dtype=jnp.int32)
        self.chosen = low(jnp.any(routes[:, :, None] == expert_ids, axis=1))
        self.own = (gate_weight[0], up_weight[0], down_weight[0])
        self.arriving = [
            ring_gather(half, "dp")[1:] for w in self.own for half in jnp.split(w, 2)
        ]
        self.picks = []

    def here(self, blocks):
        lane = jnp.arange(HD, dtype=jnp.int32) == self.expert
        return jnp.sum(jnp.where(lane, jnp.stack(blocks).astype(jnp.float32), 0.0), axis=-1)

    def pick(self, here):
        member = here > 0
        tok_rows = member.shape[1]
        token = jnp.arange(tok_rows, dtype=jnp.int32)
        before = low(token[:, None] < token[None, :])
        slots = contract(low(member), before, 1, 0).astype(jnp.int32)
        slot_index = jnp.arange(self.capacity, dtype=jnp.int32)
        matches = slots[:, None, :] == slot_index[None, :, None]
        self.picks.append(low(matches & member[:, None, :]))

    def begin(self):
        whole = []
        for i, own in enumerate(self.own):
            halves = zip(*self.arriving[2 * i : 2 * i + 2])
            whole.append([own] + [jnp.concatenate(pair) for pair in halves])
        self.gate_weight, self.up_weight = (jnp.concatenate(w, axis=1) for w in whole[:2])
        self.down_weight = jnp.concatenate(whole[2])
        self.units = self.gate_weight.shape[1]
        self.picks = jnp.stack(self.picks)
        self.chained, self.chained_back = ((), ())
        self.terms, self.terms_back = ({}, {})

    def shapes(self):
        ring, count, capacity, tok_rows = self.picks.shape
        width = self.gate_weight.shape[0]
        return ring, count, count * capacity, tok_rows, width

    def plan(self, s, more=0):
        ring, count, rows, tok_rows, width = self.shapes()
        tiles = self.units // UNIT_TILE
        tile = math.gcd(WIDTH_TILE, width)

        def unit(j):
            return jnp.minimum(j, tiles - 1)

        def column(j):
            return jnp.maximum(j - tiles, 0)

        half = count // 2
        all_rows = ring * rows
        term = (
            (half, tok_rows + more, width),
            jnp.bfloat16,
            pl.BlockSpec((half, tok_rows + more, tile), lambda j, *_: (0, 0, column(j))),
        )
        unit_spec = pl.BlockSpec((rows, UNIT_TILE), lambda j, *_: (s, unit(j)))
        whole_spec = pl.BlockSpec((rows, width), lambda j, *_: (s, 0))
        scalar_spec = pl.BlockSpec((rows, HD), lambda j, *_: (s, 0))
        column_spec = pl.BlockSpec((rows, tile), lambda j, *_: (s, column(j)))
        block_specs = [pl.BlockSpec((tok_rows, width), lambda j, *_: (0, 0))] * count
        pick_spec = pl.BlockSpec((None, *self.picks.shape[1:]), lambda j, *_: (s, 0, 0, 0))
        narrow = ((all_rows, self.units), jnp.bfloat16, unit_spec)
        wide = ((all_rows, width), jnp.bfloat16, whole_spec)
        cost = takes(21.0)
        return (
            unit,
            column,
            tiles,
            tile,
            term,
            unit_spec,
            whole_spec,
            scalar_spec,
            column_spec,
            block_specs,
            pick_spec,
            narrow,
            wide,
            cost,
        )

    def forward_chunk(self, s, blocks):
        ring, count, rows, tok_rows, width = self.shapes()
        (
            unit,
            column,
            tiles,
            tile,
            term,
            unit_spec,
            whole_spec,
            scalar_spec,
            column_spec,
            block_specs,
            pick_spec,
            narrow,
            wide,
            cost,
        ) = self.plan(s)
        results = chunk_call(
            functools.partial(
                expert_forward_kernel,
                count=count,
                experts_all=self.experts_all,
                unit_tiles=tiles,
            ),
            (
                *blocks,
                self.picks,
                self.router_weight,
                self.gate_weight,
                self.up_weight,
                self.down_weight,
            ),
            [
                *block_specs,
                pick_spec,
                fixed_spec(width, HD),
                pl.BlockSpec((width, UNIT_TILE), lambda j, *_: (0, unit(j))),
                pl.BlockSpec((width, UNIT_TILE), lambda j, *_: (0, unit(j))),
                pl.BlockSpec((self.units, tile), lambda j, *_: (0, column(j))),
            ],
            [
                wide,
                narrow,
                narrow,
                narrow,
                (wide[0], wide[1], column_spec),
                ((ring * rows, HD), jnp.float32, scalar_spec),
                term,
                term,
            ],
            dict(enumerate(self.chained)),
            [
                pltpu.VMEM(self.picks.shape[1:], jnp.bfloat16),
                pltpu.VMEM((rows, self.units), jnp.bfloat16),
            ],
            tiles + width // tile,
            cost,
            (self.expert.reshape(1).astype(jnp.int32),),
        )
        self.chained = results[:6]
        self.terms[s] = results[6:]
        return results[7]

    def forward(self, ffn_in):
        last = lax.axis_size("context") - 1
        done, _ = gather_chunks(ffn_in, self.forward_chunk)
        idle = ((), lambda result: result)
        works = [((), lambda result: done[last])] + [idle] * last
        mixture, _ = scatter_chunks(lambda s: self.terms[s], works)
        return mixture

    def backward_chunk(self, s, blocks):
        ring, count, rows, tok_rows, width = self.shapes()
        (
            unit,
            column,
            tiles,
            tile,
            term,
            unit_spec,
            whole_spec,
            scalar_spec,
            column_spec,
            block_specs,
            pick_spec,
            narrow,
            wide,
            cost,
        ) = self.plan(s, -(-self.experts_all // 16) * 16)
        chunk_rows, gate_part, up_part, hidden, out, row_gates = self.chained
        results = chunk_call(
            functools.partial(expert_backward_kernel, count=count, unit_tiles=tiles),
            (
                *blocks,
                self.picks,
                row_gates,
                gate_part,
                up_part,
                out,
                self.down_weight,
                self.gate_weight,
                self.up_weight,
            ),
            [
                *block_specs,
                pick_spec,
                scalar_spec,
                unit_spec,
                unit_spec,
                whole_spec,
                pl.BlockSpec((UNIT_TILE, width), lambda j, *_: (unit(j), 0)),
                pl.BlockSpec((tile, self.units), lambda j, *_: (column(j), 0)),
                pl.BlockSpec((tile, self.units), lambda j, *_: (column(j), 0)),
            ],
            [
                ((count, tok_rows), jnp.float32, fixed_spec(count, tok_rows)),
                wide,
                narrow,
                narrow,
                term,
                term,
            ],
            {j + 1: array for j, array in enumerate(self.chained_back)},
            [
                pltpu.VMEM((rows, self.units), jnp.bfloat16),
                pltpu.VMEM((rows, self.units), jnp.bfloat16),
                pltpu.VMEM((rows, tile), jnp.bfloat16),
            ],
            tiles + width // tile,
            cost,
            (self.expert.reshape(1).astype(jnp.int32),),
        )
        self.chained_back = results[1:4]
        self.terms_back[s] = results[4:]
        return results[0]

    def backward(self, grad_out):
        last = lax.axis_size("context") - 1
        self.gate_done, _ = gather_chunks(low(grad_out), self.backward_chunk)
        grad_rows_out, grad_gate, grad_up = self.chained_back
        chunk_rows, hidden = (self.chained[0], self.chained[3])
        size = lax.axis_size("dp")

        def parts(left, right, axis):
            return jnp.split(contract_rows(left, right), size, axis=axis)

        pending = []

        def product(left, right, axis):
            shares = parts(left, right, axis)
            halves = zip(*(jnp.split(share, 2) for share in shares))
            return [list(half) for half in halves]

        def begin(half):
            pending.append(ring_sum_begin(half, "dp"))
            return pending[-1][1]

        def second(_, *arrays):
            self.gates_grad = product(*arrays, 1)
            return self.gates_grad[0][0], ()

        def third(_, *arrays):
            self.ups_grad = product(*arrays, 1)
            return self.ups_grad[0][0], begin(self.gates_grad[0])

        def fourth(_, *arrays):
            self.downs_grad = product(*arrays, 0)
            return self.downs_grad[0][0], begin(self.gates_grad[1])

        works = [((), lambda result: result)] * (last + 1)
        works[0] = ((), lambda _: self.gate_done[last])
        works[1] = ((chunk_rows, grad_gate), second)
        works[2] = ((chunk_rows, grad_up), third)
        works[-1] = ((hidden, grad_rows_out), fourth)
        total, done = scatter_chunks(lambda s: self.terms_back[s], works)
        total, done = together(total, done)
        tok_rows = self.picks.shape[3]
        grad_ffn, rest = (total[:tok_rows], total[tok_rows:])
        grad_gates = (rest[:, :tok_rows] + rest[:, tok_rows : 2 * tok_rows])[: self.experts_all].T
        for half in (*self.ups_grad, *self.downs_grad):
            begin(half)
        return grad_ffn, grad_gates, pending


def per_device(
    block_input,
    teacher_states,
    seq_lengths,
    expert_routes,
    attn_gain,
    query_weight,
    key_weight,
    value_weight,
    query_gain,
    key_gain,
    output_weight,
    ffn_gain,
    router_weight,
    gate_weight,
    up_weight,
    down_weight,
):
    tok_rows = block_input.shape[0]
    experts_all = router_weight.shape[1]
    capacity = 5 * tok_rows * TOPK // (4 * experts_all)
    context_size = lax.axis_size("context")
    expert_size = lax.axis_size("expert")
    token_count_all = tok_rows * lax.axis_size("dp") * context_size * expert_size
    length = seq_lengths[0]
    own_start = (
        lax.axis_index("context") * expert_size + lax.axis_index("expert")
    ) * tok_rows
    tokens = block_input.astype(jnp.float32)
    inverse_one = rms_scale(tokens)
    normed = low(tokens * inverse_one * attn_gain)
    heads_here = query_weight.shape[1] // HD
    count_total = small_sum(jnp.full((8, 128), length, jnp.int32), ("dp",))
    experts = Experts(
        expert_routes, capacity, router_weight, gate_weight, up_weight, down_weight
    )
    attention_kind = HeadAttention if heads_here == context_size else BlockAttention
    attention = attention_kind(
        normed,
        length,
        (query_weight, key_weight, value_weight),
        (query_gain, key_gain),
        output_weight,
        experts,
        count_total,
    )
    experts.begin()
    count_total = attention.count_total[0, 0].astype(jnp.float32)
    residual = tokens + attention.output()
    inverse_two = rms_scale(residual)
    ffn_in = low(residual * inverse_two * ffn_gain)
    logits = jnp.dot(ffn_in, router_weight, preferred_element_type=jnp.float32)
    weights_router = jnp.exp(logits - jnp.max(logits, axis=-1, keepdims=True))
    router_probs = weights_router / jnp.sum(weights_router, axis=-1, keepdims=True)
    expert_ids = jnp.arange(experts_all, dtype=jnp.int32)
    chosen = jnp.any(expert_routes[:, :, None] == expert_ids, axis=1)
    mixture = experts.forward(ffn_in)
    output_full = residual + mixture
    own_pos = own_start + jnp.arange(tok_rows, dtype=jnp.int32)
    valid = (own_pos < length).astype(jnp.float32)
    difference = output_full - teacher_states
    local_loss = jnp.sum(jnp.sum(difference * difference, axis=-1) * valid)
    grad_out = difference * (valid * (token_count_all / count_total))[:, None]
    grad_ffn_experts, grad_gates, pending = experts.backward(grad_out)
    grad_router_probs = jnp.where(chosen, grad_gates, 0.0)
    grad_logits = router_probs * (
        grad_router_probs - jnp.sum(router_probs * grad_router_probs, axis=-1, keepdims=True)
    )
    router_grad = lax.dot_general(
        grad_logits,
        ffn_in.astype(jnp.float32),
        (((0,), (0,)), ((), ())),
        precision=lax.Precision.HIGHEST,
    )
    grad_ffn = grad_ffn_experts + lax.dot_general(
        grad_logits,
        router_weight.astype(jnp.float32),
        (((1,), (1,)), ((), ())),
        precision=lax.Precision.HIGHEST,
    )
    ffn_gain_grad = jnp.sum(residual * inverse_two * grad_ffn, axis=0)
    weighted_two = grad_ffn * ffn_gain
    grad_residual = (
        grad_out
        + inverse_two * weighted_two
        - residual * inverse_two**3 * jnp.mean(residual * weighted_two, axis=-1, keepdims=True)
    )
    sums = jnp.concatenate(
        [
            router_grad,
            ffn_gain_grad[None],
            jnp.broadcast_to(local_loss, ffn_gain_grad.shape)[None],
        ]
    )
    grad_normed, sums, gains, query_total, key_total, value_total, output_total = (
        attention.backward(low(grad_residual), sums, pending)
    )
    attn_gain_grad = jnp.sum(tokens * inverse_one * grad_normed, axis=0)
    gains = small_sum(jnp.concatenate([attn_gain_grad[None], gains]), ("dp", *TOKEN_AXES))
    head_width = query_gain.shape[0]
    query_gain_total, key_gain_total = lax.dynamic_slice_in_dim(
        gains[1:], lax.axis_index("expert") * head_width, head_width, 1
    )
    weighted_one = grad_normed * attn_gain
    input_grad = (
        grad_residual
        + inverse_one * weighted_one
        - tokens * inverse_one**3 * jnp.mean(tokens * weighted_one, axis=-1, keepdims=True)
    )
    router_total, ffn_total = (sums[:experts_all].T, sums[experts_all])
    loss_total = sums[experts_all + 1, 0]
    return (
        low(output_full),
        loss_total / count_total,
        input_grad,
        gains[0],
        query_total,
        key_total,
        value_total,
        query_gain_total,
        key_gain_total,
        output_total,
        ffn_total,
        router_total,
        *attention.finished,
    )


def solution(mesh):
    rows = P(ALL_AXES, None)
    placed = (
        rows,
        rows,
        P("dp"),
        rows,
        P(),
        P(None, "expert"),
        P(None, "expert"),
        P(None, "expert"),
        P("expert"),
        P("expert"),
        P("expert", None),
        P(),
        P(),
        P(TOKEN_AXES, None, "dp"),
        P(TOKEN_AXES, None, "dp"),
        P(TOKEN_AXES, "dp", None),
    )
    return jax.shard_map(
        per_device,
        mesh=mesh,
        in_specs=placed,
        out_specs=(
            rows,
            P(),
            rows,
            P(),
            P(None, "expert"),
            P(None, "expert"),
            P(None, "expert"),
            P("expert"),
            P("expert"),
            P("expert", None),
            P(),
            P(),
            P(TOKEN_AXES, None, "dp"),
            P(TOKEN_AXES, None, "dp"),
            P(TOKEN_AXES, "dp", None),
        ),
        check_vma=False,
    )
```

```python
import functools
import math

import jax
import jax.numpy as jnp
from jax import lax
from jax.experimental import pallas as pl
from jax.experimental.pallas import tpu as pltpu
from jax.sharding import PartitionSpec as P

HEADS = 16
HD = 128
TOPK = 8


EPSILON = 1e-05
ROPE_BASE = 10000.0
NEGATIVE = -1e30
LOG2E = math.log2(math.e)
SCORE_SCALE = HD ** (-0.5)
TOKEN_AXES = ("context", "expert")
ALL_AXES = ("dp", "context", "expert")
VMEM_LIMIT = 56 * 2**20


def takes(microseconds):
    return pl.CostEstimate(
        flops=int(microseconds * 1.1e9), bytes_accessed=int(microseconds * 3e6), transcendentals=0
    )


def rms_scale(values):
    return lax.rsqrt(jnp.mean(values * values, axis=-1, keepdims=True) + EPSILON)


def rope_tables(positions):
    exponent = jnp.arange(HD // 2, dtype=jnp.float32) * (2.0 / HD)
    angles = positions.astype(jnp.float32)[:, None] * (ROPE_BASE ** (-exponent))[None, :]
    return (jnp.cos(angles), jnp.sin(angles))


def rotate(values, cosine, sine_part):
    halfway = values.shape[-1] // 2
    leading = values[..., :halfway]
    trailing = values[..., halfway:]
    cos_wide = cosine[:, None, :]
    sin_wide = sine_part[:, None, :]
    return jnp.concatenate(
        [leading * cos_wide - trailing * sin_wide, trailing * cos_wide + leading * sin_wide],
        axis=-1,
    )


def rotate_back(gradient, cosine, sine_part):
    return rotate(gradient, cosine, -sine_part)


def silu_parts(gate_part):
    sigmoid = jax.nn.sigmoid(gate_part)
    return (gate_part * sigmoid, sigmoid * (1.0 + gate_part * (1.0 - sigmoid)))


def contract(left, right, left_dim, right_dim):
    return lax.dot_general(
        left,
        right,
        (((left_dim,), (right_dim,)), ((), ())),
        preferred_element_type=jnp.float32,
    )


def contract_rows(left, right):
    return contract(left, right, 0, 0)


def contract_last(left, right):
    return contract(left, right, 1, 1)


def low(values):
    return values.astype(jnp.bfloat16)


def steps_back(axis, size, stride=1):
    group = size * stride
    total = lax.axis_size(axis)
    return tuple(
        (i, i // group * group + (i + stride) % group) for i in range(total)
    )


def moved(values, axis, pairs):
    return jax.tree.map(lambda v: lax.ppermute(v, axis, pairs), values)


def next_on(axis, values):
    return moved(values, axis, steps_back(axis, lax.axis_size(axis)))


def next_chip(values):
    return moved(values, "expert", steps_back("expert", chips_of_expert(), 2))


def partner(values):
    pairs = tuple((i, i ^ 1) for i in range(lax.axis_size("expert")))
    return moved(values, "expert", pairs)


def chips_of_expert():
    return lax.axis_size("expert") // 2


def together(*values):
    return lax.optimization_barrier(values)


def place_of(z, e):
    return z, e // 2, e % 2


def relative_to_absolute():
    ring, chips = (lax.axis_size("context"), chips_of_expert())
    z, x, c = place_of(lax.axis_index("context"), lax.axis_index("expert"))
    r = jnp.arange(ring * chips * 2, dtype=jnp.int32)
    s, dc, dx = (r // (2 * chips), r // chips % 2, r % chips)
    return ((z + ring - s) % ring * chips + (x + chips - dx) % chips) * 2 + (c + dc) % 2


def absolute_to_relative():
    ring, chips = (lax.axis_size("context"), chips_of_expert())
    z, x, c = place_of(lax.axis_index("context"), lax.axis_index("expert"))
    b = jnp.arange(ring * chips * 2, dtype=jnp.int32)
    bz, bx, bc = (b // (2 * chips), b // 2 % chips, b % 2)
    return ((z + ring - bz) % ring * 2 + (c + bc) % 2) * chips + (x + chips - bx) % chips


def reorder(blocks, order):
    count = blocks.shape[0]
    onehot = (order[:, None] == jnp.arange(count, dtype=jnp.int32)[None, :]).astype(jnp.float32)
    moved = lax.dot_general(
        onehot,
        blocks.reshape(count, -1),
        (((1,), (0,)), ((), ())),
        precision=lax.Precision.HIGHEST,
    )
    return moved.reshape(blocks.shape)


def after_exchange(values, token):
    return together(values, partner(token[:16, :HD]))[0]


def gather_expert(rows):
    parts = [rows]
    for _ in range(chips_of_expert() - 1):
        parts.append(next_chip(parts[-1]))
    return parts + [partner(p) for p in parts]


def gather_chunks(rows, work, beside=(), slack=0):
    ring = lax.axis_size("context")
    results, done = ([], [])
    for s in range(ring):
        following = next_on("context", rows) if s < ring - 1 else rows
        parts = [rows]
        for _ in range(chips_of_expert() - 1):
            parts.append(next_chip(parts[-1]))
        extra = beside[s] if s < len(beside) else ()
        due = s - 1 - slack
        result = results[due] if due >= 0 else None
        following, parts[-1], result, extra = together(following, parts[-1], result, extra)
        if due >= 0:
            results[due] = result
        done.append(extra)
        results.append(work(s, parts + [partner(p) for p in parts]))
        rows = following
    return results, done


def core_sum(kept, sent):
    return kept.astype(jnp.float32) + partner(low(sent)).astype(jnp.float32)


def scatter_chips(terms, waiting=None, beside=()):
    running = low(terms[1])
    running, waiting, beside = together(running, waiting, beside)
    if waiting is not None:
        waiting = next_on("context", waiting)
    for d in range(2, terms.shape[0]):
        running = low(terms[d] + next_chip(running).astype(jnp.float32))
    total = terms[0] + next_chip(running).astype(jnp.float32)
    rest = None
    if waiting is not None:
        count = total.shape[0]
        total = total + waiting[:count].astype(jnp.float32)
        rest = waiting[count:]
    return total, rest, beside


def scatter_chunks(term, works, rider=None):
    ring = lax.axis_size("context")
    order = (*range(1, ring), 0)
    total, result = (None, ())
    terms = core_sum(*term(order[0]))
    for i in range(ring):
        arrays, work = works[i]
        ahead = core_sum(*term(order[i + 1])) if i + 1 < ring else None
        waiting = None if total is None else low(total)
        if i:
            if rider is not None:
                waiting = jnp.concatenate([waiting, rider(result)])
            total, rest, (result, arrays, ahead) = scatter_chips(
                terms, waiting, (result, arrays, ahead)
            )
            if rider is not None:
                arrays = (rest, *arrays)
        else:
            total, _, (result, arrays) = scatter_chips(terms, waiting, (result, arrays))
        terms = ahead
        result = work(result, *arrays)
    return total, result


def ring_sum_begin(parts, axis):
    running = parts[1]
    for part in parts[2:]:
        running = part + next_on(axis, low(running)).astype(jnp.float32)
    return parts[0], next_on(axis, low(running))


def ring_sum(parts, axis):
    kept, received = ring_sum_begin(parts, axis)
    return kept + received.astype(jnp.float32)


def ring_parts(values, axis, dim):
    size, me = (lax.axis_size(axis), lax.axis_index(axis))
    share = values.shape[dim] // size
    return [
        lax.dynamic_slice_in_dim(values, ((me - d) % size) * share, share, dim)
        for d in range(size)
    ]


def ring_gather(values, axis):
    parts = [values]
    for _ in range(lax.axis_size(axis) - 1):
        parts.append(next_on(axis, parts[-1]))
    return parts


def small_sum(values, axes):
    for axis in axes:
        size = lax.axis_size(axis)
        parts = [values] + [
            lax.ppermute(values, axis, tuple((i, i ^ bits) for i in range(size)))
            for bits in range(1, size)
        ]
        while len(parts) > 1:
            parts = [left + right for left, right in zip(parts[::2], parts[1::2])]
        values = parts[0]
    return values


def gather_block(rows):
    return lax.all_gather(rows, "expert", axis=0, tiled=True)


def sum_low(values, axes):
    return lax.psum(low(values), axes).astype(jnp.float32)


def as_row(column):
    return jnp.broadcast_to(column, (column.shape[0], HD)).T[0:1, :]


def project_kernel(places_ref, *refs, count):
    blocks, weight_ref = (refs[:count], refs[count])
    raw_ref, copy_ref, square_ref, member_ref = refs[-4:]
    width = weight_ref.shape[0]
    for i, block_ref in enumerate(blocks):

        @pl.when(pl.program_id(0) == i)
        def _(block_ref=block_ref):
            rows = block_ref[:, :width]
            raw = contract(rows, weight_ref[...], 1, 0)
            raw_ref[...] = raw
            copy_ref[...] = rows
            for j in range(2):
                part = raw[:, j * HD : (j + 1) * HD]
                square_ref[j : j + 1, :] = as_row(jnp.sum(part * part, axis=1, keepdims=True))
            chosen = block_ref[:, width:].astype(jnp.float32)
            lane = lax.broadcasted_iota(jnp.int32, chosen.shape, 1)
            here = lane == places_ref[count]
            member = jnp.sum(jnp.where(here, chosen, 0.0), axis=1, keepdims=True)
            member_ref[0] = as_row(member)


def project_chunk(blocks, weight, places, before, total_rows):
    count = len(blocks)
    tok_rows = blocks[0].shape[0]
    width, columns = weight.shape
    whole = fixed_spec(*blocks[0].shape)
    outs = [
        (
            (total_rows, columns),
            jnp.float32,
            pl.BlockSpec((tok_rows, columns), lambda i, places: (places[i], 0)),
        ),
        (
            (total_rows, width),
            jnp.bfloat16,
            pl.BlockSpec((tok_rows, width), lambda i, places: (places[i], 0)),
        ),
        (
            (2, total_rows),
            jnp.float32,
            pl.BlockSpec((2, tok_rows), lambda i, places: (0, places[i])),
        ),
        (
            (count, 1, tok_rows),
            jnp.float32,
            pl.BlockSpec((1, 1, tok_rows), lambda i, places: (i, 0, 0)),
        ),
    ]
    return chunk_call(
        functools.partial(project_kernel, count=count),
        (*blocks, weight),
        [whole] * count + [fixed_spec(width, columns)],
        outs,
        dict(enumerate(before)),
        [],
        count,
        takes(8.5),
        (places,),
    )


def inverse_norms(totals):
    return lax.rsqrt(totals * (1.0 / (HEADS * HD)) + EPSILON).T


def turn_kernel(raw_ref, total_ref, gain_ref, cos_ref, sin_ref, q_ref, k_ref, v_ref):
    inverse = inverse_norms(total_ref[...])
    cosine, sine_part = (cos_ref[...], sin_ref[...])
    for i, (out_ref, factor) in enumerate(((q_ref, SCORE_SCALE * LOG2E), (k_ref, 1.0))):
        values = raw_ref[:, i * HD : (i + 1) * HD] * inverse[:, i : i + 1] * gain_ref[i : i + 1, :]
        turned = values * cosine + pltpu.roll(values, HD // 2, 1) * sine_part
        out_ref[...] = low(turned * factor)
    v_ref[...] = low(raw_ref[:, 2 * HD :])


def turned_back(grad, cosine, sine_part):
    return grad * cosine - pltpu.roll(grad, HD // 2, 1) * sine_part


def turn_grad_kernel(
    raw_ref, total_ref, gain_ref, cos_ref, sin_ref, dq_ref, dk_ref, dots_ref, gains_ref
):
    @pl.when(pl.program_id(0) == 0)
    def _():
        gains_ref[...] = jnp.zeros_like(gains_ref)

    inverse = inverse_norms(total_ref[...])
    for i, grad_ref in enumerate((dq_ref, dk_ref)):
        back = turned_back(grad_ref[...], cos_ref[...], sin_ref[...])
        scaled = raw_ref[:, i * HD : (i + 1) * HD] * back
        dots = jnp.sum(scaled * gain_ref[i : i + 1, :], axis=1, keepdims=True)
        dots_ref[i : i + 1, :] = as_row(dots)
        gains_ref[i : i + 1, :] += jnp.sum(scaled * inverse[:, i : i + 1], axis=0, keepdims=True)


def norm_grad_kernel(
    places_ref,
    raw_ref,
    total_ref,
    gain_ref,
    cos_ref,
    sin_ref,
    dq_ref,
    dk_ref,
    dv_ref,
    dots_ref,
    out_ref,
    relative_ref,
    *,
    share,
):
    inverse = inverse_norms(total_ref[...])
    dots = dots_ref[...].T
    for i, grad_ref in enumerate((dq_ref, dk_ref)):
        back = turned_back(grad_ref[...], cos_ref[...], sin_ref[...])
        raw = raw_ref[:, i * HD : (i + 1) * HD]
        inv = inverse[:, i : i + 1]
        shared = inv * inv * inv * dots[:, i : i + 1] * (1.0 / (HEADS * HD))
        out_ref[:, i * HD : (i + 1) * HD] = low(
            back * gain_ref[i : i + 1, :] * inv - raw * shared
        )
    out_ref[:, 2 * HD :] = low(dv_ref[...])
    spread_relative(places_ref, out_ref, relative_ref, share)


def spread_relative(places_ref, from_ref, to_ref, share):
    ring = places_ref.shape[0] - share
    rows = from_ref.shape[0] // share
    for b in range(share):
        place = pl.multiple_of(places_ref[ring + b] * rows, rows)
        to_ref[pl.ds(place, rows), :] = from_ref[b * rows : (b + 1) * rows, :]


def context_grad_kernel(places_ref, grad_ref, context_ref, out_ref, delta_ref, *, share):
    ring = places_ref.shape[0] - share
    rows = out_ref.shape[0] // share
    for b in range(share):
        place = pl.multiple_of(places_ref[ring + b] * rows, rows)
        here = pl.ds(b * rows, rows)
        grads = grad_ref[pl.ds(place, rows), :]
        out_ref[here, :] = grads
        product = grads.astype(jnp.float32) * context_ref[here, :].astype(jnp.float32)
        delta_ref[0:1, here] = as_row(jnp.sum(product, axis=1, keepdims=True))


def sequence_places():
    ring, chips = (lax.axis_size("context"), chips_of_expert())
    z, x, c = place_of(lax.axis_index("context"), lax.axis_index("expert"))
    distances = (z + ring - jnp.arange(ring, dtype=jnp.int32)) % ring
    b = jnp.arange(2 * chips, dtype=jnp.int32)
    places = (c + b % 2) % 2 * chips + (x + chips - b // 2) % chips
    return jnp.concatenate([distances, places])


def block_call(kernel, arrays, in_specs, out_specs, out_shape, count, time, places=None):
    prefetch = [] if places is None else [places]
    return pl.pallas_call(
        kernel,
        grid_spec=pltpu.PrefetchScalarGridSpec(
            num_scalar_prefetch=len(prefetch),
            grid=(count,),
            in_specs=in_specs,
            out_specs=out_specs,
        ),
        out_shape=out_shape,
        compiler_params=pltpu.CompilerParams(vmem_limit_bytes=VMEM_LIMIT),
        cost_estimate=takes(time),
    )(*prefetch, *arrays)


def rows_spec(rows, width):
    return pl.BlockSpec((rows, width), lambda b, *_: (b, 0))


def distance_spec(rows, width):
    return pl.BlockSpec((rows, width), lambda b, places: (places[b], 0))


def scalars_spec(rows, count=8):
    return pl.BlockSpec((count, rows), lambda b, *_: (0, b))


def fixed_spec(*shape):
    return pl.BlockSpec(shape, lambda *_: (0,) * len(shape))


def flash_forward_kernel(
    length_ref, places_ref, q_ref, k_ref, v_ref, out_ref, log_ref, relative_ref, *, block, share
):
    row_block = pl.program_id(0)
    length = length_ref[0]
    queries = q_ref[...]

    def step(j, carry, masked):
        highest, total, acc = carry
        rows = pl.ds(pl.multiple_of(j * block, block), block)
        scores = contract_last(queries, k_ref[rows, :])
        if masked:
            query_pos = row_block * block + lax.broadcasted_iota(jnp.int32, (block, block), 0)
            key_pos = j * block + lax.broadcasted_iota(jnp.int32, (block, block), 1)
            allowed = (key_pos <= query_pos) & (key_pos < length)
            scores = jnp.where(allowed, scores, NEGATIVE)
        higher = jnp.maximum(highest, jnp.max(scores, axis=1, keepdims=True))
        weights = jnp.exp2(scores - higher)
        decay = jnp.exp2(highest - higher)
        total = total * decay + jnp.sum(weights, axis=1, keepdims=True)
        acc = acc * decay + contract(low(weights), v_ref[rows, :], 1, 0)
        return higher, total, acc

    start = (
        jnp.full((block, 1), NEGATIVE, jnp.float32),
        jnp.zeros((block, 1), jnp.float32),
        jnp.zeros((block, HD), jnp.float32),
    )
    full = jnp.minimum(row_block, length // block)
    end = jnp.minimum(row_block + 1, (length + block - 1) // block)
    carry = lax.fori_loop(0, full, lambda j, c: step(j, c, False), start)
    highest, total, acc = lax.fori_loop(full, end, lambda j, c: step(j, c, True), carry)
    out_ref[...] = low(acc / total)
    log_ref[...] = jnp.broadcast_to(highest + jnp.log2(total), (block, HD)).T[:8, :]
    spread_relative(places_ref, out_ref, relative_ref, share)


def flash_forward(queries, keys, values, length, places, block, share):
    rows = queries.shape[0]
    whole = pl.BlockSpec((rows, HD), lambda i, *_: (0, 0))
    part = pl.BlockSpec((block, HD), lambda i, *_: (i, 0))
    return pl.pallas_call(
        functools.partial(flash_forward_kernel, block=block, share=share),
        grid_spec=pltpu.PrefetchScalarGridSpec(
            num_scalar_prefetch=2,
            grid=(rows // block,),
            in_specs=[part, whole, whole],
            out_specs=[
                part,
                pl.BlockSpec((8, block), lambda i, *_: (0, i)),
                pl.BlockSpec((block, HD), lambda i, _, places: (places[i], 0)),
            ],
        ),
        out_shape=[
            jax.ShapeDtypeStruct((rows, HD), jnp.bfloat16),
            jax.ShapeDtypeStruct((8, rows), jnp.float32),
            jax.ShapeDtypeStruct((rows, HD), jnp.bfloat16),
        ],
        compiler_params=pltpu.CompilerParams(vmem_limit_bytes=VMEM_LIMIT),
        cost_estimate=takes(20.0),
    )(length, places, queries, keys, values)


def flash_backward_kernel(
    length_ref, q_ref, do_ref, log_ref, delta_ref, k_ref, v_ref, dq_ref, dk_ref, dv_ref, *, block
):
    key_block = pl.program_id(0)
    count = q_ref.shape[0] // block
    length = length_ref[0]

    @pl.when(key_block == 0)
    def _():
        dq_ref[...] = jnp.zeros_like(dq_ref)

    keys = k_ref[...]
    values = v_ref[...]

    def step(i, carry, masked):
        key_acc, value_acc = carry
        rows = pl.ds(pl.multiple_of(i * block, block), block)
        queries = q_ref[rows, :]
        grads = do_ref[rows, :]
        weights = jnp.exp2(contract_last(keys, queries) - log_ref[0:1, rows])
        if masked:
            query_pos = i * block + lax.broadcasted_iota(jnp.int32, (block, block), 1)
            key_pos = key_block * block + lax.broadcasted_iota(jnp.int32, (block, block), 0)
            allowed = (key_pos <= query_pos) & (key_pos < length)
            weights = jnp.where(allowed, weights, 0.0)
        grad_weights = contract_last(values, grads)
        grad_scores = low(weights * (grad_weights - delta_ref[0:1, rows]))
        value_acc = value_acc + contract(low(weights), grads, 1, 0)
        key_acc = key_acc + contract(grad_scores, queries, 1, 0)
        dq_ref[rows, :] += contract_rows(grad_scores, keys)
        return key_acc, value_acc

    zeros = jnp.zeros((block, HD), jnp.float32)
    beyond = key_block * block >= length
    ragged = (key_block + 1) * block > length
    start = jnp.where(beyond, count, key_block)
    masked_end = jnp.where(ragged, count, key_block + 1)
    carry = lax.fori_loop(start, masked_end, lambda i, c: step(i, c, True), (zeros, zeros))
    key_acc, value_acc = lax.fori_loop(
        masked_end, count, lambda i, c: step(i, c, False), carry
    )
    dk_ref[...] = key_acc * (1.0 / LOG2E)
    dv_ref[...] = value_acc

    @pl.when(key_block == count - 1)
    def _():
        dq_ref[...] = dq_ref[...] * SCORE_SCALE


def flash_backward(queries, keys, values, grads, logs, delta, length, block):
    rows = queries.shape[0]
    whole = pl.BlockSpec((rows, HD), lambda j, _: (0, 0))
    part = pl.BlockSpec((block, HD), lambda j, _: (j, 0))
    return pl.pallas_call(
        functools.partial(flash_backward_kernel, block=block),
        grid_spec=pltpu.PrefetchScalarGridSpec(
            num_scalar_prefetch=1,
            grid=(rows // block,),
            in_specs=[
                whole,
                whole,
                pl.BlockSpec((8, rows), lambda j, _: (0, 0)),
                pl.BlockSpec((8, rows), lambda j, _: (0, 0)),
                part,
                part,
            ],
            out_specs=[whole, part, part],
        ),
        out_shape=[jax.ShapeDtypeStruct((rows, HD), jnp.float32)] * 3,
        compiler_params=pltpu.CompilerParams(vmem_limit_bytes=VMEM_LIMIT),
        cost_estimate=takes(30.0),
    )(length, queries, grads, logs, delta, keys, values)


def finish(kept, received):
    halves = [part + other.astype(jnp.float32) for part, other in zip(kept, received)]
    return [jnp.concatenate(halves[i : i + 2])[None] for i in (0, 2, 4)]


def place_kernel(order_ref, in_ref, out_ref):
    out_ref[...] = in_ref[...].astype(out_ref.dtype)


def place(blocks, order, dtype):
    count, rows, width = blocks.shape
    return pl.pallas_call(
        place_kernel,
        grid_spec=pltpu.PrefetchScalarGridSpec(
            num_scalar_prefetch=1,
            grid=(count,),
            in_specs=[pl.BlockSpec((1, rows, width), lambda b, order: (order[b], 0, 0))],
            out_specs=pl.BlockSpec((1, rows, width), lambda b, order: (b, 0, 0)),
        ),
        out_shape=jax.ShapeDtypeStruct(blocks.shape, dtype),
        compiler_params=pltpu.CompilerParams(vmem_limit_bytes=VMEM_LIMIT),
        cost_estimate=takes(4.0),
    )(order, blocks)


class OutputTotal:
    def __init__(self, ring, grad):
        self.ring, self.width = (ring, grad.shape[1])
        self.state = ring_parts(grad.reshape(ring, HD, self.width), "dp", 1)

    def over_dp(self):
        self.state = list(ring_sum_begin(self.state, "dp"))
        self.taken = 0

    def step(self):
        ring = self.ring
        if not self.taken:
            kept, received = self.state
            total = kept + received.astype(jnp.float32)
            self.state = [total[(ring - d) % ring] for d in range(ring)]
            arrived = 0.0
        else:
            *self.state, arrived = self.state
            arrived = arrived.astype(jnp.float32)
        self.taken += 1
        self.state = [*self.state, next_on("context", low(self.state[self.taken] + arrived))]

    def finish(self):
        for _ in range(self.taken, self.ring - 1):
            self.step()
        *parts, arrived = self.state
        self.state = [low(parts[0] + arrived.astype(jnp.float32))]

    def collect(self):
        self.state = [*self.state, next_on("context", self.state[-1])]

    def exchange(self):
        here = jnp.stack(self.state)
        self.state = [here, *ring_gather(here, "dp")[1:]]

    def total(self):
        ring, size = (self.ring, lax.axis_size("dp"))
        z, y = (lax.axis_index("context"), lax.axis_index("dp"))
        order = jnp.stack(
            [((y - j) % size) * ring + (z - i) % ring for i in range(ring) for j in range(size)]
        ).astype(jnp.int32)
        placed = place(jnp.concatenate(self.state), order, jnp.float32)
        return placed.reshape(ring * HD, self.width)


def context_terms_kernel(*refs, count):
    blocks, weight_ref, outs = (refs[:count], refs[count], refs[count + 1 :])
    for i, block_ref in enumerate(blocks):

        @pl.when(pl.program_id(0) == i)
        def _(block_ref=block_ref):
            terms = low(contract_last(block_ref[...], weight_ref[...]))
            for d, out_ref in enumerate(outs):
                out_ref[...] = terms[:, d * HD : (d + 1) * HD]


def context_terms(blocks, weight, ring):
    count = len(blocks)
    tok_rows, width = blocks[0].shape
    return pl.pallas_call(
        functools.partial(context_terms_kernel, count=count),
        grid=(count,),
        in_specs=[fixed_spec(tok_rows, width)] * count + [fixed_spec(*weight.shape)],
        out_specs=[rows_spec(tok_rows, HD)] * ring,
        out_shape=[jax.ShapeDtypeStruct((count * tok_rows, HD), jnp.bfloat16)] * ring,
        compiler_params=pltpu.CompilerParams(vmem_limit_bytes=VMEM_LIMIT),
        cost_estimate=takes(6.0),
    )(*blocks, weight)


def permute_by(axis, values, distance):
    size = lax.axis_size(axis)
    return lax.ppermute(values, axis, tuple((i, (i + distance) % size) for i in range(size)))


class HeadAttention:
    def __init__(self, normed, length, weights, gains, output_weight, experts, count):
        self.ring = ring = lax.axis_size("context")
        self.share = share = 2 * chips_of_expert()
        self.tok_rows = tok_rows = normed.shape[0]
        self.block = block = share * tok_rows
        self.rows = rows = ring * block
        self.length = length.reshape(1)
        head = lax.axis_index("context")

        def mine(array):
            return lax.dynamic_slice_in_dim(array, head * HD, HD, array.ndim - 1)

        self.weight = jnp.concatenate([mine(w) for w in weights], axis=1)
        self.gains = jnp.pad(jnp.stack([mine(g) for g in gains]), ((0, 6), (0, 0)))
        self.output_weight = jnp.concatenate(
            [
                lax.dynamic_slice_in_dim(output_weight, (head + d) % ring * HD, HD, 0)
                for d in range(ring)
            ]
        )
        self.places = sequence_places()
        absolute = relative_to_absolute()
        cosine, sine_part = rope_tables(jnp.arange(rows, dtype=jnp.int32))
        tables = (
            jnp.concatenate([cosine, cosine], axis=1),
            jnp.concatenate([-sine_part, sine_part], axis=1),
        )
        made = [()]

        def project(s, blocks):
            places = absolute[s * share : (s + 1) * share]
            places = jnp.concatenate([places, experts.expert.reshape(1).astype(jnp.int32)])
            results = project_chunk(blocks, self.weight, places, made[0], rows)
            made[0] = results[:3]
            experts.pick(results[3][:, 0, :])
            return results[3]

        arriving = experts.arriving
        _, done = gather_chunks(
            jnp.concatenate([normed, experts.chosen], axis=1),
            project,
            [arriving[0], (tables, arriving[1]), arriving[2], (arriving[3], count)],
            1,
        )
        tables, second = done[1]
        fourth, self.count_total = done[3]
        self.raw, self.normed, squares = made[0]
        totals = small_sum(squares, TOKEN_AXES)
        self.common = (self.raw, totals, self.gains, *tables)
        self.common_specs = [
            rows_spec(block, 3 * HD),
            scalars_spec(block, 2),
            fixed_spec(8, HD),
            rows_spec(block, HD),
            rows_spec(block, HD),
        ]
        self.queries, self.keys, self.values = block_call(
            turn_kernel,
            self.common,
            self.common_specs,
            [rows_spec(block, HD)] * 3,
            [jax.ShapeDtypeStruct((rows, HD), jnp.bfloat16)] * 3,
            ring,
            7.5,
        )
        self.queries, fifth = together(self.queries, arriving[4])
        self.context, self.logs, pieces = flash_forward(
            self.queries, self.keys, self.values, self.length, self.places, block, share
        )
        pieces, sixth = together(pieces, arriving[5])
        experts.arriving = [done[0], second, done[2], fourth, fifth, sixth]
        pieces = jnp.split(pieces, ring)
        self.context_block = jnp.concatenate(
            [pieces[0]] + [permute_by("context", pieces[d], -d) for d in range(1, ring)], axis=1
        )

    def output(self):
        shape = (self.share // 2, self.tok_rows, self.output_weight.shape[1])
        half = self.block // 2
        kept, sent = (
            contract(part, self.output_weight, 1, 0).reshape(shape)
            for part in (self.context_block[:half], self.context_block[half:])
        )
        return scatter_chips(core_sum(kept, sent))[0]

    def backward(self, grad_attn, sums, pending):
        tok_rows, ring, block, rows = (self.tok_rows, self.ring, self.block, self.rows)
        kept, received = (list(part) for part in zip(*pending))
        block_grad = gather_expert(grad_attn)
        sums, block_grad[-1], received[2] = together(
            small_sum(sums, ("context",)), block_grad[-1], received[2]
        )
        pieces = context_terms(block_grad, self.output_weight, ring)
        sums, pieces = together(sums, pieces)
        sums = small_sum(sums, ("expert",))
        output_grad = contract_rows(self.context_block, jnp.concatenate(block_grad))
        output_sum = OutputTotal(ring, output_grad)
        pieces = jnp.concatenate(
            [pieces[0]] + [permute_by("context", pieces[d], d) for d in range(1, ring)]
        )
        pieces, output_sum.state, received[3] = together(pieces, output_sum.state, received[3])
        output_sum.over_dp()
        grad_context, delta = block_call(
            functools.partial(context_grad_kernel, share=self.share),
            (pieces, self.context),
            [distance_spec(block, HD), rows_spec(block, HD)],
            [rows_spec(block, HD), scalars_spec(block)],
            [
                jax.ShapeDtypeStruct((rows, HD), jnp.bfloat16),
                jax.ShapeDtypeStruct((8, rows), jnp.float32),
            ],
            ring,
            5.0,
            self.places,
        )
        sums, delta = together(sums, delta)
        sums = small_sum(sums, ("dp",))
        query_grad, key_grad, value_grad = flash_backward(
            self.queries,
            self.keys,
            self.values,
            grad_context,
            self.logs,
            delta,
            self.length,
            block,
        )
        query_grad, kept, received[4], output_sum.state = together(
            query_grad, kept, received[4], output_sum.state
        )
        output_sum.step()
        dots, gain_grads = block_call(
            turn_grad_kernel,
            (*self.common, query_grad, key_grad),
            self.common_specs + [rows_spec(block, HD)] * 2,
            [scalars_spec(block, 2), fixed_spec(8, HD)],
            [
                jax.ShapeDtypeStruct((2, rows), jnp.float32),
                jax.ShapeDtypeStruct((8, HD), jnp.float32),
            ],
            ring,
            10.0,
        )
        dots, output_sum.state = together(dots, output_sum.state)
        output_sum.step()
        dots = small_sum(dots, TOKEN_AXES)
        dots, received[5], output_sum.state = together(dots, received[5], output_sum.state)
        output_sum.step()
        self.finished = finish(kept, received)
        grad_joint, relative = block_call(
            functools.partial(norm_grad_kernel, share=self.share),
            (*self.common, query_grad, key_grad, value_grad, dots),
            self.common_specs + [rows_spec(block, HD)] * 3 + [scalars_spec(block, 2)],
            [rows_spec(block, 3 * HD), distance_spec(block, 3 * HD)],
            [jax.ShapeDtypeStruct((rows, 3 * HD), jnp.bfloat16)] * 2,
            ring,
            12.0,
            self.places,
        )
        grad_joint, relative, output_sum.state = together(grad_joint, relative, output_sum.state)
        output_sum.finish()
        output_sum.collect()
        head = lax.axis_index("context")
        half = block // 2
        width = self.weight.shape[0]
        joint_grad = contract_rows(grad_joint, self.normed)
        here = (lax.axis_index("expert") * ring + head) * HD
        gains = lax.dynamic_update_slice(
            jnp.zeros((2, width), jnp.float32), gain_grads[:2], (0, here)
        )
        parts = ring_parts(joint_grad.reshape(3, HD, width), "dp", 1)
        mine, others = ring_sum_begin([part.reshape(-1, width) for part in parts], "dp")
        relative, mine, output_sum.state = together(relative, mine, output_sum.state)

        def term(s):
            return tuple(
                contract_last(relative[start : start + half], self.weight).reshape(
                    -1, tok_rows, width
                )
                for start in (s * block, s * block + half)
            )

        joint = JointTotal(ring)

        def first(_):
            for _ in range(ring - 2):
                output_sum.collect()
            return low(mine + others.astype(jnp.float32)), (), output_sum.state

        def later(i):
            def work(result, rest):
                piece, joint.outs, output_sum.state = result
                joint.add(piece, i)
                if not i:
                    output_sum.exchange()
                return rest, joint.outs, output_sum.state

            return work

        works = [((), first)] + [((), later(i)) for i in range(ring - 1)]
        total, result = scatter_chunks(term, works, lambda result: result[0])
        piece, joint.outs, output_sum.state = result
        joint.add(piece, ring - 1)
        return total, sums, gains, *joint.outs, output_sum.total()


def spread_kernel(place_ref, *refs, size):
    parts, outs = (refs[:size], refs[-3:])
    rows = HD // size
    for i, out_ref in enumerate(outs):
        slabs = []
        for j in range(size):
            slab = 0.0
            for d, part in enumerate(parts):
                here = part[i * rows : (i + 1) * rows, :].astype(jnp.float32)
                slab = slab + jnp.where(place_ref[1 + d] == j, here, 0.0)
            slabs.append(slab)
        out_ref[...] = jnp.concatenate(slabs, axis=0).T


class JointTotal:
    def __init__(self, ring):
        self.ring = ring
        self.outs = ()

    def add(self, piece, distance):
        ring, size = (self.ring, lax.axis_size("dp"))
        head = (lax.axis_index("context") + ring - distance) % ring
        parts = ring_gather(piece, "dp")
        width = piece.shape[1]
        place = [head] + [(lax.axis_index("dp") + size - d) % size for d in range(size)]
        out = ((width, ring * HD), jnp.float32, pl.BlockSpec((width, HD), lambda i, p: (0, p[0])))
        self.outs = chunk_call(
            functools.partial(spread_kernel, size=size),
            parts,
            [fixed_spec(*piece.shape)] * size,
            [out] * 3,
            dict(enumerate(self.outs)),
            [],
            1,
            takes(5.0),
            (jnp.stack(place).astype(jnp.int32),),
        )


class BlockAttention:
    def __init__(self, normed, length, weights, gains, output_weight, experts, count):
        self.tok_rows = normed.shape[0]
        self.output_weight = output_weight
        self.count_total = count
        gather_chunks(experts.chosen, lambda s, blocks: experts.pick(experts.here(blocks)))
        self.length = length
        self.query_gain, self.key_gain = gains
        self.head_width = head_width = weights[0].shape[1]
        self.heads = head_width // HD
        self.weight = jnp.concatenate(weights, axis=1)
        self.normed = gather_block(normed)
        self.rows = rows = self.normed.shape[0]
        self.block_start = lax.axis_index("context") * rows
        projected = jnp.dot(self.normed, self.weight, preferred_element_type=jnp.float32)
        self.query_raw = projected[:, :head_width]
        self.key_raw = projected[:, head_width : 2 * head_width]
        value_raw = projected[:, 2 * head_width :]
        query_total, key_total = lax.psum(
            (jnp.sum(self.query_raw**2, axis=-1), jnp.sum(self.key_raw**2, axis=-1)), "expert"
        )
        self.query_inv = lax.rsqrt(query_total / (HEADS * HD) + EPSILON)[:, None]
        self.key_inv = lax.rsqrt(key_total / (HEADS * HD) + EPSILON)[:, None]
        self.tables = rope_tables(self.block_start + jnp.arange(rows, dtype=jnp.int32))
        query_rot = self.turn(self.query_raw * self.query_inv * self.query_gain, rotate)
        key_rot = self.turn(self.key_raw * self.key_inv * self.key_gain, rotate)
        self.keys, self.values = (
            lax.all_gather(low(key_rot), "context", axis=0, tiled=True),
            lax.all_gather(
                low(value_raw.reshape(rows, self.heads, HD)), "context", axis=0, tiled=True
            ),
        )
        self.query_block = min(512, rows)
        self.count = rows // self.query_block
        self.starts = jnp.arange(self.count, dtype=jnp.int32) * self.query_block
        self.queries = self.in_blocks(low(query_rot))

        def forward_block(packed):
            query_part, offset = packed
            masked, _ = self.scores_for(query_part, offset)
            highest = jnp.max(masked, axis=-1, keepdims=True)
            scores = jnp.exp(masked - highest)
            totals = jnp.sum(scores, axis=-1, keepdims=True)
            context = jnp.einsum(
                "hqk,khd->qhd",
                low(scores / totals),
                self.values,
                preferred_element_type=jnp.float32,
            )
            return (context, (highest + jnp.log(totals))[..., 0])

        context, self.logs = lax.map(forward_block, (self.queries, self.starts))
        self.context = low(context.reshape(rows, head_width))

    def turn(self, values, how):
        return how(values.reshape(self.rows, self.heads, HD), *self.tables)

    def in_blocks(self, values):
        return values.reshape(self.count, self.query_block, self.heads, HD)

    def scores_for(self, query_part, offset):
        raw_scores = (
            jnp.einsum("qhd,khd->hqk", query_part, self.keys, preferred_element_type=jnp.float32)
            * SCORE_SCALE
        )
        key_pos = jnp.arange(self.keys.shape[0], dtype=jnp.int32)
        query_pos = self.block_start + offset + jnp.arange(self.query_block, dtype=jnp.int32)
        allowed = (key_pos[None, :] <= query_pos[:, None]) & (key_pos[None, :] < self.length)
        return (jnp.where(allowed[None], raw_scores, NEGATIVE), allowed)

    def output(self):
        term = jnp.dot(self.context, self.output_weight, preferred_element_type=jnp.float32)
        return lax.psum_scatter(low(term), "expert", scatter_dimension=0, tiled=True).astype(
            jnp.float32
        )

    def backward(self, grad_attn, sums, pending):
        self.finished = finish(*zip(*pending))
        sums = small_sum(sums, ALL_AXES)
        rows, heads = (self.rows, self.heads)
        block_grad = gather_block(grad_attn)
        output_total = sum_low(contract_rows(self.context, block_grad), ("dp", "context"))
        grad_blocks = self.in_blocks(low(contract_last(block_grad, self.output_weight)))

        def backward_block(running, packed):
            key_acc, value_acc = running
            query_part, grad_part, log_part, offset = packed
            masked, allowed = self.scores_for(query_part, offset)
            probs = jnp.where(allowed[None], jnp.exp(masked - log_part[..., None]), 0.0)
            grad_probs = jnp.einsum(
                "qhd,khd->hqk", grad_part, self.values, preferred_element_type=jnp.float32
            )
            row_dot = jnp.sum(probs * grad_probs, axis=-1, keepdims=True)
            grad_scores = low(probs * (grad_probs - row_dot))
            query_grad = (
                jnp.einsum(
                    "hqk,khd->qhd", grad_scores, self.keys, preferred_element_type=jnp.float32
                )
                * SCORE_SCALE
            )
            key_acc = (
                key_acc
                + jnp.einsum(
                    "hqk,qhd->khd", grad_scores, query_part, preferred_element_type=jnp.float32
                )
                * SCORE_SCALE
            )
            value_acc = value_acc + jnp.einsum(
                "hqk,qhd->khd", low(probs), grad_part, preferred_element_type=jnp.float32
            )
            return ((key_acc, value_acc), query_grad)

        zeros = jnp.zeros((self.keys.shape[0], heads, HD), jnp.float32)
        (key_acc, value_acc), query_grads = lax.scan(
            backward_block, (zeros, zeros), (self.queries, grad_blocks, self.logs, self.starts)
        )
        key_grad, value_grad = (
            lax.psum_scatter(low(acc), "context", scatter_dimension=0, tiled=True).astype(
                jnp.float32
            )
            for acc in (key_acc, value_acc)
        )
        grad_query_normed = self.turn(query_grads, rotate_back).reshape(rows, -1)
        grad_key_normed = self.turn(key_grad, rotate_back).reshape(rows, -1)
        query_dot, key_dot = lax.psum(
            (
                jnp.sum(self.query_raw * self.query_gain * grad_query_normed, axis=-1),
                jnp.sum(self.key_raw * self.key_gain * grad_key_normed, axis=-1),
            ),
            "expert",
        )
        grad_query = low(
            self.query_inv * self.query_gain * grad_query_normed
            - self.query_raw * self.query_inv**3 * (query_dot / (HEADS * HD))[:, None]
        )
        grad_key = low(
            self.key_inv * self.key_gain * grad_key_normed
            - self.key_raw * self.key_inv**3 * (key_dot / (HEADS * HD))[:, None]
        )
        grad_value = low(value_grad.reshape(rows, -1))
        grad_joint = jnp.concatenate([grad_query, grad_key, grad_value], axis=1)
        joint_total = sum_low(contract_rows(self.normed, grad_joint), ("dp", "context"))
        term = contract_last(grad_joint, self.weight)
        grad_normed = lax.psum_scatter(
            low(term), "expert", scatter_dimension=0, tiled=True
        ).astype(jnp.float32)
        gains_total = lax.psum(
            (
                jnp.sum(self.query_raw * self.query_inv * grad_query_normed, axis=0),
                jnp.sum(self.key_raw * self.key_inv * grad_key_normed, axis=0),
            ),
            ("dp", "context"),
        )
        gains = jnp.zeros((2, self.weight.shape[0]), jnp.float32)
        here = lax.axis_index("expert") * self.head_width
        own = jnp.stack(gains_total) / (lax.axis_size("dp") * lax.axis_size("context"))
        gains = lax.dynamic_update_slice(gains, own, (0, here))
        return (grad_normed, sums, gains, *jnp.split(joint_total, 3, axis=1), output_total)


UNIT_TILE = 256
WIDTH_TILE = 512


def expert_forward_kernel(expert_ref, *refs, count, experts_all, unit_tiles):
    blocks = refs[:count]
    pick_ref, router_ref, gate_weight_ref, up_weight_ref, down_weight_ref = refs[
        count : count + 5
    ]
    (
        rows_ref,
        gate_ref,
        up_ref,
        hidden_ref,
        out_ref,
        row_gate_ref,
        kept_ref,
        sent_ref,
        scaled_ref,
        units_ref,
    ) = refs[-10:]
    step = pl.program_id(0)
    capacity = pick_ref.shape[1]

    @pl.when(step == 0)
    def _():
        for i, block_ref in enumerate(blocks):
            here = pl.ds(i * capacity, capacity)
            tokens = block_ref[...]
            pick = pick_ref[i]
            rows_ref[here, :] = low(contract(pick, tokens, 1, 0))
            logits = contract(tokens, router_ref[...], 1, 0)
            lane = lax.broadcasted_iota(jnp.int32, logits.shape, 1)
            logits = jnp.where(lane < experts_all, logits, NEGATIVE)
            weights = jnp.exp(logits - jnp.max(logits, axis=1, keepdims=True))
            chosen = jnp.sum(
                jnp.where(lane == expert_ref[0], weights, 0.0), axis=1, keepdims=True
            )
            gates = as_row(chosen / jnp.sum(weights, axis=1, keepdims=True))
            scaled = pick.astype(jnp.float32) * gates
            scaled_ref[i] = low(scaled)
            row_gates = jnp.sum(scaled, axis=1, keepdims=True)
            row_gate_ref[here, :] = jnp.broadcast_to(row_gates, (capacity, HD))

    @pl.when(step < unit_tiles)
    def _():
        rows = rows_ref[...]
        gate_part = contract(rows, gate_weight_ref[...], 1, 0)
        up_part = contract(rows, up_weight_ref[...], 1, 0)
        hidden = low(silu_parts(gate_part)[0] * up_part)
        gate_ref[...] = low(gate_part)
        up_ref[...] = low(up_part)
        hidden_ref[...] = hidden
        for j in range(unit_tiles):

            @pl.when(step == j)
            def _(j=j):
                units_ref[:, j * UNIT_TILE : (j + 1) * UNIT_TILE] = hidden

    @pl.when(step >= unit_tiles)
    def _():
        out_ref[...] = low(contract(units_ref[...], down_weight_ref[...], 1, 0))
        spread_tokens(scaled_ref, out_ref, kept_ref, sent_ref)


def spread_tokens(pick_ref, rows_ref, kept_ref, sent_ref):
    count, capacity, tok_rows = pick_ref.shape
    half = count // 2
    for i in range(count):
        terms = contract_rows(pick_ref[i], rows_ref[pl.ds(i * capacity, capacity), :])
        if i < half:
            kept_ref[i, :tok_rows, :] = low(terms)
        else:
            sent_ref[i - half, :tok_rows, :] = low(terms)


def spread_scalars(expert, values_ref, kept_ref, sent_ref):
    count, tok_rows = values_ref.shape
    half = count // 2
    for i in range(count):
        out_ref, place = (kept_ref, i) if i < half else (sent_ref, i - half)
        values = values_ref[i : i + 1, :]
        first = low(values).astype(jnp.float32)
        both = jnp.concatenate([first, values - first], axis=1)
        rows, width = (out_ref.shape[1] - tok_rows, out_ref.shape[2])
        out_ref[place, tok_rows:, :] = jnp.zeros((rows, width), jnp.bfloat16)
        row = lax.broadcasted_iota(jnp.int32, (rows, 2 * tok_rows), 0)
        out_ref[place, tok_rows:, : 2 * tok_rows] = low(jnp.where(row == expert, both, 0.0))


def expert_backward_kernel(expert_ref, *refs, count, unit_tiles):
    blocks = refs[:count]
    (
        pick_ref,
        row_gate_ref,
        gate_ref,
        up_ref,
        out_ref,
        down_weight_ref,
        gate_weight_ref,
        up_weight_ref,
    ) = refs[count : count + 8]
    (
        gate_grad_ref,
        grad_out_ref,
        grad_gate_ref,
        grad_up_ref,
        kept_ref,
        sent_ref,
        gates_ref,
        ups_ref,
        rows_ref,
    ) = refs[-9:]
    step = pl.program_id(0)
    capacity = pick_ref.shape[1]

    @pl.when(step == 0)
    def _():
        for i, block_ref in enumerate(blocks):
            here = pl.ds(i * capacity, capacity)
            pick = pick_ref[i]
            grads = contract(pick, block_ref[...], 1, 0)
            dots = jnp.sum(grads * out_ref[here, :].astype(jnp.float32), axis=1, keepdims=True)
            gate_grad_ref[i : i + 1, :] = jnp.sum(
                pick.astype(jnp.float32) * dots, axis=0, keepdims=True
            )
            grad_out_ref[here, :] = low(grads * row_gate_ref[here, 0:1])

    @pl.when(step < unit_tiles)
    def _():
        grad_hidden = contract_last(grad_out_ref[...], down_weight_ref[...])
        silu_value, silu_slope = silu_parts(gate_ref[...].astype(jnp.float32))
        grad_gate = low(grad_hidden * up_ref[...].astype(jnp.float32) * silu_slope)
        grad_up = low(grad_hidden * silu_value)
        grad_gate_ref[...] = grad_gate
        grad_up_ref[...] = grad_up
        for j in range(unit_tiles):

            @pl.when(step == j)
            def _(j=j):
                gates_ref[:, j * UNIT_TILE : (j + 1) * UNIT_TILE] = grad_gate
                ups_ref[:, j * UNIT_TILE : (j + 1) * UNIT_TILE] = grad_up

    @pl.when(step >= unit_tiles)
    def _():
        rows_ref[...] = low(
            contract_last(gates_ref[...], gate_weight_ref[...])
            + contract_last(ups_ref[...], up_weight_ref[...])
        )
        spread_tokens(pick_ref, rows_ref, kept_ref, sent_ref)

        @pl.when(step == unit_tiles)
        def _():
            spread_scalars(expert_ref[0], gate_grad_ref, kept_ref, sent_ref)

        @pl.when(step > unit_tiles)
        def _():
            tok_rows = gate_grad_ref.shape[1]
            for out_ref in (kept_ref, sent_ref):
                rest = out_ref.shape[0], out_ref.shape[1] - tok_rows, out_ref.shape[2]
                out_ref[:, tok_rows:, :] = jnp.zeros(rest, jnp.bfloat16)


def chunk_call(kernel, arrays, in_specs, outs, before, scratch, steps, cost, prefetch=()):
    first = len(prefetch) + len(arrays)
    return pl.pallas_call(
        kernel,
        grid_spec=pltpu.PrefetchScalarGridSpec(
            num_scalar_prefetch=len(prefetch),
            grid=(steps,),
            in_specs=in_specs + [pl.BlockSpec(memory_space=pl.ANY)] * len(before),
            out_specs=[out[2] for out in outs],
            scratch_shapes=scratch,
        ),
        out_shape=[jax.ShapeDtypeStruct(out[0], out[1]) for out in outs],
        input_output_aliases={first + i: j for i, j in enumerate(before)},
        compiler_params=pltpu.CompilerParams(vmem_limit_bytes=VMEM_LIMIT),
        cost_estimate=cost,
    )(*prefetch, *arrays, *before.values())


class Experts:
    def __init__(self, routes, capacity, router_weight, gate_weight, up_weight, down_weight):
        self.capacity = -(-capacity // 16) * 16
        self.experts_all = router_weight.shape[1]
        self.expert = lax.axis_index("context") * lax.axis_size("expert") + lax.axis_index(
            "expert"
        )
        self.router_weight = jnp.pad(router_weight, ((0, 0), (0, HD - self.experts_all)))
        expert_ids = jnp.arange(HD, dtype=jnp.int32)
        self.chosen = low(jnp.any(routes[:, :, None] == expert_ids, axis=1))
        self.own = (gate_weight[0], up_weight[0], down_weight[0])
        self.arriving = [
            ring_gather(half, "dp")[1:] for w in self.own for half in jnp.split(w, 2)
        ]
        self.picks = []

    def here(self, blocks):
        lane = jnp.arange(HD, dtype=jnp.int32) == self.expert
        return jnp.sum(jnp.where(lane, jnp.stack(blocks).astype(jnp.float32), 0.0), axis=-1)

    def pick(self, here):
        member = here > 0
        tok_rows = member.shape[1]
        token = jnp.arange(tok_rows, dtype=jnp.int32)
        before = low(token[:, None] < token[None, :])
        slots = contract(low(member), before, 1, 0).astype(jnp.int32)
        slot_index = jnp.arange(self.capacity, dtype=jnp.int32)
        matches = slots[:, None, :] == slot_index[None, :, None]
        self.picks.append(low(matches & member[:, None, :]))

    def begin(self):
        whole = []
        for i, own in enumerate(self.own):
            halves = zip(*self.arriving[2 * i : 2 * i + 2])
            whole.append([own] + [jnp.concatenate(pair) for pair in halves])
        self.gate_weight, self.up_weight = (jnp.concatenate(w, axis=1) for w in whole[:2])
        self.down_weight = jnp.concatenate(whole[2])
        self.units = self.gate_weight.shape[1]
        self.picks = jnp.stack(self.picks)
        self.chained, self.chained_back = ((), ())
        self.terms, self.terms_back = ({}, {})

    def shapes(self):
        ring, count, capacity, tok_rows = self.picks.shape
        width = self.gate_weight.shape[0]
        return ring, count, count * capacity, tok_rows, width

    def plan(self, s, more=0):
        ring, count, rows, tok_rows, width = self.shapes()
        tiles = self.units // UNIT_TILE
        tile = math.gcd(WIDTH_TILE, width)

        def unit(j):
            return jnp.minimum(j, tiles - 1)

        def column(j):
            return jnp.maximum(j - tiles, 0)

        half = count // 2
        all_rows = ring * rows
        term = (
            (half, tok_rows + more, width),
            jnp.bfloat16,
            pl.BlockSpec((half, tok_rows + more, tile), lambda j, *_: (0, 0, column(j))),
        )
        unit_spec = pl.BlockSpec((rows, UNIT_TILE), lambda j, *_: (s, unit(j)))
        whole_spec = pl.BlockSpec((rows, width), lambda j, *_: (s, 0))
        scalar_spec = pl.BlockSpec((rows, HD), lambda j, *_: (s, 0))
        column_spec = pl.BlockSpec((rows, tile), lambda j, *_: (s, column(j)))
        block_specs = [pl.BlockSpec((tok_rows, width), lambda j, *_: (0, 0))] * count
        pick_spec = pl.BlockSpec((None, *self.picks.shape[1:]), lambda j, *_: (s, 0, 0, 0))
        narrow = ((all_rows, self.units), jnp.bfloat16, unit_spec)
        wide = ((all_rows, width), jnp.bfloat16, whole_spec)
        cost = takes(21.0)
        return (
            unit,
            column,
            tiles,
            tile,
            term,
            unit_spec,
            whole_spec,
            scalar_spec,
            column_spec,
            block_specs,
            pick_spec,
            narrow,
            wide,
            cost,
        )

    def forward_chunk(self, s, blocks):
        ring, count, rows, tok_rows, width = self.shapes()
        (
            unit,
            column,
            tiles,
            tile,
            term,
            unit_spec,
            whole_spec,
            scalar_spec,
            column_spec,
            block_specs,
            pick_spec,
            narrow,
            wide,
            cost,
        ) = self.plan(s)
        results = chunk_call(
            functools.partial(
                expert_forward_kernel,
                count=count,
                experts_all=self.experts_all,
                unit_tiles=tiles,
            ),
            (
                *blocks,
                self.picks,
                self.router_weight,
                self.gate_weight,
                self.up_weight,
                self.down_weight,
            ),
            [
                *block_specs,
                pick_spec,
                fixed_spec(width, HD),
                pl.BlockSpec((width, UNIT_TILE), lambda j, *_: (0, unit(j))),
                pl.BlockSpec((width, UNIT_TILE), lambda j, *_: (0, unit(j))),
                pl.BlockSpec((self.units, tile), lambda j, *_: (0, column(j))),
            ],
            [
                wide,
                narrow,
                narrow,
                narrow,
                (wide[0], wide[1], column_spec),
                ((ring * rows, HD), jnp.float32, scalar_spec),
                term,
                term,
            ],
            dict(enumerate(self.chained)),
            [
                pltpu.VMEM(self.picks.shape[1:], jnp.bfloat16),
                pltpu.VMEM((rows, self.units), jnp.bfloat16),
            ],
            tiles + width // tile,
            cost,
            (self.expert.reshape(1).astype(jnp.int32),),
        )
        self.chained = results[:6]
        self.terms[s] = results[6:]
        return results[7]

    def forward(self, ffn_in):
        last = lax.axis_size("context") - 1
        done, _ = gather_chunks(ffn_in, self.forward_chunk)
        idle = ((), lambda result: result)
        works = [((), lambda result: done[last])] + [idle] * last
        mixture, _ = scatter_chunks(lambda s: self.terms[s], works)
        return mixture

    def backward_chunk(self, s, blocks):
        ring, count, rows, tok_rows, width = self.shapes()
        (
            unit,
            column,
            tiles,
            tile,
            term,
            unit_spec,
            whole_spec,
            scalar_spec,
            column_spec,
            block_specs,
            pick_spec,
            narrow,
            wide,
            cost,
        ) = self.plan(s, -(-self.experts_all // 16) * 16)
        chunk_rows, gate_part, up_part, hidden, out, row_gates = self.chained
        results = chunk_call(
            functools.partial(expert_backward_kernel, count=count, unit_tiles=tiles),
            (
                *blocks,
                self.picks,
                row_gates,
                gate_part,
                up_part,
                out,
                self.down_weight,
                self.gate_weight,
                self.up_weight,
            ),
            [
                *block_specs,
                pick_spec,
                scalar_spec,
                unit_spec,
                unit_spec,
                whole_spec,
                pl.BlockSpec((UNIT_TILE, width), lambda j, *_: (unit(j), 0)),
                pl.BlockSpec((tile, self.units), lambda j, *_: (column(j), 0)),
                pl.BlockSpec((tile, self.units), lambda j, *_: (column(j), 0)),
            ],
            [
                ((count, tok_rows), jnp.float32, fixed_spec(count, tok_rows)),
                wide,
                narrow,
                narrow,
                term,
                term,
            ],
            {j + 1: array for j, array in enumerate(self.chained_back)},
            [
                pltpu.VMEM((rows, self.units), jnp.bfloat16),
                pltpu.VMEM((rows, self.units), jnp.bfloat16),
                pltpu.VMEM((rows, tile), jnp.bfloat16),
            ],
            tiles + width // tile,
            cost,
            (self.expert.reshape(1).astype(jnp.int32),),
        )
        self.chained_back = results[1:4]
        self.terms_back[s] = results[4:]
        return results[0]

    def backward(self, grad_out):
        last = lax.axis_size("context") - 1
        self.gate_done, _ = gather_chunks(low(grad_out), self.backward_chunk)
        grad_rows_out, grad_gate, grad_up = self.chained_back
        chunk_rows, hidden = (self.chained[0], self.chained[3])
        size = lax.axis_size("dp")

        def parts(left, right, axis):
            return jnp.split(contract_rows(left, right), size, axis=axis)

        pending = []

        def product(left, right, axis):
            shares = parts(after_exchange(left, left), right, axis)
            halves = zip(*(jnp.split(share, 2) for share in shares))
            return [list(half) for half in halves]

        def begin(half):
            pending.append(ring_sum_begin(half, "dp"))
            return pending[-1][1]

        def second(_, *arrays):
            self.gates_grad = product(*arrays, 1)
            return self.gates_grad[0][0], ()

        def third(_, *arrays):
            self.ups_grad = product(*arrays, 1)
            return self.ups_grad[0][0], begin(self.gates_grad[0])

        def fourth(_, *arrays):
            self.downs_grad = product(*arrays, 0)
            return self.downs_grad[0][0], begin(self.gates_grad[1])

        works = [((), lambda result: result)] * (last + 1)
        works[0] = ((), lambda _: self.gate_done[last])
        works[1] = ((chunk_rows, grad_gate), second)
        works[2] = ((chunk_rows, grad_up), third)
        works[-1] = ((hidden, grad_rows_out), fourth)
        total, done = scatter_chunks(lambda s: self.terms_back[s], works)
        total, done = together(total, done)
        tok_rows = self.picks.shape[3]
        grad_ffn, rest = (total[:tok_rows], total[tok_rows:])
        grad_gates = (rest[:, :tok_rows] + rest[:, tok_rows : 2 * tok_rows])[: self.experts_all].T
        for half in (*self.ups_grad, *self.downs_grad):
            begin(half)
        return grad_ffn, grad_gates, pending


def per_device(
    block_input,
    teacher_states,
    seq_lengths,
    expert_routes,
    attn_gain,
    query_weight,
    key_weight,
    value_weight,
    query_gain,
    key_gain,
    output_weight,
    ffn_gain,
    router_weight,
    gate_weight,
    up_weight,
    down_weight,
):
    tok_rows = block_input.shape[0]
    experts_all = router_weight.shape[1]
    capacity = 5 * tok_rows * TOPK // (4 * experts_all)
    context_size = lax.axis_size("context")
    expert_size = lax.axis_size("expert")
    token_count_all = tok_rows * lax.axis_size("dp") * context_size * expert_size
    length = seq_lengths[0]
    own_start = (
        lax.axis_index("context") * expert_size + lax.axis_index("expert")
    ) * tok_rows
    tokens = block_input.astype(jnp.float32)
    inverse_one = rms_scale(tokens)
    normed = low(tokens * inverse_one * attn_gain)
    heads_here = query_weight.shape[1] // HD
    count_total = small_sum(jnp.full((8, 128), length, jnp.int32), ("dp",))
    experts = Experts(
        expert_routes, capacity, router_weight, gate_weight, up_weight, down_weight
    )
    attention_kind = HeadAttention if heads_here == context_size else BlockAttention
    attention = attention_kind(
        normed,
        length,
        (query_weight, key_weight, value_weight),
        (query_gain, key_gain),
        output_weight,
        experts,
        count_total,
    )
    experts.begin()
    count_total = attention.count_total[0, 0].astype(jnp.float32)
    residual = tokens + attention.output()
    inverse_two = rms_scale(residual)
    ffn_in = low(residual * inverse_two * ffn_gain)
    logits = jnp.dot(ffn_in, router_weight, preferred_element_type=jnp.float32)
    weights_router = jnp.exp(logits - jnp.max(logits, axis=-1, keepdims=True))
    router_probs = weights_router / jnp.sum(weights_router, axis=-1, keepdims=True)
    expert_ids = jnp.arange(experts_all, dtype=jnp.int32)
    chosen = jnp.any(expert_routes[:, :, None] == expert_ids, axis=1)
    mixture = experts.forward(ffn_in)
    output_full = residual + mixture
    own_pos = own_start + jnp.arange(tok_rows, dtype=jnp.int32)
    valid = (own_pos < length).astype(jnp.float32)
    difference = output_full - teacher_states
    local_loss = jnp.sum(jnp.sum(difference * difference, axis=-1) * valid)
    grad_out = difference * (valid * (token_count_all / count_total))[:, None]
    grad_ffn_experts, grad_gates, pending = experts.backward(grad_out)
    grad_router_probs = jnp.where(chosen, grad_gates, 0.0)
    grad_logits = router_probs * (
        grad_router_probs - jnp.sum(router_probs * grad_router_probs, axis=-1, keepdims=True)
    )
    router_grad = lax.dot_general(
        grad_logits,
        ffn_in.astype(jnp.float32),
        (((0,), (0,)), ((), ())),
        precision=lax.Precision.HIGHEST,
    )
    grad_ffn = grad_ffn_experts + lax.dot_general(
        grad_logits,
        router_weight.astype(jnp.float32),
        (((1,), (1,)), ((), ())),
        precision=lax.Precision.HIGHEST,
    )
    ffn_gain_grad = jnp.sum(residual * inverse_two * grad_ffn, axis=0)
    weighted_two = grad_ffn * ffn_gain
    grad_residual = (
        grad_out
        + inverse_two * weighted_two
        - residual * inverse_two**3 * jnp.mean(residual * weighted_two, axis=-1, keepdims=True)
    )
    sums = jnp.concatenate(
        [
            router_grad,
            ffn_gain_grad[None],
            jnp.broadcast_to(local_loss, ffn_gain_grad.shape)[None],
        ]
    )
    grad_normed, sums, gains, query_total, key_total, value_total, output_total = (
        attention.backward(low(grad_residual), sums, pending)
    )
    attn_gain_grad = jnp.sum(tokens * inverse_one * grad_normed, axis=0)
    gains = small_sum(jnp.concatenate([attn_gain_grad[None], gains]), ("dp", *TOKEN_AXES))
    head_width = query_gain.shape[0]
    query_gain_total, key_gain_total = lax.dynamic_slice_in_dim(
        gains[1:], lax.axis_index("expert") * head_width, head_width, 1
    )
    weighted_one = grad_normed * attn_gain
    input_grad = (
        grad_residual
        + inverse_one * weighted_one
        - tokens * inverse_one**3 * jnp.mean(tokens * weighted_one, axis=-1, keepdims=True)
    )
    router_total, ffn_total = (sums[:experts_all].T, sums[experts_all])
    loss_total = sums[experts_all + 1, 0]
    return (
        low(output_full),
        loss_total / count_total,
        input_grad,
        gains[0],
        query_total,
        key_total,
        value_total,
        query_gain_total,
        key_gain_total,
        output_total,
        ffn_total,
        router_total,
        *attention.finished,
    )


def solution(mesh):
    rows = P(ALL_AXES, None)
    placed = (
        rows,
        rows,
        P("dp"),
        rows,
        P(),
        P(None, "expert"),
        P(None, "expert"),
        P(None, "expert"),
        P("expert"),
        P("expert"),
        P("expert", None),
        P(),
        P(),
        P(TOKEN_AXES, None, "dp"),
        P(TOKEN_AXES, None, "dp"),
        P(TOKEN_AXES, "dp", None),
    )
    return jax.shard_map(
        per_device,
        mesh=mesh,
        in_specs=placed,
        out_specs=(
            rows,
            P(),
            rows,
            P(),
            P(None, "expert"),
            P(None, "expert"),
            P(None, "expert"),
            P("expert"),
            P("expert"),
            P("expert", None),
            P(),
            P(),
            P(TOKEN_AXES, None, "dp"),
            P(TOKEN_AXES, None, "dp"),
            P(TOKEN_AXES, "dp", None),
        ),
        check_vma=False,
    )
```
